32 devices in a mesh: tm: 4 (over z), space: 8 (over y, x, core).
Axes of the slice: x: 2, y: 2, z: 4, core: 2. Of those that a mesh axis runs over, the one named last changes fastest.
Arguments:
- queries: bfloat16 [4096, 2560], P(('tm', 'space')), may hold values from -6 to 6
- keys: bfloat16 [4096, 2560], P(('tm', 'space')), may hold values from -6 to 6
- values: bfloat16 [4096, 2560], P(('tm', 'space')), may hold values from -6 to 6
- grad_out: bfloat16 [4096, 2560], P(('tm', 'space')), may hold values from -6 to 6
- saved_state: bfloat16 [4, 20, 128, 128], P('tm', None, 'space'), may hold values from -0.3984375 to 0.3984375
Outputs:
- grad_q: bfloat16 [4096, 2560], P(('tm', 'space'))
- grad_k: bfloat16 [4096, 2560], P(('tm', 'space'))
- grad_v: bfloat16 [4096, 2560], P(('tm', 'space'))
The draws below stay inside these ranges and needn't reach their ends.
All inputs are finite; a program needn't handle non-finite values.
Results may differ from the reference program's by a relative error of at most 0.0049.
Values may be sent and summed in bfloat16 or wider, within the bound.
No kernel may reach another device: no remote copies, remote signals or barrier semaphores. Data moves between devices by JAX's collectives and lax.ppermute only.
A program may use at most 64 MiB of HBM per device.

```python
import math
import jax
import jax.numpy as jnp
from jax import lax

HEADS = 20
HD = 128
WIDTH = 2560
BLOCKS = 4
BLOCK_TOK = 1024
TOKENS = 4096


def block_scale(own_key, extent, cuts, smallest, top_value):
    def one(position, shards_of):
        steps = jax.random.uniform(jax.random.fold_in(jax.random.fold_in(own_key, 6), position), (shards_of,), jnp.float32, smallest / len(cuts), top_value / len(cuts))
        return jnp.repeat(jnp.exp(steps), extent[position] // shards_of).reshape((-1,) + (1,) * (len(extent) - position - 1))

    level = one(*cuts[0])
    for cut in cuts[1:]:
        level = level * one(*cut)
    return level


def noise(rng, dims, scale, bound, cuts=(), held_as=jnp.bfloat16):
    drawn = scale * jax.random.normal(rng, dims, jnp.float32)
    if cuts:
        drawn = drawn * block_scale(rng, dims, cuts, -0.22, 0.18)
    return jnp.clip(drawn, -bound, bound).astype(held_as)


def setup_inputs(seed: int = 0) -> dict:
    arg_keys = jax.random.split(jax.random.key(seed), 6)
    return {
        "queries": noise(arg_keys[0], (TOKENS, WIDTH), 1.0, 6.0, ((0, 32),)),
        "keys": noise(arg_keys[1], (TOKENS, WIDTH), 1.0, 6.0, ((0, 32),)),
        "values": noise(arg_keys[2], (TOKENS, WIDTH), 1.0, 6.0, ((0, 32),)),
        "grad_out": noise(arg_keys[3], (TOKENS, WIDTH), 1.0, 6.0, ((0, 32),)),
        "saved_state": noise(arg_keys[4], (BLOCKS, HEADS, HD, HD), 0.05, 0.3984375, ((0, 4), (2, 8))),
    }


def block_partial(pair):
    q_block, out_block = pair
    scale = 1.0 / math.sqrt(TOKENS * HD)
    q_feat = jnp.maximum(q_block, 0).astype(jnp.float32)
    return scale * jnp.einsum('thd,the->hde', q_feat, out_block.astype(jnp.float32))

def block_grads(items):
    q_block, k_block, v_block, out_block, state_block, grad_block = items
    state_f = state_block.astype(jnp.float32)
    grad_f = grad_block.astype(jnp.float32)
    dq_full = jnp.einsum('the,hde->thd', out_block.astype(jnp.float32), state_f)
    dq_out = jnp.where(q_block > 0, dq_full, 0.0).astype(jnp.bfloat16)
    dk_full = jnp.einsum('the,hde->thd', v_block.astype(jnp.float32), grad_f)
    dk_out = jnp.where(k_block > 0, dk_full, 0.0).astype(jnp.bfloat16)
    k_feat = jnp.maximum(k_block, 0).astype(jnp.float32)
    dv_out = jnp.einsum('thd,hde->the', k_feat, grad_f).astype(jnp.bfloat16)
    return (dq_out, dk_out, dv_out)

def reference(queries, keys, values, grad_out, saved_state):
    shape4 = (BLOCKS, BLOCK_TOK, HEADS, HD)
    q_all = queries.reshape(shape4)
    k_all = keys.reshape(shape4)
    v_all = values.reshape(shape4)
    o_all = grad_out.reshape(shape4)
    parts = lax.map(block_partial, (q_all, o_all))
    gsum = jnp.flip(jnp.cumsum(jnp.flip(parts, 0), axis=0), 0)
    gstate = gsum.astype(jnp.bfloat16)
    dq_all, dk_all, dv_all = lax.map(block_grads, (q_all, k_all, v_all, o_all, saved_state, gstate))
    return (dq_all.reshape(TOKENS, WIDTH), dk_all.reshape(TOKENS, WIDTH), dv_all.reshape(TOKENS, WIDTH))
```

```python
import functools
import math

import jax
import jax.numpy as jnp
from jax import lax
from jax.experimental import pallas as pl
from jax.experimental.pallas import tpu as pltpu
from jax.sharding import PartitionSpec as P

CONTRACT_ROWS = (((0,), (0,)), ((), ()))
CONTRACT_COLS = (((1,), (1,)), ((), ()))
VMEM_BYTES = 24 * 1024 * 1024


def partner(group, hop, groups):
    if groups & (groups - 1) == 0:
        return group ^ hop
    return (group + hop) % groups


def source(group, hop, groups):
    if groups & (groups - 1) == 0:
        return group ^ hop
    return (group - hop) % groups


def place_on_space(lanes):
    index = lax.axis_index("space")
    return index // lanes, index % lanes


def traced_partner(group, hop, groups):
    if groups & (groups - 1) == 0:
        return group ^ hop
    return lax.rem(group + hop, groups)


def traced_source(group, hop, groups):
    if groups & (groups - 1) == 0:
        return group ^ hop
    return lax.rem(group - hop + groups, groups)


def swap_lanes(value, lanes, groups):
    pairs = [(g * lanes + c, g * lanes + 1 - c) for g in range(groups) for c in range(lanes)]
    return lax.ppermute(value, "space", pairs)


def hop_groups(value, hop, lanes, groups):
    pairs = [
        (g * lanes + c, partner(g, hop, groups) * lanes + c)
        for g in range(groups)
        for c in range(lanes)
    ]
    return lax.ppermute(value, "space", pairs)


def partial_kernel(lanes, groups, scale, q_ref, o_ref, own_ref, send_ref, part):
    head = part.shape[1]
    for h in range(q_ref.shape[1] // head):
        cols = pl.ds(h * head, head)
        part[cols, :] = scale * lax.dot_general(
            jnp.maximum(q_ref[:, cols], 0),
            o_ref[:, cols],
            CONTRACT_ROWS,
            preferred_element_type=jnp.float32,
        )
    group, lane = place_on_space(lanes)
    rows = own_ref.shape[1]
    for hop in range(groups):
        there = traced_partner(group, hop, groups)
        mine = pl.multiple_of((lane * groups + there) * rows, rows)
        own_ref[hop] = part[pl.ds(mine, rows), :]
        if lanes > 1:
            theirs = pl.multiple_of(((1 - lane) * groups + there) * rows, rows)
            send_ref[hop] = part[pl.ds(theirs, rows), :].astype(send_ref.dtype)


def partial_products(queries, grad_out, head, lanes, groups, scale):
    width = queries.shape[1]
    rows = width // (lanes * groups)
    return pl.pallas_call(
        functools.partial(partial_kernel, lanes, groups, scale),
        out_shape=(
            jax.ShapeDtypeStruct((groups, rows, head), jnp.float32),
            jax.ShapeDtypeStruct((groups, rows, head), jnp.bfloat16),
        ),
        scratch_shapes=[pltpu.VMEM((width, head), jnp.float32)],
        compiler_params=pltpu.CompilerParams(vmem_limit_bytes=VMEM_BYTES),
        name="partial_products",
    )(queries, grad_out)


def query_kernel(lanes, groups, q_ref, o_ref, *rest):
    pieces, (dq_ref, state, sems) = rest[:-3], rest[-3:]
    head = state.shape[1]
    rows = pieces[0].shape[1]
    group, lane = place_on_space(lanes)
    copies = []
    for side in range(lanes):
        there_lane = lane if side == 0 else 1 - lane
        for hop in range(groups):
            at = side * groups + hop
            owner = traced_source(group, hop, groups) * lanes + there_lane
            copies.append(
                pltpu.make_async_copy(
                    pieces[at],
                    state.at[:, pl.ds(pl.multiple_of(owner * rows, rows), rows), :],
                    sems.at[at],
                )
            )
    for copy in copies:
        copy.start()
    for copy in copies:
        copy.wait()
    for h in range(state.shape[0]):
        cols = pl.ds(h * head, head)
        full = lax.dot_general(
            o_ref[:, cols], state[h], CONTRACT_COLS, preferred_element_type=jnp.float32
        )
        dq_ref[:, cols] = jnp.where(q_ref[:, cols] > 0, full, 0.0).astype(dq_ref.dtype)


def query_grads(queries, grad_out, pieces, lanes, groups):
    heads, _, head = pieces[0].shape
    whole = pl.BlockSpec(memory_space=pltpu.VMEM)
    return pl.pallas_call(
        functools.partial(query_kernel, lanes, groups),
        out_shape=jax.ShapeDtypeStruct(queries.shape, queries.dtype),
        in_specs=[whole, whole] + [pl.BlockSpec(memory_space=pl.ANY)] * len(pieces),
        out_specs=whole,
        scratch_shapes=[
            pltpu.VMEM((heads, head, head), pieces[0].dtype),
            pltpu.SemaphoreType.DMA((len(pieces),)),
        ],
        compiler_params=pltpu.CompilerParams(vmem_limit_bytes=VMEM_BYTES),
        name="query_grads",
    )(queries, grad_out, *pieces)


def key_value_kernel(lanes, groups, k_ref, v_ref, *rest):
    pieces, (dk_ref, dv_ref, state, sems) = rest[:-4], rest[-4:]
    head = state.shape[1]
    rows = pieces[0].shape[0]
    group, lane = place_on_space(lanes)
    copies = []
    for side in range(lanes):
        there_lane = lane if side == 0 else 1 - lane
        for hop in range(groups):
            at = side * groups + hop
            share = there_lane * groups + traced_source(group, hop, groups)
            copies.append(
                pltpu.make_async_copy(
                    pieces[at],
                    state.at[pl.ds(pl.multiple_of(share * rows, rows), rows), :],
                    sems.at[at],
                )
            )
    for copy in copies:
        copy.start()
    for copy in copies:
        copy.wait()
    for h in range(k_ref.shape[1] // head):
        cols = pl.ds(h * head, head)
        keys = k_ref[:, cols]
        grad_state = state[cols, :]
        full = lax.dot_general(
            v_ref[:, cols], grad_state, CONTRACT_COLS, preferred_element_type=jnp.float32
        )
        dk_ref[:, cols] = jnp.where(keys > 0, full, 0.0).astype(dk_ref.dtype)
        dv_ref[:, cols] = jnp.dot(
            jnp.maximum(keys, 0), grad_state, preferred_element_type=jnp.float32
        ).astype(dv_ref.dtype)


def key_value_grads(keys, values, pieces, lanes, groups):
    width, head = keys.shape[1], pieces[0].shape[1]
    whole = pl.BlockSpec(memory_space=pltpu.VMEM)
    return pl.pallas_call(
        functools.partial(key_value_kernel, lanes, groups),
        out_shape=(
            jax.ShapeDtypeStruct(keys.shape, keys.dtype),
            jax.ShapeDtypeStruct(values.shape, values.dtype),
        ),
        in_specs=[whole, whole] + [pl.BlockSpec(memory_space=pl.ANY)] * len(pieces),
        out_specs=(whole, whole),
        scratch_shapes=[
            pltpu.VMEM((width, head), pieces[0].dtype),
            pltpu.SemaphoreType.DMA((len(pieces),)),
        ],
        compiler_params=pltpu.CompilerParams(vmem_limit_bytes=VMEM_BYTES),
        name="key_value_grads",
    )(keys, values, *pieces)


def gather_space(value, lanes, groups):
    near = [value] + [hop_groups(value, hop, lanes, groups) for hop in range(1, groups)]
    far = [swap_lanes(piece, lanes, groups) for piece in near] if lanes > 1 else []
    return near + far


def per_device(queries, keys, values, grad_out, saved_state):
    heads, _, head = saved_state.shape[1:]
    blocks, devices = lax.axis_size("tm"), lax.axis_size("space")
    lanes = 2 if devices % 2 == 0 else 1
    groups = devices // lanes
    scale = 1.0 / math.sqrt(queries.shape[0] * blocks * devices * head)

    own, send = partial_products(queries, grad_out, head, lanes, groups, scale)
    if lanes > 1:
        own = own + swap_lanes(send, lanes, groups).astype(jnp.float32)
    share = own[0]
    for hop in range(1, groups):
        share = share + hop_groups(own[hop].astype(jnp.bfloat16), hop, lanes, groups).astype(
            jnp.float32
        )
    saved = gather_space(saved_state[0], lanes, groups)
    grad_q = query_grads(queries, grad_out, saved, lanes, groups)
    suffix, narrow = share, share.astype(jnp.bfloat16)
    for hop in range(1, blocks):
        later = lax.ppermute(narrow, "tm", [(b, b - hop) for b in range(hop, blocks)])
        suffix = suffix + later.astype(jnp.float32)
    grad_state = gather_space(suffix.astype(jnp.bfloat16), lanes, groups)
    grad_k, grad_v = key_value_grads(keys, values, grad_state, lanes, groups)
    return grad_q, grad_k, grad_v


def solution(mesh):
    tokens = P(("tm", "space"), None)
    return jax.shard_map(
        per_device,
        mesh=mesh,
        in_specs=(tokens, tokens, tokens, tokens, P("tm", None, "space", None)),
        out_specs=(tokens, tokens, tokens),
        check_vma=False,
    )
```

```python
import functools
import math

import jax
import jax.numpy as jnp
from jax import lax
from jax.experimental import pallas as pl
from jax.experimental.pallas import tpu as pltpu
from jax.sharding import PartitionSpec as P

CONTRACT_ROWS = (((0,), (0,)), ((), ()))
CONTRACT_COLS = (((1,), (1,)), ((), ()))
VMEM_BYTES = 16 * 1024 * 1024
VMEM_ALL = 56 * 1024 * 1024
ANYWHERE = pl.BlockSpec(memory_space=pl.ANY)
IN_HBM = pl.BlockSpec(memory_space=pltpu.HBM)
IN_VMEM = pl.BlockSpec(memory_space=pltpu.VMEM)


def place_on_space(lanes):
    index = lax.axis_index("space")
    return index // lanes, index % lanes


def swap_lanes(value, lanes, groups):
    if lanes == 1:
        return value
    pairs = [(g * lanes + c, g * lanes + 1 - c) for g in range(groups) for c in range(lanes)]
    return lax.ppermute(value, "space", pairs)


def exchange_groups(pieces, lanes, groups):
    if groups == 1:
        return pieces
    members = [[g * lanes + c for g in range(groups)] for c in range(lanes)]
    return lax.all_to_all(pieces, "space", 0, 0, axis_index_groups=members)


def gather_groups(value, lanes, groups):
    return exchange_groups(jnp.broadcast_to(value, (groups, *value.shape)), lanes, groups)


def side_columns(lanes, other, width):
    _, lane = place_on_space(lanes)
    side = 1 - lane if other else lane
    return side * (width // lanes)


def partial_kernel(lanes, other, steps, scale, q_hbm, o_hbm, part_ref, q_buf, o_buf, sems):
    head = part_ref.shape[1]
    base = side_columns(lanes, other, q_hbm.shape[1])
    span = q_buf.shape[1] // steps
    copies = []
    for step in range(steps):
        src = pl.ds(pl.multiple_of(base + step * span, head), span)
        dst = pl.ds(step * span, span)
        copies.append(
            (
                pltpu.make_async_copy(q_hbm.at[:, src], q_buf.at[:, dst], sems.at[0, step]),
                pltpu.make_async_copy(o_hbm.at[:, src], o_buf.at[:, dst], sems.at[1, step]),
            )
        )
    for pair in copies:
        for copy in pair:
            copy.start()
    for step in range(steps):
        for copy in copies[step]:
            copy.wait()
        for h in range(span // head):
            cols = pl.ds(step * span + h * head, head)
            part_ref[cols, :] = (
                scale
                * lax.dot_general(
                    jnp.maximum(q_buf[:, cols], 0),
                    o_buf[:, cols],
                    CONTRACT_ROWS,
                    preferred_element_type=jnp.float32,
                )
            ).astype(part_ref.dtype)


def partial_products(queries, grad_out, head, lanes, other, scale, dtype):
    tokens, width = queries.shape
    half = width // lanes
    steps = 2 if (half // head) % 2 == 0 else 1
    return pl.pallas_call(
        functools.partial(partial_kernel, lanes, other, steps, scale),
        out_shape=jax.ShapeDtypeStruct((half, head), dtype),
        in_specs=[IN_HBM, IN_HBM],
        out_specs=IN_VMEM,
        scratch_shapes=[
            pltpu.VMEM((tokens, half), queries.dtype),
            pltpu.VMEM((tokens, half), grad_out.dtype),
            pltpu.SemaphoreType.DMA((2, steps)),
        ],
        compiler_params=pltpu.CompilerParams(vmem_limit_bytes=VMEM_ALL),
        name="partial_other" if other else "partial_own",
    )(queries, grad_out)


def query_kernel(lanes, q_ref, o_ref, *rest):
    sides, (dq_ref, state, sems) = rest[:lanes], rest[lanes:]
    head = state.shape[1]
    groups, _, rows, _ = sides[0].shape
    _, lane = place_on_space(lanes)
    copies = []
    for other in range(lanes):
        there = 1 - lane if other else lane
        for g in range(groups):
            row = pl.multiple_of((g * lanes + there) * rows, rows)
            copies.append(
                pltpu.make_async_copy(
                    sides[other].at[g], state.at[:, pl.ds(row, rows), :], sems.at[other, g]
                )
            )
    for copy in copies:
        copy.start()
    for copy in copies:
        copy.wait()
    for h in range(state.shape[0]):
        cols = pl.ds(h * head, head)
        full = lax.dot_general(
            o_ref[:, cols], state[h], CONTRACT_COLS, preferred_element_type=jnp.float32
        )
        dq_ref[:, cols] = jnp.where(q_ref[:, cols] > 0, full, 0.0).astype(dq_ref.dtype)


def query_grads(queries, grad_out, sides):
    lanes, (groups, heads, _, head) = len(sides), sides[0].shape
    return pl.pallas_call(
        functools.partial(query_kernel, lanes),
        out_shape=jax.ShapeDtypeStruct(queries.shape, queries.dtype),
        in_specs=[IN_VMEM, IN_VMEM] + [ANYWHERE] * lanes,
        out_specs=IN_VMEM,
        scratch_shapes=[
            pltpu.VMEM((heads, head, head), sides[0].dtype),
            pltpu.SemaphoreType.DMA((lanes, groups)),
        ],
        compiler_params=pltpu.CompilerParams(vmem_limit_bytes=VMEM_BYTES),
        name="query_grads",
    )(queries, grad_out, *sides)


def key_value_kernel(lanes, other, steps, k_ref, v_ref, state_ref, *rest):
    dk_hbm, dv_hbm, dk_buf, dv_buf, sems = rest[-5:]
    head = state_ref.shape[1]
    base = side_columns(lanes, other, k_ref.shape[1])
    span = dk_buf.shape[1] // steps
    copies = []
    for step in range(steps):
        for h in range(span // head):
            local = pl.ds(step * span + h * head, head)
            cols = pl.ds(pl.multiple_of(base + step * span + h * head, head), head)
            keys = k_ref[:, cols]
            grad_state = state_ref[local, :]
            full = lax.dot_general(
                v_ref[:, cols], grad_state, CONTRACT_COLS, preferred_element_type=jnp.float32
            )
            dk_buf[:, local] = jnp.where(keys > 0, full, 0.0).astype(dk_buf.dtype)
            dv_buf[:, local] = jnp.dot(
                jnp.maximum(keys, 0), grad_state, preferred_element_type=jnp.float32
            ).astype(dv_buf.dtype)
        src = pl.ds(step * span, span)
        dst = pl.ds(pl.multiple_of(base + step * span, head), span)
        for at, (buf, hbm) in enumerate(((dk_buf, dk_hbm), (dv_buf, dv_hbm))):
            copy = pltpu.make_async_copy(buf.at[:, src], hbm.at[:, dst], sems.at[at, step])
            copy.start()
            copies.append(copy)
    for copy in copies:
        copy.wait()


def key_value_grads(keys, values, state, before, lanes, other):
    (tokens, width), head = keys.shape, state.shape[1]
    half = width // lanes
    steps = 2 if (half // head) % 2 == 0 else 1
    return pl.pallas_call(
        functools.partial(key_value_kernel, lanes, other, steps),
        out_shape=(
            jax.ShapeDtypeStruct(keys.shape, keys.dtype),
            jax.ShapeDtypeStruct(values.shape, values.dtype),
        ),
        in_specs=[IN_VMEM, IN_VMEM, IN_VMEM] + [ANYWHERE] * len(before),
        out_specs=(ANYWHERE, ANYWHERE),
        scratch_shapes=[
            pltpu.VMEM((tokens, half), keys.dtype),
            pltpu.VMEM((tokens, half), values.dtype),
            pltpu.SemaphoreType.DMA((2, steps)),
        ],
        input_output_aliases={3 + at: at for at in range(len(before))},
        compiler_params=pltpu.CompilerParams(vmem_limit_bytes=VMEM_BYTES),
        name="key_value_other" if other else "key_value_own",
    )(keys, values, state, *before)


def total_kernel(terms_ref, total_ref):
    total = terms_ref[0].astype(jnp.float32)
    for at in range(1, terms_ref.shape[0]):
        total = total + terms_ref[at].astype(jnp.float32)
    total_ref[...] = total.astype(total_ref.dtype)


def add_up(terms):
    return pl.pallas_call(
        total_kernel,
        out_shape=jax.ShapeDtypeStruct(terms.shape[1:], terms.dtype),
        in_specs=[IN_VMEM],
        out_specs=IN_VMEM,
        compiler_params=pltpu.CompilerParams(vmem_limit_bytes=VMEM_BYTES),
        name="add_up",
    )(terms)


def suffix_kernel(terms_ref, sums_ref):
    last = terms_ref.shape[0] - 1
    total = terms_ref[last].astype(jnp.float32)
    sums_ref[last] = total.astype(sums_ref.dtype)
    for block in range(last - 1, -1, -1):
        total = total + terms_ref[block].astype(jnp.float32)
        sums_ref[block] = total.astype(sums_ref.dtype)


def suffix_sums(share, blocks):
    if blocks == 1:
        return share
    rows, head = share.shape
    terms = lax.all_to_all(share.reshape(blocks, rows // blocks, head), "tm", 0, 0)
    sums = pl.pallas_call(
        suffix_kernel,
        out_shape=jax.ShapeDtypeStruct(terms.shape, terms.dtype),
        in_specs=[IN_VMEM],
        out_specs=IN_VMEM,
        compiler_params=pltpu.CompilerParams(vmem_limit_bytes=VMEM_BYTES),
        name="suffix_sums",
    )(terms)
    return lax.all_to_all(sums, "tm", 0, 0).reshape(rows, head)


def per_device(queries, keys, values, grad_out, saved_state):
    heads, _, head = saved_state.shape[1:]
    blocks, devices = lax.axis_size("tm"), lax.axis_size("space")
    lanes = 2 if devices % 2 == 0 and heads % 2 == 0 else 1
    groups = devices // lanes
    scale = 1.0 / math.sqrt(queries.shape[0] * blocks * devices * head)

    saved = [gather_groups(saved_state[0], lanes, groups)]
    own = partial_products(queries, grad_out, head, lanes, False, scale, jnp.float32)
    if lanes > 1:
        send = partial_products(queries, grad_out, head, lanes, True, scale, jnp.bfloat16)
        own = own + swap_lanes(send, lanes, groups).astype(jnp.float32)
        saved.append(swap_lanes(saved[0], lanes, groups))
    pieces = own.astype(jnp.bfloat16).reshape(groups, -1, head)
    share = add_up(exchange_groups(pieces, lanes, groups))
    grad_q = query_grads(queries, grad_out, saved)
    grad_state = gather_groups(suffix_sums(share, blocks), lanes, groups).reshape(-1, head)
    grads = key_value_grads(keys, values, grad_state, (), lanes, False)
    if lanes > 1:
        swapped = swap_lanes(grad_state, lanes, groups)
        grads = key_value_grads(keys, values, swapped, grads, lanes, True)
    return grad_q, *grads


def solution(mesh):
    tokens = P(("tm", "space"), None)
    return jax.shard_map(
        per_device,
        mesh=mesh,
        in_specs=(tokens, tokens, tokens, tokens, P("tm", None, "space", None)),
        out_specs=(tokens, tokens, tokens),
        check_vma=False,
    )
```

```python
import functools
import math

import jax
import jax.numpy as jnp
from jax import lax
from jax.experimental import pallas as pl
from jax.experimental.pallas import tpu as pltpu
from jax.sharding import PartitionSpec as P

CONTRACT_ROWS = (((0,), (0,)), ((), ()))
CONTRACT_COLS = (((1,), (1,)), ((), ()))
VMEM_BYTES = 16 * 1024 * 1024
ANYWHERE = pl.BlockSpec(memory_space=pl.ANY)
IN_VMEM = pl.BlockSpec(memory_space=pltpu.VMEM)


def power_of_two(count):
    return count & (count - 1) == 0


def partner(group, hop, groups):
    if power_of_two(groups):
        return group ^ hop
    return (group + hop) % groups


def source(group, hop, groups):
    if power_of_two(groups):
        return group ^ hop
    return (group - hop + groups) % groups


def cost(flops, *arrays):
    moved = sum(array.size * array.dtype.itemsize for array in arrays)
    return pl.CostEstimate(flops=flops, bytes_accessed=moved, transcendentals=0)


def place_on_space(lanes):
    index = lax.axis_index("space")
    return index // lanes, index % lanes


def swap_lanes(value, lanes, groups):
    pairs = [(g * lanes + c, g * lanes + 1 - c) for g in range(groups) for c in range(lanes)]
    return lax.ppermute(value, "space", pairs)


def hop_groups(value, hop, lanes, groups):
    pairs = [
        (g * lanes + c, partner(g, hop, groups) * lanes + c)
        for g in range(groups)
        for c in range(lanes)
    ]
    return lax.ppermute(value, "space", pairs)


def products(scale, q_ref, o_ref, cols):
    return scale * lax.dot_general(
        jnp.maximum(q_ref[:, cols], 0),
        o_ref[:, cols],
        CONTRACT_ROWS,
        preferred_element_type=jnp.float32,
    )


def partial_own_kernel(lanes, scale, q_ref, o_ref, part_ref):
    span, head = part_ref.shape
    _, lane = place_on_space(lanes)
    for h in range(span // head):
        cols = pl.ds(pl.multiple_of(lane * span + h * head, head), head)
        part_ref[pl.ds(h * head, head), :] = products(scale, q_ref, o_ref, cols)


def partial_other_kernel(lanes, groups, scale, *refs):
    inputs, part_ref, outs, total = refs[: 2 * lanes - 2], refs[2 * lanes - 2], refs[2 * lanes - 1 : -1], refs[-1]
    span, head = total.shape
    group, lane = place_on_space(lanes)
    for h in range(span // head):
        rows = pl.ds(h * head, head)
        cols = pl.ds(pl.multiple_of(lane * span + h * head, head), head)
        value = part_ref[rows, :]
        for q_ref, o_ref in zip(inputs[::2], inputs[1::2]):
            value = value + products(scale, q_ref, o_ref, cols)
        total[rows, :] = value
    rows = outs[0].shape[0]
    for hop, out_ref in enumerate(outs):
        there = partner(group, hop, groups)
        out_ref[...] = total[pl.ds(pl.multiple_of(there * rows, rows), rows), :].astype(
            out_ref.dtype
        )


def partial_products(queries, grad_out, head, lanes, groups, scale):
    tokens, width = queries.shape
    span = width // lanes
    rows = span // groups
    inputs = []
    if lanes > 1:
        inputs = [swap_lanes(queries, lanes, groups), swap_lanes(grad_out, lanes, groups)]
    params = pltpu.CompilerParams(vmem_limit_bytes=VMEM_BYTES)
    part = pl.pallas_call(
        functools.partial(partial_own_kernel, lanes, scale),
        out_shape=jax.ShapeDtypeStruct((span, head), jnp.float32),
        in_specs=[IN_VMEM, IN_VMEM],
        out_specs=IN_VMEM,
        compiler_params=params,
        cost_estimate=cost(2 * tokens * span * head, queries, grad_out),
        name="partial_own",
    )(queries, grad_out)
    outs = [jax.ShapeDtypeStruct((rows, head), jnp.float32)]
    outs += [jax.ShapeDtypeStruct((rows, head), jnp.bfloat16)] * (groups - 1)
    return pl.pallas_call(
        functools.partial(partial_other_kernel, lanes, groups, scale),
        out_shape=outs,
        in_specs=[IN_VMEM] * (len(inputs) + 1),
        out_specs=[IN_VMEM] * len(outs),
        scratch_shapes=[pltpu.VMEM((span, head), jnp.float32)],
        compiler_params=params,
        cost_estimate=cost(2 * tokens * span * head, *inputs),
        name="partial_other",
    )(*inputs, part)


def query_kernel(lanes, groups, q_ref, o_ref, *rest):
    pieces, (dq_ref, state, sems) = rest[:-3], rest[-3:]
    head = state.shape[1]
    rows = pieces[0].shape[1]
    group, lane = place_on_space(lanes)
    copies = []
    for at, piece in enumerate(pieces):
        there = lane if at < groups else 1 - lane
        owner = source(group, at % groups, groups) * lanes + there
        place = pl.ds(pl.multiple_of(owner * rows, rows), rows)
        if rows % 16 == 0:
            state[:, place, :] = piece[...]
        else:
            copies.append(pltpu.make_async_copy(piece, state.at[:, place, :], sems.at[at]))
    for copy in copies:
        copy.start()
    for copy in copies:
        copy.wait()
    for h in range(state.shape[0]):
        cols = pl.ds(h * head, head)
        full = lax.dot_general(
            o_ref[:, cols], state[h], CONTRACT_COLS, preferred_element_type=jnp.float32
        )
        dq_ref[:, cols] = jnp.where(q_ref[:, cols] > 0, full, 0.0).astype(dq_ref.dtype)


def query_grads(queries, grad_out, pieces, lanes, groups):
    heads, _, head = pieces[0].shape
    return pl.pallas_call(
        functools.partial(query_kernel, lanes, groups),
        out_shape=jax.ShapeDtypeStruct(queries.shape, queries.dtype),
        in_specs=[IN_VMEM] * (2 + len(pieces)),
        out_specs=IN_VMEM,
        scratch_shapes=[
            pltpu.VMEM((heads, head, head), pieces[0].dtype),
            pltpu.SemaphoreType.DMA((len(pieces),)),
        ],
        compiler_params=pltpu.CompilerParams(vmem_limit_bytes=VMEM_BYTES),
        cost_estimate=cost(2 * queries.size * head, queries, queries, grad_out, *pieces),
        name="query_grads",
    )(queries, grad_out, *pieces)


def key_value_kernel(lanes, groups, other, steps, k_ref, v_ref, *rest):
    pieces = rest[:groups]
    dk_hbm, dv_hbm, state, dk_buf, dv_buf, sems = rest[-6:]
    head, rows = state.shape[1], pieces[0].shape[0]
    group, lane = place_on_space(lanes)
    base = (1 - lane if other else lane) * state.shape[0]
    for hop, piece in enumerate(pieces):
        owner = source(group, hop, groups)
        state[pl.ds(pl.multiple_of(owner * rows, rows), rows), :] = piece[...]
    span = state.shape[0] // steps
    copies = []
    for step in range(steps):
        for h in range(span // head):
            local = pl.ds(step * span + h * head, head)
            cols = pl.ds(pl.multiple_of(base + step * span + h * head, head), head)
            keys = k_ref[:, cols]
            grad_state = state[local, :]
            full = lax.dot_general(
                v_ref[:, cols], grad_state, CONTRACT_COLS, preferred_element_type=jnp.float32
            )
            dk_buf[:, local] = jnp.where(keys > 0, full, 0.0).astype(dk_buf.dtype)
            dv_buf[:, local] = jnp.dot(
                jnp.maximum(keys, 0), grad_state, preferred_element_type=jnp.float32
            ).astype(dv_buf.dtype)
        src = pl.ds(step * span, span)
        dst = pl.ds(pl.multiple_of(base + step * span, head), span)
        for at, (buf, hbm) in enumerate(((dk_buf, dk_hbm), (dv_buf, dv_hbm))):
            copy = pltpu.make_async_copy(buf.at[:, src], hbm.at[:, dst], sems.at[at, step])
            copy.start()
            copies.append(copy)
    for copy in copies:
        copy.wait()


def key_value_grads(keys, values, pieces, before, lanes, groups):
    (tokens, width), (_, head) = keys.shape, pieces[0].shape
    half = width // lanes
    other = len(before) > 0
    steps = 2 if (half // head) % 2 == 0 else 1
    return pl.pallas_call(
        functools.partial(key_value_kernel, lanes, groups, other, steps),
        out_shape=(
            jax.ShapeDtypeStruct(keys.shape, keys.dtype),
            jax.ShapeDtypeStruct(values.shape, values.dtype),
        ),
        in_specs=[IN_VMEM] * (2 + groups) + [ANYWHERE] * len(before),
        out_specs=(ANYWHERE, ANYWHERE),
        scratch_shapes=[
            pltpu.VMEM((half, head), pieces[0].dtype),
            pltpu.VMEM((tokens, half), keys.dtype),
            pltpu.VMEM((tokens, half), values.dtype),
            pltpu.SemaphoreType.DMA((2, steps)),
        ],
        input_output_aliases={2 + groups + at: at for at in range(len(before))},
        compiler_params=pltpu.CompilerParams(vmem_limit_bytes=VMEM_BYTES),
        cost_estimate=cost(2 * keys.size * head, keys, values),
        name="key_value_other" if other else "key_value_own",
    )(keys, values, *pieces, *before)


def suffix_sum(share, blocks):
    block = lax.axis_index("tm")
    suffix = share
    if power_of_two(blocks):
        total, hop = share, 1
        while hop < blocks:
            met = lax.ppermute(
                total.astype(jnp.bfloat16), "tm", [(b, b ^ hop) for b in range(blocks)]
            ).astype(jnp.float32)
            suffix = suffix + jnp.where(block & hop == 0, met, 0.0)
            total = total + met
            hop *= 2
    else:
        narrow = share.astype(jnp.bfloat16)
        for hop in range(1, blocks):
            later = lax.ppermute(narrow, "tm", [(b, b - hop) for b in range(hop, blocks)])
            suffix = suffix + later.astype(jnp.float32)
    return suffix.astype(jnp.bfloat16)


def per_device(queries, keys, values, grad_out, saved_state):
    heads, _, head = saved_state.shape[1:]
    blocks, devices = lax.axis_size("tm"), lax.axis_size("space")
    lanes = 2 if devices % 2 == 0 and heads % 2 == 0 else 1
    groups = devices // lanes
    scale = 1.0 / math.sqrt(queries.shape[0] * blocks * devices * head)

    share, *sends = partial_products(queries, grad_out, head, lanes, groups, scale)
    for hop, send in enumerate(sends, 1):
        share = share + hop_groups(send, hop, lanes, groups).astype(jnp.float32)

    def gather_space(value):
        near = [value] + [hop_groups(value, hop, lanes, groups) for hop in range(1, groups)]
        far = [swap_lanes(piece, lanes, groups) for piece in near] if lanes > 1 else []
        return near, far

    near, far = gather_space(saved_state[0])
    grad_q = query_grads(queries, grad_out, near + far, lanes, groups)
    near, far = gather_space(suffix_sum(share, blocks))
    grads = key_value_grads(keys, values, near, (), lanes, groups)
    if lanes > 1:
        grads = key_value_grads(keys, values, far, grads, lanes, groups)
    return grad_q, *grads


def solution(mesh):
    tokens = P(("tm", "space"), None)
    return jax.shard_map(
        per_device,
        mesh=mesh,
        in_specs=(tokens, tokens, tokens, tokens, P("tm", None, "space", None)),
        out_specs=(tokens, tokens, tokens),
        check_vma=False,
    )
```

```python
import functools
import math

import jax
import jax.numpy as jnp
from jax import lax
from jax.experimental import pallas as pl
from jax.experimental.pallas import tpu as pltpu
from jax.sharding import PartitionSpec as P

CONTRACT_ROWS = (((0,), (0,)), ((), ()))
CONTRACT_COLS = (((1,), (1,)), ((), ()))
VMEM_BYTES = 16 * 1024 * 1024
ANYWHERE = pl.BlockSpec(memory_space=pl.ANY)
IN_VMEM = pl.BlockSpec(memory_space=pltpu.VMEM)


def power_of_two(count):
    return count & (count - 1) == 0


def partner(group, hop, groups):
    if power_of_two(groups):
        return group ^ hop
    return (group + hop) % groups


def source(group, hop, groups):
    if power_of_two(groups):
        return group ^ hop
    return (group - hop + groups) % groups


def cost(flops, *arrays):
    moved = sum(array.size * array.dtype.itemsize for array in arrays)
    return pl.CostEstimate(flops=flops, bytes_accessed=moved, transcendentals=0)


def after(value, earlier):
    return lax.optimization_barrier((value, earlier))[0]


def place_on_space(lanes):
    index = lax.axis_index("space")
    return index // lanes, index % lanes


def swap_lanes(value, lanes, groups):
    pairs = [(g * lanes + c, g * lanes + 1 - c) for g in range(groups) for c in range(lanes)]
    return lax.ppermute(value, "space", pairs)


def hop_groups(value, hop, lanes, groups):
    pairs = [
        (g * lanes + c, partner(g, hop, groups) * lanes + c)
        for g in range(groups)
        for c in range(lanes)
    ]
    return lax.ppermute(value, "space", pairs)


def gather_groups(value, waits, lanes, groups):
    if power_of_two(groups):
        for step in range(groups.bit_length() - 1):
            if waits[min(step, len(waits) - 1)] is not None:
                value = after(value, waits[min(step, len(waits) - 1)])
            value = jnp.concatenate([value, hop_groups(value, 1 << step, lanes, groups)])
        return value
    return jnp.concatenate(
        [value] + [hop_groups(value, hop, lanes, groups) for hop in range(1, groups)]
    )


def products(scale, q_ref, o_ref, cols):
    return scale * lax.dot_general(
        jnp.maximum(q_ref[:, cols], 0),
        o_ref[:, cols],
        CONTRACT_ROWS,
        preferred_element_type=jnp.float32,
    )


def partial_own_kernel(lanes, scale, q_ref, o_ref, part_ref):
    span, head = part_ref.shape
    _, lane = place_on_space(lanes)
    for h in range(span // head):
        cols = pl.ds(pl.multiple_of(lane * span + h * head, head), head)
        part_ref[pl.ds(h * head, head), :] = products(scale, q_ref, o_ref, cols)


def partial_other_kernel(lanes, groups, scale, *refs):
    inputs, part_ref, outs, total = (
        refs[: 2 * lanes - 2],
        refs[2 * lanes - 2],
        refs[2 * lanes - 1 : -1],
        refs[-1],
    )
    span, head = total.shape
    group, lane = place_on_space(lanes)
    for h in range(span // head):
        rows = pl.ds(h * head, head)
        cols = pl.ds(pl.multiple_of(lane * span + h * head, head), head)
        value = part_ref[rows, :]
        for q_ref, o_ref in zip(inputs[::2], inputs[1::2]):
            value = value + products(scale, q_ref, o_ref, cols)
        total[rows, :] = value
    rows = outs[0].shape[0]
    for at, out_ref in enumerate(outs):
        chunk, hop = at // groups, at % groups
        there = (chunk * groups + partner(group, hop, groups)) * rows
        out_ref[...] = total[pl.ds(pl.multiple_of(there, rows), rows), :].astype(out_ref.dtype)


def partial_products(queries, grad_out, head, lanes, groups, chunks, scale):
    tokens, width = queries.shape
    span = width // lanes
    rows = span // groups // chunks
    inputs = []
    if lanes > 1:
        inputs = [swap_lanes(queries, lanes, groups), swap_lanes(grad_out, lanes, groups)]
    params = pltpu.CompilerParams(vmem_limit_bytes=VMEM_BYTES)
    part = pl.pallas_call(
        functools.partial(partial_own_kernel, lanes, scale),
        out_shape=jax.ShapeDtypeStruct((span, head), jnp.float32),
        in_specs=[IN_VMEM, IN_VMEM],
        out_specs=IN_VMEM,
        compiler_params=params,
        cost_estimate=cost(2 * tokens * span * head, queries, grad_out),
        name="partial_own",
    )(queries, grad_out)
    outs = [jax.ShapeDtypeStruct((rows, head), jnp.float32)]
    outs += [jax.ShapeDtypeStruct((rows, head), jnp.bfloat16)] * (groups - 1)
    outs = pl.pallas_call(
        functools.partial(partial_other_kernel, lanes, groups, scale),
        out_shape=outs * chunks,
        in_specs=[IN_VMEM] * (len(inputs) + 1),
        out_specs=[IN_VMEM] * (groups * chunks),
        scratch_shapes=[pltpu.VMEM((span, head), jnp.float32)],
        compiler_params=params,
        cost_estimate=cost(2 * tokens * span * head, *inputs),
        name="partial_other",
    )(*inputs, part)
    return [outs[chunk * groups : (chunk + 1) * groups] for chunk in range(chunks)]


def query_kernel(lanes, q_ref, o_ref, *rest):
    sides, (dq_ref, state, sems) = rest[:lanes], rest[lanes:]
    head = state.shape[1]
    groups, _, rows, _ = sides[0].shape
    group, lane = place_on_space(lanes)
    copies = []
    for other, side in enumerate(sides):
        there = 1 - lane if other else lane
        for hop in range(groups):
            owner = source(group, hop, groups) * lanes + there
            place = pl.ds(pl.multiple_of(owner * rows, rows), rows)
            if rows % 16 == 0:
                state[:, place, :] = side[hop]
            else:
                copies.append(
                    pltpu.make_async_copy(side.at[hop], state.at[:, place, :], sems.at[other, hop])
                )
    for copy in copies:
        copy.start()
    for copy in copies:
        copy.wait()
    for h in range(state.shape[0]):
        cols = pl.ds(h * head, head)
        full = lax.dot_general(
            o_ref[:, cols], state[h], CONTRACT_COLS, preferred_element_type=jnp.float32
        )
        dq_ref[:, cols] = jnp.where(q_ref[:, cols] > 0, full, 0.0).astype(dq_ref.dtype)


def query_grads(queries, grad_out, sides):
    lanes, (groups, heads, _, head) = len(sides), sides[0].shape
    return pl.pallas_call(
        functools.partial(query_kernel, lanes),
        out_shape=jax.ShapeDtypeStruct(queries.shape, queries.dtype),
        in_specs=[IN_VMEM] * (2 + lanes),
        out_specs=IN_VMEM,
        scratch_shapes=[
            pltpu.VMEM((heads, head, head), sides[0].dtype),
            pltpu.SemaphoreType.DMA((lanes, groups)),
        ],
        compiler_params=pltpu.CompilerParams(vmem_limit_bytes=VMEM_BYTES),
        cost_estimate=cost(2 * queries.size * head, queries, queries, grad_out, *sides),
        name="query_grads",
    )(queries, grad_out, *sides)


def key_value_kernel(lanes, other, k_ref, v_ref, *rest):
    dk_hbm, dv_hbm, state, dk_buf, dv_buf, sems = rest[-6:]
    chunks, span, head = state.shape
    sides = rest[:chunks]
    groups, rows, _ = sides[0].shape
    group, lane = place_on_space(lanes)
    copies = []
    for chunk, side in enumerate(sides):
        for hop in range(groups):
            owner = source(group, hop, groups)
            state[chunk, pl.ds(pl.multiple_of(owner * rows, rows), rows), :] = side[hop]
        base = ((1 - lane if other else lane) * chunks + chunk) * span
        for h in range(span // head):
            local = pl.ds(h * head, head)
            cols = pl.ds(pl.multiple_of(base + h * head, head), head)
            keys = k_ref[:, cols]
            grad_state = state[chunk, local, :]
            full = lax.dot_general(
                v_ref[:, cols], grad_state, CONTRACT_COLS, preferred_element_type=jnp.float32
            )
            dk_buf[chunk, :, local] = jnp.where(keys > 0, full, 0.0).astype(dk_buf.dtype)
            dv_buf[chunk, :, local] = jnp.dot(
                jnp.maximum(keys, 0), grad_state, preferred_element_type=jnp.float32
            ).astype(dv_buf.dtype)
        dst = pl.ds(pl.multiple_of(base, head), span)
        for kind, (buf, hbm) in enumerate(((dk_buf, dk_hbm), (dv_buf, dv_hbm))):
            copy = pltpu.make_async_copy(buf.at[chunk], hbm.at[:, dst], sems.at[kind, chunk])
            copy.start()
            copies.append(copy)
    for copy in copies:
        copy.wait()


def key_value_grads(keys, values, sides, other, before, lanes):
    tokens, (groups, rows, head) = keys.shape[0], sides[0].shape
    span, chunks = groups * rows, len(sides)
    return pl.pallas_call(
        functools.partial(key_value_kernel, lanes, other),
        out_shape=(
            jax.ShapeDtypeStruct(keys.shape, keys.dtype),
            jax.ShapeDtypeStruct(values.shape, values.dtype),
        ),
        in_specs=[IN_VMEM] * (2 + chunks) + [ANYWHERE] * len(before),
        out_specs=(ANYWHERE, ANYWHERE),
        scratch_shapes=[
            pltpu.VMEM((chunks, span, head), sides[0].dtype),
            pltpu.VMEM((chunks, tokens, span), keys.dtype),
            pltpu.VMEM((chunks, tokens, span), values.dtype),
            pltpu.SemaphoreType.DMA((2, chunks)),
        ],
        input_output_aliases={2 + chunks + at: at for at in range(len(before))},
        compiler_params=pltpu.CompilerParams(vmem_limit_bytes=VMEM_BYTES),
        cost_estimate=cost(4 * tokens * span * head * chunks, *sides, *sides),
        name="key_value_other" if other else "key_value_own",
    )(keys, values, *sides, *before)


def suffix_sums(shares, blocks):
    block = lax.axis_index("tm")
    suffixes, totals, first = list(shares), list(shares), shares
    if power_of_two(blocks):
        hop = 1
        while hop < blocks:
            pairs = [(b, b ^ hop) for b in range(blocks)]
            for at, total in enumerate(totals):
                met = lax.ppermute(total.astype(jnp.bfloat16), "tm", pairs).astype(jnp.float32)
                suffixes[at] = suffixes[at] + jnp.where(block & hop == 0, met, 0.0)
                totals[at] = total + met
            first = list(totals) if hop == 1 else first
            hop *= 2
    else:
        for hop in range(1, blocks):
            pairs = [(b, b - hop) for b in range(hop, blocks)]
            for at, share in enumerate(shares):
                later = lax.ppermute(share.astype(jnp.bfloat16), "tm", pairs)
                suffixes[at] = suffixes[at] + later.astype(jnp.float32)
    return [suffix.astype(jnp.bfloat16) for suffix in suffixes], first


def per_device(queries, keys, values, grad_out, saved_state):
    heads, _, head = saved_state.shape[1:]
    blocks, devices = lax.axis_size("tm"), lax.axis_size("space")
    lanes = 2 if devices % 2 == 0 and heads % 2 == 0 else 1
    groups = devices // lanes
    span = heads // lanes
    chunks = 2 if span % 2 == 0 and (span * head // groups) % 32 == 0 else 1
    scale = 1.0 / math.sqrt(queries.shape[0] * blocks * devices * head)

    parts = partial_products(queries, grad_out, head, lanes, groups, chunks, scale)
    shares = []
    for share, *sends in parts:
        for hop, send in enumerate(sends, 1):
            share = share + hop_groups(send, hop, lanes, groups).astype(jnp.float32)
        shares.append(share)
    sums, first = suffix_sums(shares, blocks)
    states = [
        [own] + [hop_groups(own, hop, lanes, groups) for hop in range(1, groups)] for own in sums
    ]

    saved = gather_groups(saved_state, [None, shares], lanes, groups)
    sides = [saved]
    if lanes > 1:
        sides.append(swap_lanes(saved, lanes, groups))
    grad_q = query_grads(queries, grad_out, sides)

    near = [jnp.stack(after(pieces, (grad_q, states[-1]))) for pieces in states]
    far = [swap_lanes(side, lanes, groups) for side in near] if lanes > 1 else []
    grads = key_value_grads(keys, values, near, False, (), lanes)
    if lanes > 1:
        grads = key_value_grads(keys, values, far, True, grads, lanes)
    return grad_q, *grads


def solution(mesh):
    tokens = P(("tm", "space"), None)
    return jax.shard_map(
        per_device,
        mesh=mesh,
        in_specs=(tokens, tokens, tokens, tokens, P("tm", None, "space", None)),
        out_specs=(tokens, tokens, tokens),
        check_vma=False,
    )
```

```python
import functools
import math

import jax
import jax.numpy as jnp
from jax import lax
from jax.experimental import pallas as pl
from jax.experimental.pallas import tpu as pltpu
from jax.sharding import PartitionSpec as P

CONTRACT_ROWS = (((0,), (0,)), ((), ()))
CONTRACT_COLS = (((1,), (1,)), ((), ()))
VMEM_BYTES = 16 * 1024 * 1024
ANYWHERE = pl.BlockSpec(memory_space=pl.ANY)
IN_VMEM = pl.BlockSpec(memory_space=pltpu.VMEM)


def power_of_two(count):
    return count & (count - 1) == 0


def partner(group, hop, groups):
    if power_of_two(groups):
        return group ^ hop
    return (group + hop) % groups


def source(group, hop, groups):
    if power_of_two(groups):
        return group ^ hop
    return (group - hop + groups) % groups


def cost(flops, *arrays):
    moved = sum(array.size * array.dtype.itemsize for array in arrays)
    return pl.CostEstimate(flops=flops, bytes_accessed=moved, transcendentals=0)


def after(value, earlier):
    return lax.optimization_barrier((value, earlier))[0]


def place_on_space(lanes):
    index = lax.axis_index("space")
    return lax.div(index, lanes), lax.rem(index, lanes)


def swap_lanes(value, lanes, groups):
    pairs = [(g * lanes + c, g * lanes + 1 - c) for g in range(groups) for c in range(lanes)]
    return lax.ppermute(value, "space", pairs)


def hop_groups(value, hop, lanes, groups):
    pairs = [
        (g * lanes + c, partner(g, hop, groups) * lanes + c)
        for g in range(groups)
        for c in range(lanes)
    ]
    return lax.ppermute(value, "space", pairs)


def gather_groups(value, waits, lanes, groups):
    if power_of_two(groups):
        for step in range(groups.bit_length() - 1):
            if waits[min(step, len(waits) - 1)] is not None:
                value = after(value, waits[min(step, len(waits) - 1)])
            value = jnp.concatenate([value, hop_groups(value, 1 << step, lanes, groups)])
        return value
    return jnp.concatenate(
        [value] + [hop_groups(value, hop, lanes, groups) for hop in range(1, groups)]
    )


def products(scale, q_ref, o_ref, cols):
    return scale * lax.dot_general(
        jnp.maximum(q_ref[:, cols], 0),
        o_ref[:, cols],
        CONTRACT_ROWS,
        preferred_element_type=jnp.float32,
    )


def partial_own_kernel(scale, q_ref, o_ref, part_ref):
    span, head = part_ref.shape
    for h in range(span // head):
        cols = pl.ds(h * head, head)
        part_ref[cols, :] = products(scale, q_ref, o_ref, cols)


def partial_other_kernel(lanes, groups, scale, *refs):
    part_ref, inputs, outs, total = refs[0], refs[1:lanes], refs[lanes:-1], refs[-1]
    span, head = total.shape
    group, _ = place_on_space(lanes)
    for h in range(span // head):
        cols = pl.ds(h * head, head)
        value = part_ref[cols, :]
        for both in inputs:
            value = value + products(scale, both.at[0], both.at[1], cols)
        total[cols, :] = value
    rows = outs[0].shape[0]
    for hop, out_ref in enumerate(outs):
        there = partner(group, hop, groups) * rows
        out_ref[...] = total[pl.ds(pl.multiple_of(there, rows), rows), :].astype(out_ref.dtype)


def partial_products(queries, grad_out, head, lanes, groups, scale):
    tokens, width = queries.shape
    span = width // lanes
    rows = span // groups
    _, lane = place_on_space(lanes)

    def half(array, side):
        starts = (jnp.zeros_like(side), side * span)
        return lax.dynamic_slice(array, starts, (tokens, span), allow_negative_indices=False)

    inputs = []
    if lanes > 1:
        both = jnp.stack([half(queries, 1 - lane), half(grad_out, 1 - lane)])
        inputs = [swap_lanes(both, lanes, groups)]
    params = pltpu.CompilerParams(vmem_limit_bytes=VMEM_BYTES)
    part = pl.pallas_call(
        functools.partial(partial_own_kernel, scale),
        out_shape=jax.ShapeDtypeStruct((span, head), jnp.float32),
        in_specs=[IN_VMEM, IN_VMEM],
        out_specs=IN_VMEM,
        compiler_params=params,
        cost_estimate=cost(2 * tokens * span * head, queries, grad_out),
        name="partial_own",
    )(half(queries, lane), half(grad_out, lane))
    outs = [jax.ShapeDtypeStruct((rows, head), jnp.float32)]
    outs += [jax.ShapeDtypeStruct((rows, head), jnp.bfloat16)] * (groups - 1)
    return pl.pallas_call(
        functools.partial(partial_other_kernel, lanes, groups, scale),
        out_shape=outs,
        in_specs=[IN_VMEM] * lanes,
        out_specs=[IN_VMEM] * groups,
        scratch_shapes=[pltpu.VMEM((span, head), jnp.float32)],
        compiler_params=params,
        cost_estimate=cost(2 * tokens * span * head, *inputs),
        name="partial_other",
    )(part, *inputs)


def query_kernel(lanes, q_ref, o_ref, *rest):
    sides, (dq_ref, state, sems) = rest[:lanes], rest[lanes:]
    head = state.shape[1]
    groups, _, rows, _ = sides[0].shape
    group, lane = place_on_space(lanes)
    copies = []
    for other, side in enumerate(sides):
        there = 1 - lane if other else lane
        for hop in range(groups):
            owner = source(group, hop, groups) * lanes + there
            place = pl.ds(pl.multiple_of(owner * rows, rows), rows)
            if rows % 16 == 0:
                state[:, place, :] = side[hop]
            else:
                copies.append(
                    pltpu.make_async_copy(side.at[hop], state.at[:, place, :], sems.at[other, hop])
                )
    for copy in copies:
        copy.start()
    for copy in copies:
        copy.wait()
    for h in range(state.shape[0]):
        cols = pl.ds(h * head, head)
        full = lax.dot_general(
            o_ref[:, cols], state[h], CONTRACT_COLS, preferred_element_type=jnp.float32
        )
        dq_ref[:, cols] = jnp.where(q_ref[:, cols] > 0, full, 0.0).astype(dq_ref.dtype)


def query_grads(queries, grad_out, sides):
    lanes, (groups, heads, _, head) = len(sides), sides[0].shape
    return pl.pallas_call(
        functools.partial(query_kernel, lanes),
        out_shape=jax.ShapeDtypeStruct(queries.shape, queries.dtype),
        in_specs=[IN_VMEM] * (2 + lanes),
        out_specs=IN_VMEM,
        scratch_shapes=[
            pltpu.VMEM((heads, head, head), sides[0].dtype),
            pltpu.SemaphoreType.DMA((lanes, groups)),
        ],
        compiler_params=pltpu.CompilerParams(vmem_limit_bytes=VMEM_BYTES),
        cost_estimate=cost(2 * queries.size * head, queries, queries, grad_out, *sides),
        name="query_grads",
    )(queries, grad_out, *sides)


def key_value_kernel(lanes, other, steps, k_ref, v_ref, state_ref, *rest):
    dk_hbm, dv_hbm, state, dk_buf, dv_buf, sems = rest[-6:]
    span, head = state.shape
    groups, rows, _ = state_ref.shape
    group, lane = place_on_space(lanes)
    for hop in range(groups):
        owner = source(group, hop, groups)
        state[pl.ds(pl.multiple_of(owner * rows, rows), rows), :] = state_ref[hop]
    base = (1 - lane if other else lane) * span
    part = span // steps
    copies = []
    for step in range(steps):
        for h in range(part // head):
            local = pl.ds(step * part + h * head, head)
            cols = pl.ds(pl.multiple_of(base + step * part + h * head, head), head)
            keys = k_ref[:, cols]
            grad_state = state[local, :]
            full = lax.dot_general(
                v_ref[:, cols], grad_state, CONTRACT_COLS, preferred_element_type=jnp.float32
            )
            dk_buf[:, local] = jnp.where(keys > 0, full, 0.0).astype(dk_buf.dtype)
            dv_buf[:, local] = jnp.dot(
                jnp.maximum(keys, 0), grad_state, preferred_element_type=jnp.float32
            ).astype(dv_buf.dtype)
        src = pl.ds(step * part, part)
        dst = pl.ds(pl.multiple_of(base + step * part, head), part)
        for kind, (buf, hbm) in enumerate(((dk_buf, dk_hbm), (dv_buf, dv_hbm))):
            copy = pltpu.make_async_copy(buf.at[:, src], hbm.at[:, dst], sems.at[kind, step])
            copy.start()
            copies.append(copy)
    for copy in copies:
        copy.wait()


def key_value_grads(keys, values, state, other, before, lanes):
    tokens, (groups, rows, head) = keys.shape[0], state.shape
    span = groups * rows
    steps = 2 if (span // head) % 2 == 0 else 1
    return pl.pallas_call(
        functools.partial(key_value_kernel, lanes, other, steps),
        out_shape=(
            jax.ShapeDtypeStruct(keys.shape, keys.dtype),
            jax.ShapeDtypeStruct(values.shape, values.dtype),
        ),
        in_specs=[IN_VMEM] * 3 + [ANYWHERE] * len(before),
        out_specs=(ANYWHERE, ANYWHERE),
        scratch_shapes=[
            pltpu.VMEM((span, head), state.dtype),
            pltpu.VMEM((tokens, span), keys.dtype),
            pltpu.VMEM((tokens, span), values.dtype),
            pltpu.SemaphoreType.DMA((2, steps)),
        ],
        input_output_aliases={3 + at: at for at in range(len(before))},
        compiler_params=pltpu.CompilerParams(vmem_limit_bytes=VMEM_BYTES),
        cost_estimate=cost(4 * tokens * span * head, state, state),
        name="key_value_other" if other else "key_value_own",
    )(keys, values, state, *before)


def suffix_sum(share, blocks):
    block = lax.axis_index("tm")
    suffix = total = first = share
    if power_of_two(blocks):
        hop = 1
        while hop < blocks:
            pairs = [(b, b ^ hop) for b in range(blocks)]
            met = lax.ppermute(total.astype(jnp.bfloat16), "tm", pairs).astype(jnp.float32)
            suffix = suffix + jnp.where(block & hop == 0, met, 0.0)
            total = total + met
            first = total if hop == 1 else first
            hop *= 2
    else:
        for hop in range(1, blocks):
            pairs = [(b, b - hop) for b in range(hop, blocks)]
            later = lax.ppermute(share.astype(jnp.bfloat16), "tm", pairs)
            suffix = suffix + later.astype(jnp.float32)
    return suffix.astype(jnp.bfloat16), first


def per_device(queries, keys, values, grad_out, saved_state):
    heads, _, head = saved_state.shape[1:]
    blocks, devices = lax.axis_size("tm"), lax.axis_size("space")
    lanes = 2 if devices % 2 == 0 and heads % 2 == 0 else 1
    groups = devices // lanes
    far_first = range(groups - 1, 0, -1)
    scale = 1.0 / math.sqrt(queries.shape[0] * blocks * devices * head)

    share, *sends = partial_products(queries, grad_out, head, lanes, groups, scale)
    for hop in far_first:
        share = share + hop_groups(sends[hop - 1], hop, lanes, groups).astype(jnp.float32)
    own, first = suffix_sum(share, blocks)
    met = [hop_groups(own, hop, lanes, groups) for hop in far_first]

    saved = gather_groups(saved_state, [None, share], lanes, groups)
    sides = [saved]
    if lanes > 1:
        sides.append(swap_lanes(after(saved, first), lanes, groups))
    grad_q = query_grads(queries, grad_out, sides)

    near = jnp.stack(after([own, *met[::-1]], grad_q))
    grads = key_value_grads(keys, values, near, False, (), lanes)
    if lanes > 1:
        far = swap_lanes(near, lanes, groups)
        grads = key_value_grads(keys, values, far, True, grads, lanes)
    return grad_q, *grads


def solution(mesh):
    tokens = P(("tm", "space"), None)
    return jax.shard_map(
        per_device,
        mesh=mesh,
        in_specs=(tokens, tokens, tokens, tokens, P("tm", None, "space", None)),
        out_specs=(tokens, tokens, tokens),
        check_vma=False,
    )
```

```python
import functools
import math

import jax
import jax.numpy as jnp
from jax import lax
from jax.experimental import pallas as pl
from jax.experimental.pallas import tpu as pltpu
from jax.sharding import PartitionSpec as P

CONTRACT_ROWS = (((0,), (0,)), ((), ()))
CONTRACT_COLS = (((1,), (1,)), ((), ()))
VMEM_BYTES = 16 * 1024 * 1024
ANYWHERE = pl.BlockSpec(memory_space=pl.ANY)
IN_VMEM = pl.BlockSpec(memory_space=pltpu.VMEM)


def power_of_two(count):
    return count & (count - 1) == 0


def partner(group, hop, groups):
    if power_of_two(groups):
        return group ^ hop
    return (group + hop) % groups


def source(group, hop, groups):
    if power_of_two(groups):
        return group ^ hop
    return (group - hop + groups) % groups


def cost(flops, *arrays):
    moved = sum(array.size * array.dtype.itemsize for array in arrays)
    return pl.CostEstimate(flops=flops, bytes_accessed=moved, transcendentals=0)


def after(value, earlier):
    return lax.optimization_barrier((value, earlier))[0]


def place_on_space(lanes):
    index = lax.axis_index("space")
    return lax.div(index, lanes), lax.rem(index, lanes)


def swap_lanes(value, lanes, groups):
    pairs = [(g * lanes + c, g * lanes + 1 - c) for g in range(groups) for c in range(lanes)]
    return lax.ppermute(value, "space", pairs)


def hop_groups(value, hop, lanes, groups):
    pairs = [
        (g * lanes + c, partner(g, hop, groups) * lanes + c)
        for g in range(groups)
        for c in range(lanes)
    ]
    return lax.ppermute(value, "space", pairs)


def gather_groups(value, waits, lanes, groups):
    if power_of_two(groups):
        for step in range(groups.bit_length() - 1):
            value = after(value, waits[min(step, len(waits) - 1)])
            value = jnp.concatenate([value, hop_groups(value, 1 << step, lanes, groups)])
        return value
    return jnp.concatenate(
        [value] + [hop_groups(value, hop, lanes, groups) for hop in range(1, groups)]
    )


def products(scale, queries, grad_out):
    return scale * lax.dot_general(
        jnp.maximum(queries, 0),
        grad_out,
        CONTRACT_ROWS,
        preferred_element_type=jnp.float32,
    )


def partial_own_kernel(lanes, scale, q_ref, o_ref, part_ref):
    span, head = part_ref.shape
    _, lane = place_on_space(lanes)
    for h in range(span // head):
        cols = pl.ds(pl.multiple_of(lane * span + h * head, head), head)
        part_ref[pl.ds(h * head, head), :] = products(scale, q_ref[:, cols], o_ref[:, cols])


def partial_other_kernel(lanes, groups, scale, *refs):
    part_ref, inputs, outs, total = refs[0], refs[1:lanes], refs[lanes:-1], refs[-1]
    span, head = total.shape
    group, _ = place_on_space(lanes)
    for h in range(span // head):
        cols = pl.ds(h * head, head)
        value = part_ref[cols, :]
        for both in inputs:
            value = value + products(scale, both[0, :, cols], both[1, :, cols])
        total[cols, :] = value
    rows = outs[0].shape[0]
    for hop, out_ref in enumerate(outs):
        there = partner(group, hop, groups) * rows
        out_ref[...] = total[pl.ds(pl.multiple_of(there, rows), rows), :].astype(out_ref.dtype)


def partial_products(queries, grad_out, head, lanes, groups, scale):
    tokens, width = queries.shape
    span = width // lanes
    rows = span // groups
    _, lane = place_on_space(lanes)

    def half(array, side):
        starts = (jnp.zeros_like(side), side * span)
        return lax.dynamic_slice(array, starts, (tokens, span), allow_negative_indices=False)

    inputs, mine = [], (queries, grad_out)
    if lanes > 1:
        both = jnp.stack([half(queries, 1 - lane), half(grad_out, 1 - lane)])
        inputs = [swap_lanes(both, lanes, groups)]
        mine = after(mine, both)
    params = pltpu.CompilerParams(vmem_limit_bytes=VMEM_BYTES)
    part = pl.pallas_call(
        functools.partial(partial_own_kernel, lanes, scale),
        out_shape=jax.ShapeDtypeStruct((span, head), jnp.float32),
        in_specs=[IN_VMEM, IN_VMEM],
        out_specs=IN_VMEM,
        compiler_params=params,
        cost_estimate=cost(2 * tokens * span * head, queries, grad_out),
        name="partial_own",
    )(*mine)
    outs = [jax.ShapeDtypeStruct((rows, head), jnp.float32)]
    outs += [jax.ShapeDtypeStruct((rows, head), jnp.bfloat16)] * (groups - 1)
    outs = pl.pallas_call(
        functools.partial(partial_other_kernel, lanes, groups, scale),
        out_shape=outs,
        in_specs=[IN_VMEM] * lanes,
        out_specs=[IN_VMEM] * groups,
        scratch_shapes=[pltpu.VMEM((span, head), jnp.float32)],
        compiler_params=params,
        cost_estimate=cost(2 * tokens * span * head, *inputs),
        name="partial_other",
    )(part, *inputs)
    return part, outs


def query_kernel(lanes, q_ref, o_ref, *rest):
    sides, (dq_ref, state, sems) = rest[:lanes], rest[lanes:]
    head = state.shape[1]
    groups, _, rows, _ = sides[0].shape
    group, lane = place_on_space(lanes)
    copies = []
    for other, side in enumerate(sides):
        there = 1 - lane if other else lane
        for hop in range(groups):
            owner = source(group, hop, groups) * lanes + there
            place = pl.ds(pl.multiple_of(owner * rows, rows), rows)
            if rows % 16 == 0:
                state[:, place, :] = side[hop]
            else:
                copies.append(
                    pltpu.make_async_copy(side.at[hop], state.at[:, place, :], sems.at[other, hop])
                )
    for copy in copies:
        copy.start()
    for copy in copies:
        copy.wait()
    for h in range(state.shape[0]):
        cols = pl.ds(h * head, head)
        full = lax.dot_general(
            o_ref[:, cols], state[h], CONTRACT_COLS, preferred_element_type=jnp.float32
        )
        dq_ref[:, cols] = jnp.where(q_ref[:, cols] > 0, full, 0.0).astype(dq_ref.dtype)


def query_grads(queries, grad_out, sides):
    lanes, (groups, heads, _, head) = len(sides), sides[0].shape
    return pl.pallas_call(
        functools.partial(query_kernel, lanes),
        out_shape=jax.ShapeDtypeStruct(queries.shape, queries.dtype),
        in_specs=[IN_VMEM] * (2 + lanes),
        out_specs=IN_VMEM,
        scratch_shapes=[
            pltpu.VMEM((heads, head, head), sides[0].dtype),
            pltpu.SemaphoreType.DMA((lanes, groups)),
        ],
        compiler_params=pltpu.CompilerParams(vmem_limit_bytes=VMEM_BYTES),
        cost_estimate=cost(2 * queries.size * head, queries, queries, grad_out, *sides),
        name="query_grads",
    )(queries, grad_out, *sides)


def key_value_kernel(lanes, other, steps, k_ref, v_ref, state_ref, *rest):
    dk_hbm, dv_hbm, state, dk_buf, dv_buf, sems = rest[-6:]
    span, head = state.shape
    groups, rows, _ = state_ref.shape
    group, lane = place_on_space(lanes)
    for hop in range(groups):
        owner = source(group, hop, groups)
        state[pl.ds(pl.multiple_of(owner * rows, rows), rows), :] = state_ref[hop]
    base = (1 - lane if other else lane) * span
    part = span // steps
    copies = []
    for step in range(steps):
        for h in range(part // head):
            local = pl.ds(step * part + h * head, head)
            cols = pl.ds(pl.multiple_of(base + step * part + h * head, head), head)
            keys = k_ref[:, cols]
            grad_state = state[local, :]
            full = lax.dot_general(
                v_ref[:, cols], grad_state, CONTRACT_COLS, preferred_element_type=jnp.float32
            )
            dk_buf[:, local] = jnp.where(keys > 0, full, 0.0).astype(dk_buf.dtype)
            dv_buf[:, local] = jnp.dot(
                jnp.maximum(keys, 0), grad_state, preferred_element_type=jnp.float32
            ).astype(dv_buf.dtype)
        src = pl.ds(step * part, part)
        dst = pl.ds(pl.multiple_of(base + step * part, head), part)
        for kind, (buf, hbm) in enumerate(((dk_buf, dk_hbm), (dv_buf, dv_hbm))):
            copy = pltpu.make_async_copy(buf.at[:, src], hbm.at[:, dst], sems.at[kind, step])
            copy.start()
            copies.append(copy)
    for copy in copies:
        copy.wait()


def key_value_grads(keys, values, state, other, before, lanes):
    tokens, (groups, rows, head) = keys.shape[0], state.shape
    span = groups * rows
    steps = 2 if (span // head) % 2 == 0 else 1
    return pl.pallas_call(
        functools.partial(key_value_kernel, lanes, other, steps),
        out_shape=(
            jax.ShapeDtypeStruct(keys.shape, keys.dtype),
            jax.ShapeDtypeStruct(values.shape, values.dtype),
        ),
        in_specs=[IN_VMEM] * 3 + [ANYWHERE] * len(before),
        out_specs=(ANYWHERE, ANYWHERE),
        scratch_shapes=[
            pltpu.VMEM((span, head), state.dtype),
            pltpu.VMEM((tokens, span), keys.dtype),
            pltpu.VMEM((tokens, span), values.dtype),
            pltpu.SemaphoreType.DMA((2, steps)),
        ],
        input_output_aliases={3 + at: at for at in range(len(before))},
        compiler_params=pltpu.CompilerParams(vmem_limit_bytes=VMEM_BYTES),
        cost_estimate=cost(4 * tokens * span * head, state, state),
        name="key_value_other" if other else "key_value_own",
    )(keys, values, state, *before)


def suffix_sum(share, blocks):
    block = lax.axis_index("tm")
    suffix = total = first = share
    if power_of_two(blocks):
        hop = 1
        while hop < blocks:
            pairs = [(b, b ^ hop) for b in range(blocks)]
            met = lax.ppermute(total.astype(jnp.bfloat16), "tm", pairs).astype(jnp.float32)
            suffix = suffix + jnp.where(block & hop == 0, met, 0.0)
            total = total + met
            first = total if hop == 1 else first
            hop *= 2
    else:
        for hop in range(1, blocks):
            pairs = [(b, b - hop) for b in range(hop, blocks)]
            later = lax.ppermute(share.astype(jnp.bfloat16), "tm", pairs)
            suffix = suffix + later.astype(jnp.float32)
    return suffix.astype(jnp.bfloat16), first


def per_device(queries, keys, values, grad_out, saved_state):
    heads, _, head = saved_state.shape[1:]
    blocks, devices = lax.axis_size("tm"), lax.axis_size("space")
    lanes = 2 if devices % 2 == 0 and heads % 2 == 0 else 1
    groups = devices // lanes
    far_first = range(groups - 1, 0, -1)
    scale = 1.0 / math.sqrt(queries.shape[0] * blocks * devices * head)

    part, (share, *sends) = partial_products(queries, grad_out, head, lanes, groups, scale)
    for hop in far_first:
        share = share + hop_groups(sends[hop - 1], hop, lanes, groups).astype(jnp.float32)
    own, first = suffix_sum(share, blocks)
    met = [hop_groups(own, hop, lanes, groups) for hop in far_first]

    saved = gather_groups(saved_state, [part, share], lanes, groups)
    sides = [saved]
    if lanes > 1:
        sides.append(swap_lanes(after(saved, first), lanes, groups))
    grad_q = query_grads(queries, grad_out, sides)

    near = jnp.stack(after([own, *met[::-1]], grad_q))
    grads = key_value_grads(keys, values, near, False, (), lanes)
    if lanes > 1:
        far = swap_lanes(near, lanes, groups)
        grads = key_value_grads(keys, values, far, True, grads, lanes)
    return grad_q, *grads


def solution(mesh):
    tokens = P(("tm", "space"), None)
    return jax.shard_map(
        per_device,
        mesh=mesh,
        in_specs=(tokens, tokens, tokens, tokens, P("tm", None, "space", None)),
        out_specs=(tokens, tokens, tokens),
        check_vma=False,
    )
```

```python
import functools
import math

import jax
import jax.numpy as jnp
from jax import lax
from jax.experimental import pallas as pl
from jax.experimental.pallas import tpu as pltpu
from jax.sharding import PartitionSpec as P

CONTRACT_ROWS = (((0,), (0,)), ((), ()))
CONTRACT_COLS = (((1,), (1,)), ((), ()))
VMEM_BYTES = 16 * 1024 * 1024
ANYWHERE = pl.BlockSpec(memory_space=pl.ANY)
IN_VMEM = pl.BlockSpec(memory_space=pltpu.VMEM)


def power_of_two(count):
    return count & (count - 1) == 0


def partner(group, hop, groups):
    if power_of_two(groups):
        return group ^ hop
    return (group + hop) % groups


def source(group, hop, groups):
    if power_of_two(groups):
        return group ^ hop
    return (group - hop + groups) % groups


def cost(flops, *arrays):
    moved = sum(array.size * array.dtype.itemsize for array in arrays)
    return pl.CostEstimate(flops=flops, bytes_accessed=moved, transcendentals=0)


def after(value, earlier):
    return lax.optimization_barrier((value, earlier))[0]


def odd_bits(value, bits):
    odd = value & 1
    for bit in range(1, bits):
        odd = odd ^ ((value >> bit) & 1)
    return odd


def flip(block, group, lanes, groups, blocks):
    if lanes != 2 or not (power_of_two(groups) and power_of_two(blocks)):
        return 0 * (block + group)
    return (group & 1) ^ odd_bits(block, (blocks - 1).bit_length())


def place(lanes):
    groups, blocks = lax.axis_size("space") // lanes, lax.axis_size("tm")
    index, block = lax.axis_index("space"), lax.axis_index("tm")
    group = lax.div(index, lanes)
    half = lax.rem(index, lanes) ^ flip(block, group, lanes, groups, blocks)
    return group, half, lambda there, half: half ^ flip(block, there, lanes, groups, blocks)


def permute(value, lanes, there):
    blocks, devices = lax.axis_size("tm"), lax.axis_size("space")
    groups = devices // lanes
    pairs = []
    for b in range(blocks):
        for g in range(groups):
            for half in range(lanes):
                if there(b, g, half) is None:
                    continue
                ends = [
                    (at[0] * groups + at[1]) * lanes
                    + (at[2] ^ flip(at[0], at[1], lanes, groups, blocks))
                    for at in ((b, g, half), there(b, g, half))
                ]
                pairs.append(tuple(ends))
    return lax.ppermute(value, ("tm", "space"), pairs)


def swap_halves(value, lanes):
    return permute(value, lanes, lambda b, g, half: (b, g, 1 - half))


def hop_groups(value, hop, lanes, groups):
    return permute(value, lanes, lambda b, g, half: (b, partner(g, hop, groups), half))


def gather_groups(value, waits, lanes, groups):
    if power_of_two(groups):
        for step in range(groups.bit_length() - 1):
            value = after(value, waits[min(step, len(waits) - 1)])
            value = jnp.concatenate([value, hop_groups(value, 1 << step, lanes, groups)])
        return value
    return jnp.concatenate(
        [value] + [hop_groups(value, hop, lanes, groups) for hop in range(1, groups)]
    )


def products(scale, queries, grad_out):
    return scale * lax.dot_general(
        jnp.maximum(queries, 0),
        grad_out,
        CONTRACT_ROWS,
        preferred_element_type=jnp.float32,
    )


def partial_own_kernel(lanes, scale, q_ref, o_ref, part_ref):
    span, head = part_ref.shape
    _, half, _ = place(lanes)
    for h in range(span // head):
        cols = pl.ds(pl.multiple_of(half * span + h * head, head), head)
        part_ref[pl.ds(h * head, head), :] = products(scale, q_ref[:, cols], o_ref[:, cols])


def partial_other_kernel(lanes, groups, scale, *refs):
    part_ref, inputs, outs, total = refs[0], refs[1:lanes], refs[lanes:-1], refs[-1]
    span, head = total.shape
    group, _, _ = place(lanes)
    for h in range(span // head):
        cols = pl.ds(h * head, head)
        value = part_ref[cols, :]
        for both in inputs:
            value = value + products(scale, both[0, :, cols], both[1, :, cols])
        total[cols, :] = value
    rows = outs[0].shape[0]
    for hop, out_ref in enumerate(outs):
        there = partner(group, hop, groups) * rows
        out_ref[...] = total[pl.ds(pl.multiple_of(there, rows), rows), :].astype(out_ref.dtype)


def partial_products(queries, grad_out, head, lanes, groups, scale):
    tokens, width = queries.shape
    span = width // lanes
    rows = span // groups
    _, half, _ = place(lanes)

    def theirs(array):
        starts = (jnp.zeros_like(half), (1 - half) * span)
        return lax.dynamic_slice(array, starts, (tokens, span), allow_negative_indices=False)

    inputs, mine = [], (queries, grad_out)
    if lanes > 1:
        both = jnp.stack([theirs(queries), theirs(grad_out)])
        inputs = [swap_halves(both, lanes)]
        mine = after(mine, both)
    params = pltpu.CompilerParams(vmem_limit_bytes=VMEM_BYTES)
    part = pl.pallas_call(
        functools.partial(partial_own_kernel, lanes, scale),
        out_shape=jax.ShapeDtypeStruct((span, head), jnp.float32),
        in_specs=[IN_VMEM, IN_VMEM],
        out_specs=IN_VMEM,
        compiler_params=params,
        cost_estimate=cost(2 * tokens * span * head, queries, grad_out),
        name="partial_own",
    )(*mine)
    outs = [jax.ShapeDtypeStruct((rows, head), jnp.float32)]
    outs += [jax.ShapeDtypeStruct((rows, head), jnp.bfloat16)] * (groups - 1)
    outs = pl.pallas_call(
        functools.partial(partial_other_kernel, lanes, groups, scale),
        out_shape=outs,
        in_specs=[IN_VMEM] * lanes,
        out_specs=[IN_VMEM] * groups,
        scratch_shapes=[pltpu.VMEM((span, head), jnp.float32)],
        compiler_params=params,
        cost_estimate=cost(2 * tokens * span * head, *inputs),
        name="partial_other",
    )(part, *inputs)
    return part, outs


def query_kernel(lanes, q_ref, o_ref, *rest):
    sides, (dq_ref, state, sems) = rest[:lanes], rest[lanes:]
    head = state.shape[1]
    groups, _, rows, _ = sides[0].shape
    group, half, core = place(lanes)
    copies = []
    for other, side in enumerate(sides):
        for hop in range(groups):
            there = source(group, hop, groups)
            owner = there * lanes + core(there, 1 - half if other else half)
            dst = pl.ds(pl.multiple_of(owner * rows, rows), rows)
            if rows % 16 == 0:
                state[:, dst, :] = side[hop]
            else:
                copies.append(
                    pltpu.make_async_copy(side.at[hop], state.at[:, dst, :], sems.at[other, hop])
                )
    for copy in copies:
        copy.start()
    for copy in copies:
        copy.wait()
    for h in range(state.shape[0]):
        cols = pl.ds(h * head, head)
        full = lax.dot_general(
            o_ref[:, cols], state[h], CONTRACT_COLS, preferred_element_type=jnp.float32
        )
        dq_ref[:, cols] = jnp.where(q_ref[:, cols] > 0, full, 0.0).astype(dq_ref.dtype)


def query_grads(queries, grad_out, sides):
    lanes, (groups, heads, _, head) = len(sides), sides[0].shape
    return pl.pallas_call(
        functools.partial(query_kernel, lanes),
        out_shape=jax.ShapeDtypeStruct(queries.shape, queries.dtype),
        in_specs=[IN_VMEM] * (2 + lanes),
        out_specs=IN_VMEM,
        scratch_shapes=[
            pltpu.VMEM((heads, head, head), sides[0].dtype),
            pltpu.SemaphoreType.DMA((lanes, groups)),
        ],
        compiler_params=pltpu.CompilerParams(vmem_limit_bytes=VMEM_BYTES),
        cost_estimate=cost(2 * queries.size * head, queries, queries, grad_out, *sides),
        name="query_grads",
    )(queries, grad_out, *sides)


def key_value_kernel(lanes, other, steps, k_ref, v_ref, state_ref, *rest):
    dk_hbm, dv_hbm, state, dk_buf, dv_buf, sems = rest[-6:]
    span, head = state.shape
    groups, rows, _ = state_ref.shape
    group, half, _ = place(lanes)
    for hop in range(groups):
        owner = source(group, hop, groups)
        state[pl.ds(pl.multiple_of(owner * rows, rows), rows), :] = state_ref[hop]
    base = (1 - half if other else half) * span
    part = span // steps
    copies = []
    for step in range(steps):
        for h in range(part // head):
            local = pl.ds(step * part + h * head, head)
            cols = pl.ds(pl.multiple_of(base + step * part + h * head, head), head)
            keys = k_ref[:, cols]
            grad_state = state[local, :]
            full = lax.dot_general(
                v_ref[:, cols], grad_state, CONTRACT_COLS, preferred_element_type=jnp.float32
            )
            dk_buf[:, local] = jnp.where(keys > 0, full, 0.0).astype(dk_buf.dtype)
            dv_buf[:, local] = jnp.dot(
                jnp.maximum(keys, 0), grad_state, preferred_element_type=jnp.float32
            ).astype(dv_buf.dtype)
        src = pl.ds(step * part, part)
        dst = pl.ds(pl.multiple_of(base + step * part, head), part)
        for kind, (buf, hbm) in enumerate(((dk_buf, dk_hbm), (dv_buf, dv_hbm))):
            copy = pltpu.make_async_copy(buf.at[:, src], hbm.at[:, dst], sems.at[kind, step])
            copy.start()
            copies.append(copy)
    for copy in copies:
        copy.wait()


def key_value_grads(keys, values, state, other, before, lanes):
    tokens, (groups, rows, head) = keys.shape[0], state.shape
    span = groups * rows
    steps = 2 if (span // head) % 2 == 0 else 1
    return pl.pallas_call(
        functools.partial(key_value_kernel, lanes, other, steps),
        out_shape=(
            jax.ShapeDtypeStruct(keys.shape, keys.dtype),
            jax.ShapeDtypeStruct(values.shape, values.dtype),
        ),
        in_specs=[IN_VMEM] * 3 + [ANYWHERE] * len(before),
        out_specs=(ANYWHERE, ANYWHERE),
        scratch_shapes=[
            pltpu.VMEM((span, head), state.dtype),
            pltpu.VMEM((tokens, span), keys.dtype),
            pltpu.VMEM((tokens, span), values.dtype),
            pltpu.SemaphoreType.DMA((2, steps)),
        ],
        input_output_aliases={3 + at: at for at in range(len(before))},
        compiler_params=pltpu.CompilerParams(vmem_limit_bytes=VMEM_BYTES),
        cost_estimate=cost(4 * tokens * span * head, state, state),
        name="key_value_other" if other else "key_value_own",
    )(keys, values, state, *before)


def suffix_sum(share, lanes, blocks):
    block = lax.axis_index("tm")
    suffix = total = first = share
    if power_of_two(blocks):
        hop = 1
        while hop < blocks:
            met = permute(
                total.astype(jnp.bfloat16), lanes, lambda b, g, half: (b ^ hop, g, half)
            ).astype(jnp.float32)
            suffix = suffix + jnp.where(block & hop == 0, met, 0.0)
            total = total + met
            first = total if hop == 1 else first
            hop *= 2
    else:
        for hop in range(1, blocks):
            later = permute(
                share.astype(jnp.bfloat16),
                lanes,
                lambda b, g, half: (b - hop, g, half) if b >= hop else None,
            )
            suffix = suffix + later.astype(jnp.float32)
    return suffix.astype(jnp.bfloat16), first


def per_device(queries, keys, values, grad_out, saved_state):
    heads, _, head = saved_state.shape[1:]
    blocks, devices = lax.axis_size("tm"), lax.axis_size("space")
    lanes = 2 if devices % 2 == 0 and heads % 2 == 0 else 1
    groups = devices // lanes
    far_first = range(groups - 1, 0, -1)
    scale = 1.0 / math.sqrt(queries.shape[0] * blocks * devices * head)

    part, (share, *sends) = partial_products(queries, grad_out, head, lanes, groups, scale)
    for hop in far_first:
        share = share + hop_groups(sends[hop - 1], hop, lanes, groups).astype(jnp.float32)
    own, first = suffix_sum(share, lanes, blocks)
    met = [hop_groups(own, hop, lanes, groups) for hop in far_first]

    saved = gather_groups(saved_state, [part, share], lanes, groups)
    sides = [saved]
    if lanes > 1:
        sides.append(swap_halves(after(saved, first), lanes))
    grad_q = query_grads(queries, grad_out, sides)

    near = jnp.stack(after([own, *met[::-1]], grad_q))
    grads = key_value_grads(keys, values, near, False, (), lanes)
    if lanes > 1:
        far = swap_halves(near, lanes)
        grads = key_value_grads(keys, values, far, True, grads, lanes)
    return grad_q, *grads


def solution(mesh):
    tokens = P(("tm", "space"), None)
    return jax.shard_map(
        per_device,
        mesh=mesh,
        in_specs=(tokens, tokens, tokens, tokens, P("tm", None, "space", None)),
        out_specs=(tokens, tokens, tokens),
        check_vma=False,
    )
```

```python
import functools
import math

import jax
import jax.numpy as jnp
from jax import lax
from jax.experimental import pallas as pl
from jax.experimental.pallas import tpu as pltpu
from jax.sharding import PartitionSpec as P

CONTRACT_ROWS = (((0,), (0,)), ((), ()))
CONTRACT_COLS = (((1,), (1,)), ((), ()))
VMEM_BYTES = 16 * 1024 * 1024
ANYWHERE = pl.BlockSpec(memory_space=pl.ANY)
IN_VMEM = pl.BlockSpec(memory_space=pltpu.VMEM)


def power_of_two(count):
    return count & (count - 1) == 0


def partner(group, hop, groups):
    if power_of_two(groups):
        return group ^ hop
    return (group + hop) % groups


def source(group, hop, groups):
    if power_of_two(groups):
        return group ^ hop
    return (group - hop + groups) % groups


def cost(flops, *arrays):
    moved = sum(array.size * array.dtype.itemsize for array in arrays)
    return pl.CostEstimate(flops=flops, bytes_accessed=moved, transcendentals=0)


def after(value, earlier):
    return lax.optimization_barrier((value, earlier))[0]


def place_on_space(lanes):
    index = lax.axis_index("space")
    return lax.div(index, lanes), lax.rem(index, lanes)


def swap_lanes(value, lanes, groups):
    pairs = [(g * lanes + c, g * lanes + 1 - c) for g in range(groups) for c in range(lanes)]
    return lax.ppermute(value, "space", pairs)


def hop_groups(value, hop, lanes, groups):
    pairs = [
        (g * lanes + c, partner(g, hop, groups) * lanes + c)
        for g in range(groups)
        for c in range(lanes)
    ]
    return lax.ppermute(value, "space", pairs)


def gather_groups(value, waits, lanes, groups):
    if power_of_two(groups):
        for step in range(groups.bit_length() - 1):
            value = after(value, waits[min(step, len(waits) - 1)])
            value = jnp.concatenate([value, hop_groups(value, 1 << step, lanes, groups)])
        return value
    return jnp.concatenate(
        [value] + [hop_groups(value, hop, lanes, groups) for hop in range(1, groups)]
    )


def products(scale, queries, grad_out):
    return scale * lax.dot_general(
        jnp.maximum(queries, 0),
        grad_out,
        CONTRACT_ROWS,
        preferred_element_type=jnp.float32,
    )


def partial_kernel(lanes, other, scale, q_ref, o_ref, part_ref):
    span, head = part_ref.shape
    _, lane = place_on_space(lanes)
    base = (1 - lane if other else lane) * span
    for h in range(span // head):
        rows = pl.ds(h * head, head)
        cols = pl.ds(pl.multiple_of(base + h * head, head), head)
        part_ref[rows, :] = products(
            scale, q_ref[:, rows if other else cols], o_ref[:, cols]
        ).astype(part_ref.dtype)


def partial_products(queries, grad_out, head, lanes, other, scale):
    tokens, width = grad_out.shape
    span = width // lanes
    return pl.pallas_call(
        functools.partial(partial_kernel, lanes, other, scale),
        out_shape=jax.ShapeDtypeStruct((span, head), jnp.bfloat16 if other else jnp.float32),
        in_specs=[IN_VMEM, IN_VMEM],
        out_specs=IN_VMEM,
        compiler_params=pltpu.CompilerParams(vmem_limit_bytes=VMEM_BYTES),
        cost_estimate=cost(2 * tokens * span * head, queries),
        name="partial_other" if other else "partial_own",
    )(queries, grad_out)


def cut_kernel(lanes, groups, *refs):
    parts, outs = refs[:lanes], refs[lanes:]
    group, _ = place_on_space(lanes)
    rows = outs[0].shape[0]
    for hop, out_ref in enumerate(outs):
        there = pl.ds(pl.multiple_of(partner(group, hop, groups) * rows, rows), rows)
        total = parts[0][there, :]
        for part in parts[1:]:
            total = total + part[there, :].astype(jnp.float32)
        out_ref[...] = total.astype(out_ref.dtype)


def cut_by_group(parts, lanes, groups):
    span, head = parts[0].shape
    rows = span // groups
    outs = [jax.ShapeDtypeStruct((rows, head), jnp.float32)]
    outs += [jax.ShapeDtypeStruct((rows, head), jnp.bfloat16)] * (groups - 1)
    return pl.pallas_call(
        functools.partial(cut_kernel, lanes, groups),
        out_shape=outs,
        in_specs=[IN_VMEM] * lanes,
        out_specs=[IN_VMEM] * groups,
        compiler_params=pltpu.CompilerParams(vmem_limit_bytes=VMEM_BYTES),
        cost_estimate=cost(span * head, *parts),
        name="cut_by_group",
    )(*parts)


def query_kernel(lanes, q_ref, o_ref, *rest):
    sides, (dq_ref, state, sems) = rest[:lanes], rest[lanes:]
    head = state.shape[1]
    groups, _, rows, _ = sides[0].shape
    group, lane = place_on_space(lanes)
    copies = []
    for other, side in enumerate(sides):
        there = 1 - lane if other else lane
        for hop in range(groups):
            owner = source(group, hop, groups) * lanes + there
            place = pl.ds(pl.multiple_of(owner * rows, rows), rows)
            if rows % 16 == 0:
                state[:, place, :] = side[hop]
            else:
                copies.append(
                    pltpu.make_async_copy(side.at[hop], state.at[:, place, :], sems.at[other, hop])
                )
    for copy in copies:
        copy.start()
    for copy in copies:
        copy.wait()
    for h in range(state.shape[0]):
        cols = pl.ds(h * head, head)
        full = lax.dot_general(
            o_ref[:, cols], state[h], CONTRACT_COLS, preferred_element_type=jnp.float32
        )
        dq_ref[:, cols] = jnp.where(q_ref[:, cols] > 0, full, 0.0).astype(dq_ref.dtype)


def query_grads(queries, grad_out, sides):
    lanes, (groups, heads, _, head) = len(sides), sides[0].shape
    return pl.pallas_call(
        functools.partial(query_kernel, lanes),
        out_shape=jax.ShapeDtypeStruct(queries.shape, queries.dtype),
        in_specs=[IN_VMEM] * (2 + lanes),
        out_specs=IN_VMEM,
        scratch_shapes=[
            pltpu.VMEM((heads, head, head), sides[0].dtype),
            pltpu.SemaphoreType.DMA((lanes, groups)),
        ],
        compiler_params=pltpu.CompilerParams(vmem_limit_bytes=VMEM_BYTES),
        cost_estimate=cost(2 * queries.size * head, queries, queries, grad_out, *sides),
        name="query_grads",
    )(queries, grad_out, *sides)


def key_value_kernel(lanes, other, steps, k_ref, v_ref, state_ref, *rest):
    dk_hbm, dv_hbm, state, dk_buf, dv_buf, sems = rest[-6:]
    span, head = state.shape
    groups, rows, _ = state_ref.shape
    group, lane = place_on_space(lanes)
    for hop in range(groups):
        owner = source(group, hop, groups)
        state[pl.ds(pl.multiple_of(owner * rows, rows), rows), :] = state_ref[hop]
    base = (1 - lane if other else lane) * span
    part = span // steps
    copies = []
    for step in range(steps):
        for h in range(part // head):
            local = pl.ds(step * part + h * head, head)
            cols = pl.ds(pl.multiple_of(base + step * part + h * head, head), head)
            keys = k_ref[:, cols]
            grad_state = state[local, :]
            full = lax.dot_general(
                v_ref[:, cols], grad_state, CONTRACT_COLS, preferred_element_type=jnp.float32
            )
            dk_buf[:, local] = jnp.where(keys > 0, full, 0.0).astype(dk_buf.dtype)
            dv_buf[:, local] = jnp.dot(
                jnp.maximum(keys, 0), grad_state, preferred_element_type=jnp.float32
            ).astype(dv_buf.dtype)
        src = pl.ds(step * part, part)
        dst = pl.ds(pl.multiple_of(base + step * part, head), part)
        for kind, (buf, hbm) in enumerate(((dk_buf, dk_hbm), (dv_buf, dv_hbm))):
            copy = pltpu.make_async_copy(buf.at[:, src], hbm.at[:, dst], sems.at[kind, step])
            copy.start()
            copies.append(copy)
    for copy in copies:
        copy.wait()


def key_value_grads(keys, values, state, other, before, lanes):
    tokens, (groups, rows, head) = keys.shape[0], state.shape
    span = groups * rows
    steps = math.gcd(span // head, 5)
    return pl.pallas_call(
        functools.partial(key_value_kernel, lanes, other, steps),
        out_shape=(
            jax.ShapeDtypeStruct(keys.shape, keys.dtype),
            jax.ShapeDtypeStruct(values.shape, values.dtype),
        ),
        in_specs=[IN_VMEM] * 3 + [ANYWHERE] * len(before),
        out_specs=(ANYWHERE, ANYWHERE),
        scratch_shapes=[
            pltpu.VMEM((span, head), state.dtype),
            pltpu.VMEM((tokens, span), keys.dtype),
            pltpu.VMEM((tokens, span), values.dtype),
            pltpu.SemaphoreType.DMA((2, steps)),
        ],
        input_output_aliases={3 + at: at for at in range(len(before))},
        compiler_params=pltpu.CompilerParams(vmem_limit_bytes=VMEM_BYTES),
        cost_estimate=cost(4 * tokens * span * head, state, state),
        name="key_value_other" if other else "key_value_own",
    )(keys, values, state, *before)


def suffix_sum(share, blocks):
    block = lax.axis_index("tm")
    suffix = total = first = share
    if power_of_two(blocks):
        hop = 1
        while hop < blocks:
            pairs = [(b, b ^ hop) for b in range(blocks)]
            met = lax.ppermute(total.astype(jnp.bfloat16), "tm", pairs).astype(jnp.float32)
            suffix = suffix + jnp.where(block & hop == 0, met, 0.0)
            total = total + met
            first = total if hop == 1 else first
            hop *= 2
    else:
        for hop in range(1, blocks):
            pairs = [(b, b - hop) for b in range(hop, blocks)]
            later = lax.ppermute(share.astype(jnp.bfloat16), "tm", pairs)
            suffix = suffix + later.astype(jnp.float32)
    return suffix.astype(jnp.bfloat16), first


def per_device(queries, keys, values, grad_out, saved_state):
    heads, _, head = saved_state.shape[1:]
    blocks, devices = lax.axis_size("tm"), lax.axis_size("space")
    lanes = 2 if devices % 2 == 0 and heads % 2 == 0 else 1
    groups = devices // lanes
    far_first = range(groups - 1, 0, -1)
    scale = 1.0 / math.sqrt(queries.shape[0] * blocks * devices * head)

    parts = []
    if lanes > 1:
        _, lane = place_on_space(lanes)
        span = queries.shape[1] // lanes
        starts = (jnp.zeros_like(lane), (1 - lane) * span)
        cut = lax.dynamic_slice(
            queries, starts, (queries.shape[0], span), allow_negative_indices=False
        )
        theirs = partial_products(cut, grad_out, head, lanes, True, scale)
        parts.append(swap_lanes(theirs, lanes, groups))
        queries = after(queries, cut)
    parts.insert(0, partial_products(queries, grad_out, head, lanes, False, scale))
    share, *sends = cut_by_group(parts, lanes, groups)
    for hop in far_first:
        share = share + hop_groups(sends[hop - 1], hop, lanes, groups).astype(jnp.float32)
    own, first = suffix_sum(share, blocks)
    met = [hop_groups(own, hop, lanes, groups) for hop in far_first]

    saved = gather_groups(saved_state, [(), share], lanes, groups)
    sides = [saved]
    if lanes > 1:
        sides.append(swap_lanes(after(saved, first), lanes, groups))
    grad_q = query_grads(queries, grad_out, sides)

    near = jnp.stack(after([own, *met[::-1]], grad_q))
    grads = key_value_grads(keys, values, near, False, (), lanes)
    if lanes > 1:
        far = swap_lanes(near, lanes, groups)
        grads = key_value_grads(keys, values, far, True, grads, lanes)
    return grad_q, *grads


def solution(mesh):
    tokens = P(("tm", "space"), None)
    return jax.shard_map(
        per_device,
        mesh=mesh,
        in_specs=(tokens, tokens, tokens, tokens, P("tm", None, "space", None)),
        out_specs=(tokens, tokens, tokens),
        check_vma=False,
    )
```

```python
import functools
import math

import jax
import jax.numpy as jnp
from jax import lax
from jax.experimental import pallas as pl
from jax.experimental.pallas import tpu as pltpu
from jax.sharding import PartitionSpec as P

CONTRACT_ROWS = (((0,), (0,)), ((), ()))
CONTRACT_COLS = (((1,), (1,)), ((), ()))
VMEM_BYTES = 16 * 1024 * 1024
ANYWHERE = pl.BlockSpec(memory_space=pl.ANY)
IN_VMEM = pl.BlockSpec(memory_space=pltpu.VMEM)


def power_of_two(count):
    return count & (count - 1) == 0


def partner(group, hop, groups):
    if power_of_two(groups):
        return group ^ hop
    return (group + hop) % groups


def source(group, hop, groups):
    if power_of_two(groups):
        return group ^ hop
    return (group - hop + groups) % groups


def cost(flops, *arrays):
    moved = sum(array.size * array.dtype.itemsize for array in arrays)
    return pl.CostEstimate(flops=flops, bytes_accessed=moved, transcendentals=0)


def after(value, earlier):
    return lax.optimization_barrier((value, earlier))[0]


def place_on_space(lanes):
    index = lax.axis_index("space")
    return lax.div(index, lanes), lax.rem(index, lanes)


def swap_lanes(value, lanes, groups):
    pairs = [(g * lanes + c, g * lanes + 1 - c) for g in range(groups) for c in range(lanes)]
    return lax.ppermute(value, "space", pairs)


def hop_groups(value, hop, lanes, groups):
    pairs = [
        (g * lanes + c, partner(g, hop, groups) * lanes + c)
        for g in range(groups)
        for c in range(lanes)
    ]
    return lax.ppermute(value, "space", pairs)


def products(scale, queries, grad_out):
    return scale * lax.dot_general(
        jnp.maximum(queries, 0),
        grad_out,
        CONTRACT_ROWS,
        preferred_element_type=jnp.float32,
    )


def partial_kernel(lanes, other, scale, q_ref, o_ref, part_ref):
    span, head = part_ref.shape
    _, lane = place_on_space(lanes)
    base = (1 - lane if other else lane) * span
    for h in range(span // head):
        rows = pl.ds(h * head, head)
        cols = pl.ds(pl.multiple_of(base + h * head, head), head)
        part_ref[rows, :] = products(
            scale, q_ref[:, rows if other else cols], o_ref[:, cols]
        ).astype(part_ref.dtype)


def partial_products(queries, grad_out, head, lanes, other, scale):
    tokens, width = grad_out.shape
    span = width // lanes
    return pl.pallas_call(
        functools.partial(partial_kernel, lanes, other, scale),
        out_shape=jax.ShapeDtypeStruct((span, head), jnp.bfloat16 if other else jnp.float32),
        in_specs=[IN_VMEM, IN_VMEM],
        out_specs=IN_VMEM,
        compiler_params=pltpu.CompilerParams(vmem_limit_bytes=VMEM_BYTES),
        cost_estimate=cost(2 * tokens * span * head, queries),
        name="partial_other" if other else "partial_own",
    )(queries, grad_out)


def cut_kernel(lanes, groups, *refs):
    parts, outs = refs[:lanes], refs[lanes:]
    group, _ = place_on_space(lanes)
    rows = outs[0].shape[0]
    for hop, out_ref in enumerate(outs):
        there = pl.ds(pl.multiple_of(partner(group, hop, groups) * rows, rows), rows)
        total = parts[0][there, :]
        for part in parts[1:]:
            total = total + part[there, :].astype(jnp.float32)
        out_ref[...] = total.astype(out_ref.dtype)


def cut_by_group(parts, lanes, groups):
    span, head = parts[0].shape
    rows = span // groups
    outs = [jax.ShapeDtypeStruct((rows, head), jnp.float32)]
    outs += [jax.ShapeDtypeStruct((rows, head), jnp.bfloat16)] * (groups - 1)
    return pl.pallas_call(
        functools.partial(cut_kernel, lanes, groups),
        out_shape=outs,
        in_specs=[IN_VMEM] * lanes,
        out_specs=[IN_VMEM] * groups,
        compiler_params=pltpu.CompilerParams(vmem_limit_bytes=VMEM_BYTES),
        cost_estimate=cost(span * head, *parts),
        name="cut_by_group",
    )(*parts)


def query_kernel(lanes, groups, q_ref, o_ref, *rest):
    pieces, (dq_ref, state, sems) = rest[:-3], rest[-3:]
    head, rows = state.shape[1], pieces[0].shape[1]
    group, lane = place_on_space(lanes)
    copies = []
    for at, piece in enumerate(pieces):
        there = lane if at < groups else 1 - lane
        owner = source(group, at % groups, groups) * lanes + there
        dst = pl.ds(pl.multiple_of(owner * rows, rows), rows)
        if rows % 16 == 0:
            state[:, dst, :] = piece[...]
        else:
            copies.append(pltpu.make_async_copy(piece, state.at[:, dst, :], sems.at[at]))
    for copy in copies:
        copy.start()
    for copy in copies:
        copy.wait()
    for h in range(state.shape[0]):
        cols = pl.ds(h * head, head)
        full = lax.dot_general(
            o_ref[:, cols], state[h], CONTRACT_COLS, preferred_element_type=jnp.float32
        )
        dq_ref[:, cols] = jnp.where(q_ref[:, cols] > 0, full, 0.0).astype(dq_ref.dtype)


def query_grads(queries, grad_out, pieces, lanes, groups):
    heads, _, head = pieces[0].shape
    return pl.pallas_call(
        functools.partial(query_kernel, lanes, groups),
        out_shape=jax.ShapeDtypeStruct(queries.shape, queries.dtype),
        in_specs=[IN_VMEM] * (2 + len(pieces)),
        out_specs=IN_VMEM,
        scratch_shapes=[
            pltpu.VMEM((heads, head, head), pieces[0].dtype),
            pltpu.SemaphoreType.DMA((len(pieces),)),
        ],
        compiler_params=pltpu.CompilerParams(vmem_limit_bytes=VMEM_BYTES),
        cost_estimate=cost(2 * queries.size * head, queries, queries, grad_out, *pieces),
        name="query_grads",
    )(queries, grad_out, *pieces)


def key_value_kernel(lanes, groups, other, steps, k_ref, v_ref, *rest):
    pieces = rest[:groups]
    dk_hbm, dv_hbm, state, dk_buf, dv_buf, sems = rest[-6:]
    (span, head), rows = state.shape, pieces[0].shape[0]
    group, lane = place_on_space(lanes)
    for hop, piece in enumerate(pieces):
        owner = source(group, hop, groups)
        state[pl.ds(pl.multiple_of(owner * rows, rows), rows), :] = piece[...]
    base = (1 - lane if other else lane) * span
    part = span // steps
    copies = []
    for step in range(steps):
        for h in range(part // head):
            local = pl.ds(step * part + h * head, head)
            cols = pl.ds(pl.multiple_of(base + step * part + h * head, head), head)
            keys = k_ref[:, cols]
            grad_state = state[local, :]
            full = lax.dot_general(
                v_ref[:, cols], grad_state, CONTRACT_COLS, preferred_element_type=jnp.float32
            )
            dk_buf[:, local] = jnp.where(keys > 0, full, 0.0).astype(dk_buf.dtype)
            dv_buf[:, local] = jnp.dot(
                jnp.maximum(keys, 0), grad_state, preferred_element_type=jnp.float32
            ).astype(dv_buf.dtype)
        src = pl.ds(step * part, part)
        dst = pl.ds(pl.multiple_of(base + step * part, head), part)
        for kind, (buf, hbm) in enumerate(((dk_buf, dk_hbm), (dv_buf, dv_hbm))):
            copy = pltpu.make_async_copy(buf.at[:, src], hbm.at[:, dst], sems.at[kind, step])
            copy.start()
            copies.append(copy)
    for copy in copies:
        copy.wait()


def key_value_grads(keys, values, pieces, other, before, lanes):
    tokens, groups, (rows, head) = keys.shape[0], len(pieces), pieces[0].shape
    span = groups * rows
    steps = math.gcd(span // head, 5)
    return pl.pallas_call(
        functools.partial(key_value_kernel, lanes, groups, other, steps),
        out_shape=(
            jax.ShapeDtypeStruct(keys.shape, keys.dtype),
            jax.ShapeDtypeStruct(values.shape, values.dtype),
        ),
        in_specs=[IN_VMEM] * (2 + groups) + [ANYWHERE] * len(before),
        out_specs=(ANYWHERE, ANYWHERE),
        scratch_shapes=[
            pltpu.VMEM((span, head), pieces[0].dtype),
            pltpu.VMEM((tokens, span), keys.dtype),
            pltpu.VMEM((tokens, span), values.dtype),
            pltpu.SemaphoreType.DMA((2, steps)),
        ],
        input_output_aliases={2 + groups + at: at for at in range(len(before))},
        compiler_params=pltpu.CompilerParams(vmem_limit_bytes=VMEM_BYTES),
        cost_estimate=cost(4 * tokens * span * head, *pieces),
        name="key_value_other" if other else "key_value_own",
    )(keys, values, *pieces, *before)


def suffix_sum(share, blocks):
    block = lax.axis_index("tm")
    suffix = total = first = share
    if power_of_two(blocks):
        hop = 1
        while hop < blocks:
            pairs = [(b, b ^ hop) for b in range(blocks)]
            met = lax.ppermute(total.astype(jnp.bfloat16), "tm", pairs).astype(jnp.float32)
            suffix = suffix + jnp.where(block & hop == 0, met, 0.0)
            total = total + met
            first = total if hop == 1 else first
            hop *= 2
    else:
        for hop in range(1, blocks):
            pairs = [(b, b - hop) for b in range(hop, blocks)]
            later = lax.ppermute(share.astype(jnp.bfloat16), "tm", pairs)
            suffix = suffix + later.astype(jnp.float32)
    return suffix.astype(jnp.bfloat16), first


def per_device(queries, keys, values, grad_out, saved_state):
    heads, _, head = saved_state.shape[1:]
    blocks, devices = lax.axis_size("tm"), lax.axis_size("space")
    lanes = 2 if devices % 2 == 0 and heads % 2 == 0 else 1
    groups = devices // lanes
    far_first = range(groups - 1, 0, -1)
    scale = 1.0 / math.sqrt(queries.shape[0] * blocks * devices * head)

    parts = []
    if lanes > 1:
        _, lane = place_on_space(lanes)
        span = queries.shape[1] // lanes
        starts = (jnp.zeros_like(lane), (1 - lane) * span)
        cut = lax.dynamic_slice(
            queries, starts, (queries.shape[0], span), allow_negative_indices=False
        )
        theirs = partial_products(cut, grad_out, head, lanes, True, scale)
        parts.append(swap_lanes(theirs, lanes, groups))
        queries = after(queries, cut)
    parts.insert(0, partial_products(queries, grad_out, head, lanes, False, scale))
    share, *sends = cut_by_group(parts, lanes, groups)
    for hop in far_first:
        share = share + hop_groups(sends[hop - 1], hop, lanes, groups).astype(jnp.float32)
    own, first = suffix_sum(share, blocks)
    met = [hop_groups(own, hop, lanes, groups) for hop in far_first]

    def gather(value):
        near = [value] + [hop_groups(value, hop, lanes, groups) for hop in range(1, groups)]
        return near + [swap_lanes(piece, lanes, groups) for piece in near if lanes > 1]

    grad_q = query_grads(queries, grad_out, gather(saved_state[0]), lanes, groups)

    near = [after(piece, grad_q) for piece in (own, *met[::-1])]
    grads = key_value_grads(keys, values, near, False, (), lanes)
    if lanes > 1:
        far = [swap_lanes(piece, lanes, groups) for piece in near]
        grads = key_value_grads(keys, values, far, True, grads, lanes)
    return grad_q, *grads


def solution(mesh):
    tokens = P(("tm", "space"), None)
    return jax.shard_map(
        per_device,
        mesh=mesh,
        in_specs=(tokens, tokens, tokens, tokens, P("tm", None, "space", None)),
        out_specs=(tokens, tokens, tokens),
        check_vma=False,
    )
```

```python
import functools
import math

import jax
import jax.numpy as jnp
from jax import lax
from jax.experimental import pallas as pl
from jax.experimental.pallas import tpu as pltpu
from jax.sharding import PartitionSpec as P

CONTRACT_ROWS = (((0,), (0,)), ((), ()))
CONTRACT_COLS = (((1,), (1,)), ((), ()))
VMEM_BYTES = 16 * 1024 * 1024
ANYWHERE = pl.BlockSpec(memory_space=pl.ANY)
IN_VMEM = pl.BlockSpec(memory_space=pltpu.VMEM)


def power_of_two(count):
    return count & (count - 1) == 0


def partner(group, hop, groups):
    if power_of_two(groups):
        return group ^ hop
    return (group + hop) % groups


def source(group, hop, groups):
    if power_of_two(groups):
        return group ^ hop
    return (group - hop + groups) % groups


def cost(flops, *arrays):
    moved = sum(array.size * array.dtype.itemsize for array in arrays)
    return pl.CostEstimate(flops=flops, bytes_accessed=moved, transcendentals=0)


def after(value, earlier):
    return lax.optimization_barrier((value, earlier))[0]


def place_on_space(lanes):
    index = lax.axis_index("space")
    return lax.div(index, lanes), lax.rem(index, lanes)


def swap_lanes(value, lanes, groups):
    pairs = [(g * lanes + c, g * lanes + 1 - c) for g in range(groups) for c in range(lanes)]
    return lax.ppermute(value, "space", pairs)


def hop_groups(value, hop, lanes, groups):
    pairs = [
        (g * lanes + c, partner(g, hop, groups) * lanes + c)
        for g in range(groups)
        for c in range(lanes)
    ]
    return lax.ppermute(value, "space", pairs)


def gather_groups(value, waits, lanes, groups):
    if power_of_two(groups):
        for step in range(groups.bit_length() - 1):
            start, done = waits[min(step, len(waits) - 1)]
            met = hop_groups(after(value, start), 1 << step, lanes, groups)
            value = jnp.concatenate([value, after(met, done)])
        return value
    return jnp.concatenate(
        [value] + [hop_groups(value, hop, lanes, groups) for hop in range(1, groups)]
    )


def products(scale, queries, grad_out):
    return scale * lax.dot_general(
        jnp.maximum(queries, 0),
        grad_out,
        CONTRACT_ROWS,
        preferred_element_type=jnp.float32,
    )


def partial_kernel(lanes, other, scale, q_ref, o_ref, part_ref):
    span, head = part_ref.shape
    _, lane = place_on_space(lanes)
    base = (1 - lane if other else lane) * span
    for h in range(span // head):
        rows = pl.ds(h * head, head)
        cols = pl.ds(pl.multiple_of(base + h * head, head), head)
        part_ref[rows, :] = products(
            scale, q_ref[:, rows if other else cols], o_ref[:, cols]
        ).astype(part_ref.dtype)


def partial_products(queries, grad_out, head, lanes, other, scale):
    tokens, width = grad_out.shape
    span = width // lanes
    return pl.pallas_call(
        functools.partial(partial_kernel, lanes, other, scale),
        out_shape=jax.ShapeDtypeStruct((span, head), jnp.bfloat16 if other else jnp.float32),
        in_specs=[IN_VMEM, IN_VMEM],
        out_specs=IN_VMEM,
        compiler_params=pltpu.CompilerParams(vmem_limit_bytes=VMEM_BYTES),
        cost_estimate=cost(2 * tokens * span * head, queries),
        name="partial_other" if other else "partial_own",
    )(queries, grad_out)


def cut_kernel(lanes, groups, *refs):
    parts, outs = refs[:lanes], refs[lanes:]
    group, _ = place_on_space(lanes)
    rows = outs[0].shape[0]
    for hop, out_ref in enumerate(outs):
        there = pl.ds(pl.multiple_of(partner(group, hop, groups) * rows, rows), rows)
        total = parts[0][there, :]
        for part in parts[1:]:
            total = total + part[there, :].astype(jnp.float32)
        out_ref[...] = total.astype(out_ref.dtype)


def cut_by_group(parts, lanes, groups):
    span, head = parts[0].shape
    rows = span // groups
    outs = [jax.ShapeDtypeStruct((rows, head), jnp.float32)]
    outs += [jax.ShapeDtypeStruct((rows, head), jnp.bfloat16)] * (groups - 1)
    return pl.pallas_call(
        functools.partial(cut_kernel, lanes, groups),
        out_shape=outs,
        in_specs=[IN_VMEM] * lanes,
        out_specs=[IN_VMEM] * groups,
        compiler_params=pltpu.CompilerParams(vmem_limit_bytes=VMEM_BYTES),
        cost_estimate=cost(span * head, *parts),
        name="cut_by_group",
    )(*parts)


def query_kernel(lanes, q_ref, o_ref, *rest):
    sides, (dq_ref, state, sems) = rest[:lanes], rest[lanes:]
    head = state.shape[1]
    groups, _, rows, _ = sides[0].shape
    group, lane = place_on_space(lanes)
    copies = []
    for other, side in enumerate(sides):
        there = 1 - lane if other else lane
        for hop in range(groups):
            owner = source(group, hop, groups) * lanes + there
            place = pl.ds(pl.multiple_of(owner * rows, rows), rows)
            if rows % 16 == 0:
                state[:, place, :] = side[hop]
            else:
                copies.append(
                    pltpu.make_async_copy(side.at[hop], state.at[:, place, :], sems.at[other, hop])
                )
    for copy in copies:
        copy.start()
    for copy in copies:
        copy.wait()
    for h in range(state.shape[0]):
        cols = pl.ds(h * head, head)
        full = lax.dot_general(
            o_ref[:, cols], state[h], CONTRACT_COLS, preferred_element_type=jnp.float32
        )
        dq_ref[:, cols] = jnp.where(q_ref[:, cols] > 0, full, 0.0).astype(dq_ref.dtype)


def query_grads(queries, grad_out, sides):
    lanes, (groups, heads, _, head) = len(sides), sides[0].shape
    return pl.pallas_call(
        functools.partial(query_kernel, lanes),
        out_shape=jax.ShapeDtypeStruct(queries.shape, queries.dtype),
        in_specs=[IN_VMEM] * (2 + lanes),
        out_specs=IN_VMEM,
        scratch_shapes=[
            pltpu.VMEM((heads, head, head), sides[0].dtype),
            pltpu.SemaphoreType.DMA((lanes, groups)),
        ],
        compiler_params=pltpu.CompilerParams(vmem_limit_bytes=VMEM_BYTES),
        cost_estimate=cost(2 * queries.size * head, queries, queries, grad_out, *sides),
        name="query_grads",
    )(queries, grad_out, *sides)


def key_value_kernel(lanes, other, steps, k_ref, v_ref, state_ref, *rest):
    dk_hbm, dv_hbm, state, dk_buf, dv_buf, sems = rest[-6:]
    span, head = state.shape
    groups, rows, _ = state_ref.shape
    group, lane = place_on_space(lanes)
    for hop in range(groups):
        owner = source(group, hop, groups)
        state[pl.ds(pl.multiple_of(owner * rows, rows), rows), :] = state_ref[hop]
    base = (1 - lane if other else lane) * span
    part = span // steps
    copies = []
    for step in range(steps):
        for h in range(part // head):
            local = pl.ds(step * part + h * head, head)
            cols = pl.ds(pl.multiple_of(base + step * part + h * head, head), head)
            keys = k_ref[:, cols]
            grad_state = state[local, :]
            full = lax.dot_general(
                v_ref[:, cols], grad_state, CONTRACT_COLS, preferred_element_type=jnp.float32
            )
            dk_buf[:, local] = jnp.where(keys > 0, full, 0.0).astype(dk_buf.dtype)
            dv_buf[:, local] = jnp.dot(
                jnp.maximum(keys, 0), grad_state, preferred_element_type=jnp.float32
            ).astype(dv_buf.dtype)
        src = pl.ds(step * part, part)
        dst = pl.ds(pl.multiple_of(base + step * part, head), part)
        for kind, (buf, hbm) in enumerate(((dk_buf, dk_hbm), (dv_buf, dv_hbm))):
            copy = pltpu.make_async_copy(buf.at[:, src], hbm.at[:, dst], sems.at[kind, step])
            copy.start()
            copies.append(copy)
    for copy in copies:
        copy.wait()


def key_value_grads(keys, values, state, other, before, lanes):
    tokens, (groups, rows, head) = keys.shape[0], state.shape
    span = groups * rows
    steps = math.gcd(span // head, 5)
    return pl.pallas_call(
        functools.partial(key_value_kernel, lanes, other, steps),
        out_shape=(
            jax.ShapeDtypeStruct(keys.shape, keys.dtype),
            jax.ShapeDtypeStruct(values.shape, values.dtype),
        ),
        in_specs=[IN_VMEM] * 3 + [ANYWHERE] * len(before),
        out_specs=(ANYWHERE, ANYWHERE),
        scratch_shapes=[
            pltpu.VMEM((span, head), state.dtype),
            pltpu.VMEM((tokens, span), keys.dtype),
            pltpu.VMEM((tokens, span), values.dtype),
            pltpu.SemaphoreType.DMA((2, steps)),
        ],
        input_output_aliases={3 + at: at for at in range(len(before))},
        compiler_params=pltpu.CompilerParams(vmem_limit_bytes=VMEM_BYTES),
        cost_estimate=cost(4 * tokens * span * head, state, state),
        name="key_value_other" if other else "key_value_own",
    )(keys, values, state, *before)


def suffix_sum(share, blocks):
    block = lax.axis_index("tm")
    suffix = total = first = share
    if power_of_two(blocks):
        hop = 1
        while hop < blocks:
            pairs = [(b, b ^ hop) for b in range(blocks)]
            met = lax.ppermute(total.astype(jnp.bfloat16), "tm", pairs).astype(jnp.float32)
            suffix = suffix + jnp.where(block & hop == 0, met, 0.0)
            total = total + met
            first = total if hop == 1 else first
            hop *= 2
    else:
        for hop in range(1, blocks):
            pairs = [(b, b - hop) for b in range(hop, blocks)]
            later = lax.ppermute(share.astype(jnp.bfloat16), "tm", pairs)
            suffix = suffix + later.astype(jnp.float32)
    return suffix.astype(jnp.bfloat16), first


def per_device(queries, keys, values, grad_out, saved_state):
    heads, _, head = saved_state.shape[1:]
    blocks, devices = lax.axis_size("tm"), lax.axis_size("space")
    lanes = 2 if devices % 2 == 0 and heads % 2 == 0 else 1
    groups = devices // lanes
    far_first = range(groups - 1, 0, -1)
    scale = 1.0 / math.sqrt(queries.shape[0] * blocks * devices * head)

    parts = []
    if lanes > 1:
        _, lane = place_on_space(lanes)
        span = queries.shape[1] // lanes
        starts = (jnp.zeros_like(lane), (1 - lane) * span)
        cut = lax.dynamic_slice(
            queries, starts, (queries.shape[0], span), allow_negative_indices=False
        )
        theirs = partial_products(cut, grad_out, head, lanes, True, scale)
        parts.append(swap_lanes(theirs, lanes, groups))
        queries = after(queries, cut)
    parts.insert(0, partial_products(queries, grad_out, head, lanes, False, scale))
    share, *sends = cut_by_group(parts, lanes, groups)
    for hop in far_first:
        share = share + hop_groups(sends[hop - 1], hop, lanes, groups).astype(jnp.float32)
    own, first = suffix_sum(share, blocks)
    met = [hop_groups(own, hop, lanes, groups) for hop in far_first]

    saved = gather_groups(saved_state, [((), share), (share, ())], lanes, groups)
    sides = [saved]
    if lanes > 1:
        sides.append(swap_lanes(after(saved, first), lanes, groups))
    grad_q = query_grads(queries, grad_out, sides)

    near = jnp.stack(after([own, *met[::-1]], grad_q))
    grads = key_value_grads(keys, values, near, False, (), lanes)
    if lanes > 1:
        far = swap_lanes(near, lanes, groups)
        grads = key_value_grads(keys, values, far, True, grads, lanes)
    return grad_q, *grads


def solution(mesh):
    tokens = P(("tm", "space"), None)
    return jax.shard_map(
        per_device,
        mesh=mesh,
        in_specs=(tokens, tokens, tokens, tokens, P("tm", None, "space", None)),
        out_specs=(tokens, tokens, tokens),
        check_vma=False,
    )
```

```python
import functools
import math

import jax
import jax.numpy as jnp
from jax import lax
from jax.experimental import pallas as pl
from jax.experimental.pallas import tpu as pltpu
from jax.sharding import PartitionSpec as P

CONTRACT_ROWS = (((0,), (0,)), ((), ()))
CONTRACT_COLS = (((1,), (1,)), ((), ()))
VMEM_BYTES = 16 * 1024 * 1024
ANYWHERE = pl.BlockSpec(memory_space=pl.ANY)
IN_VMEM = pl.BlockSpec(memory_space=pltpu.VMEM)


def power_of_two(count):
    return count & (count - 1) == 0


def partner(group, hop, groups):
    if power_of_two(groups):
        return group ^ hop
    return (group + hop) % groups


def source(group, hop, groups):
    if power_of_two(groups):
        return group ^ hop
    return (group - hop + groups) % groups


def cost(flops, *arrays):
    moved = sum(array.size * array.dtype.itemsize for array in arrays)
    return pl.CostEstimate(flops=flops, bytes_accessed=moved, transcendentals=0)


def after(value, earlier):
    return lax.optimization_barrier((value, earlier))[0]


def place_on_space(lanes):
    index = lax.axis_index("space")
    return lax.div(index, lanes), lax.rem(index, lanes)


def swap_lanes(value, lanes, groups):
    pairs = [(g * lanes + c, g * lanes + 1 - c) for g in range(groups) for c in range(lanes)]
    return lax.ppermute(value, "space", pairs)


def hop_groups(value, hop, lanes, groups):
    pairs = [
        (g * lanes + c, partner(g, hop, groups) * lanes + c)
        for g in range(groups)
        for c in range(lanes)
    ]
    return lax.ppermute(value, "space", pairs)


def gather_groups(value, waits, lanes, groups):
    if power_of_two(groups):
        for step in range(groups.bit_length() - 1):
            value = after(value, waits[min(step, len(waits) - 1)])
            value = jnp.concatenate([value, hop_groups(value, 1 << step, lanes, groups)])
        return value
    return jnp.concatenate(
        [value] + [hop_groups(value, hop, lanes, groups) for hop in range(1, groups)]
    )


def products(scale, queries, grad_out):
    return scale * lax.dot_general(
        jnp.maximum(queries, 0),
        grad_out,
        CONTRACT_ROWS,
        preferred_element_type=jnp.float32,
    )


def partial_kernel(lanes, other, scale, q_ref, o_ref, part_ref):
    span, head = part_ref.shape
    _, lane = place_on_space(lanes)
    base = (1 - lane if other else lane) * span
    for h in range(span // head):
        rows = pl.ds(h * head, head)
        cols = pl.ds(pl.multiple_of(base + h * head, head), head)
        part_ref[rows, :] = products(
            scale, q_ref[:, rows if other else cols], o_ref[:, cols]
        ).astype(part_ref.dtype)


def partial_products(queries, grad_out, head, lanes, other, scale):
    tokens, width = grad_out.shape
    span = width // lanes
    return pl.pallas_call(
        functools.partial(partial_kernel, lanes, other, scale),
        out_shape=jax.ShapeDtypeStruct((span, head), jnp.bfloat16 if other else jnp.float32),
        in_specs=[IN_VMEM, IN_VMEM],
        out_specs=IN_VMEM,
        compiler_params=pltpu.CompilerParams(vmem_limit_bytes=VMEM_BYTES),
        cost_estimate=cost(2 * tokens * span * head, queries),
        name="partial_other" if other else "partial_own",
    )(queries, grad_out)


def cut_kernel(lanes, groups, *refs):
    parts, outs = refs[:lanes], refs[lanes:]
    group, _ = place_on_space(lanes)
    rows = outs[0].shape[0]
    for hop, out_ref in enumerate(outs):
        there = pl.ds(pl.multiple_of(partner(group, hop, groups) * rows, rows), rows)
        total = parts[0][there, :]
        for part in parts[1:]:
            total = total + part[there, :].astype(jnp.float32)
        out_ref[...] = total.astype(out_ref.dtype)


def cut_by_group(parts, lanes, groups):
    span, head = parts[0].shape
    rows = span // groups
    outs = [jax.ShapeDtypeStruct((rows, head), jnp.float32)]
    outs += [jax.ShapeDtypeStruct((rows, head), jnp.bfloat16)] * (groups - 1)
    return pl.pallas_call(
        functools.partial(cut_kernel, lanes, groups),
        out_shape=outs,
        in_specs=[IN_VMEM] * lanes,
        out_specs=[IN_VMEM] * groups,
        compiler_params=pltpu.CompilerParams(vmem_limit_bytes=VMEM_BYTES),
        cost_estimate=cost(span * head, *parts),
        name="cut_by_group",
    )(*parts)


def query_kernel(lanes, q_ref, o_ref, *rest):
    sides, (dq_ref, state, sems) = rest[:lanes], rest[lanes:]
    head = state.shape[1]
    groups, _, rows, _ = sides[0].shape
    group, lane = place_on_space(lanes)
    copies = []
    for other, side in enumerate(sides):
        there = 1 - lane if other else lane
        for hop in range(groups):
            owner = source(group, hop, groups) * lanes + there
            place = pl.ds(pl.multiple_of(owner * rows, rows), rows)
            if rows % 16 == 0:
                state[:, place, :] = side[hop]
            else:
                copies.append(
                    pltpu.make_async_copy(side.at[hop], state.at[:, place, :], sems.at[other, hop])
                )
    for copy in copies:
        copy.start()
    for copy in copies:
        copy.wait()
    for h in range(state.shape[0]):
        cols = pl.ds(h * head, head)
        full = lax.dot_general(
            o_ref[:, cols], state[h], CONTRACT_COLS, preferred_element_type=jnp.float32
        )
        dq_ref[:, cols] = jnp.where(q_ref[:, cols] > 0, full, 0.0).astype(dq_ref.dtype)


def query_grads(queries, grad_out, sides):
    lanes, (groups, heads, _, head) = len(sides), sides[0].shape
    return pl.pallas_call(
        functools.partial(query_kernel, lanes),
        out_shape=jax.ShapeDtypeStruct(queries.shape, queries.dtype),
        in_specs=[IN_VMEM] * (2 + lanes),
        out_specs=IN_VMEM,
        scratch_shapes=[
            pltpu.VMEM((heads, head, head), sides[0].dtype),
            pltpu.SemaphoreType.DMA((lanes, groups)),
        ],
        compiler_params=pltpu.CompilerParams(vmem_limit_bytes=VMEM_BYTES),
        cost_estimate=cost(2 * queries.size * head, queries, queries, grad_out, *sides),
        name="query_grads",
    )(queries, grad_out, *sides)


def key_value_kernel(lanes, other, steps, k_ref, v_ref, state_ref, *rest):
    dk_hbm, dv_hbm, state, dk_buf, dv_buf, sems = rest[-6:]
    span, head = state.shape
    groups, rows, _ = state_ref.shape
    group, lane = place_on_space(lanes)
    for hop in range(groups):
        owner = source(group, hop, groups)
        state[pl.ds(pl.multiple_of(owner * rows, rows), rows), :] = state_ref[hop]
    base = (1 - lane if other else lane) * span
    part = span // steps
    copies = []
    for step in range(steps):
        for h in range(part // head):
            local = pl.ds(step * part + h * head, head)
            cols = pl.ds(pl.multiple_of(base + step * part + h * head, head), head)
            keys = k_ref[:, cols]
            grad_state = state[local, :]
            full = lax.dot_general(
                v_ref[:, cols], grad_state, CONTRACT_COLS, preferred_element_type=jnp.float32
            )
            dk_buf[:, local] = jnp.where(keys > 0, full, 0.0).astype(dk_buf.dtype)
            dv_buf[:, local] = jnp.dot(
                jnp.maximum(keys, 0), grad_state, preferred_element_type=jnp.float32
            ).astype(dv_buf.dtype)
        src = pl.ds(step * part, part)
        dst = pl.ds(pl.multiple_of(base + step * part, head), part)
        for kind, (buf, hbm) in enumerate(((dk_buf, dk_hbm), (dv_buf, dv_hbm))):
            copy = pltpu.make_async_copy(buf.at[:, src], hbm.at[:, dst], sems.at[kind, step])
            copy.start()
            copies.append(copy)
    for copy in copies:
        copy.wait()


def key_value_grads(keys, values, state, other, before, lanes):
    tokens, (groups, rows, head) = keys.shape[0], state.shape
    span = groups * rows
    steps = math.gcd(span // head, 5)
    return pl.pallas_call(
        functools.partial(key_value_kernel, lanes, other, steps),
        out_shape=(
            jax.ShapeDtypeStruct(keys.shape, keys.dtype),
            jax.ShapeDtypeStruct(values.shape, values.dtype),
        ),
        in_specs=[IN_VMEM] * 3 + [ANYWHERE] * len(before),
        out_specs=(ANYWHERE, ANYWHERE),
        scratch_shapes=[
            pltpu.VMEM((span, head), state.dtype),
            pltpu.VMEM((tokens, span), keys.dtype),
            pltpu.VMEM((tokens, span), values.dtype),
            pltpu.SemaphoreType.DMA((2, steps)),
        ],
        input_output_aliases={3 + at: at for at in range(len(before))},
        compiler_params=pltpu.CompilerParams(vmem_limit_bytes=VMEM_BYTES),
        cost_estimate=cost(4 * tokens * span * head, state, state),
        name="key_value_other" if other else "key_value_own",
    )(keys, values, state, *before)


def suffix_sum(share, blocks):
    block = lax.axis_index("tm")
    suffix = total = first = share
    if power_of_two(blocks):
        hop = 1
        while hop < blocks:
            pairs = [(b, b ^ hop) for b in range(blocks)]
            met = lax.ppermute(total.astype(jnp.bfloat16), "tm", pairs).astype(jnp.float32)
            suffix = suffix + jnp.where(block & hop == 0, met, 0.0)
            total = total + met
            first = total if hop == 1 else first
            hop *= 2
    else:
        for hop in range(1, blocks):
            pairs = [(b, b - hop) for b in range(hop, blocks)]
            later = lax.ppermute(share.astype(jnp.bfloat16), "tm", pairs)
            suffix = suffix + later.astype(jnp.float32)
    return suffix.astype(jnp.bfloat16), first


def per_device(queries, keys, values, grad_out, saved_state):
    heads, _, head = saved_state.shape[1:]
    blocks, devices = lax.axis_size("tm"), lax.axis_size("space")
    lanes = 2 if devices % 2 == 0 and heads % 2 == 0 else 1
    groups = devices // lanes
    far_first = range(groups - 1, 0, -1)
    scale = 1.0 / math.sqrt(queries.shape[0] * blocks * devices * head)

    parts = []
    if lanes > 1:
        _, lane = place_on_space(lanes)
        span = queries.shape[1] // lanes
        starts = (jnp.zeros_like(lane), (1 - lane) * span)
        cut = lax.dynamic_slice(
            queries, starts, (queries.shape[0], span), allow_negative_indices=False
        )
        theirs = partial_products(cut, grad_out, head, lanes, True, scale)
        parts.append(swap_lanes(theirs, lanes, groups))
        queries = after(queries, cut)
    parts.insert(0, partial_products(queries, grad_out, head, lanes, False, scale))
    share, *sends = cut_by_group(parts, lanes, groups)
    for hop in far_first:
        share = share + hop_groups(sends[hop - 1], hop, lanes, groups).astype(jnp.float32)
    own, first = suffix_sum(share, blocks)
    met = [hop_groups(own, hop, lanes, groups) for hop in far_first]

    saved = gather_groups(saved_state, [parts[0], share], lanes, groups)
    sides = [saved]
    if lanes > 1:
        sides.append(swap_lanes(after(saved, first), lanes, groups))
    grad_q = query_grads(queries, grad_out, sides)

    near = jnp.stack(after([own, *met[::-1]], grad_q))
    grads = key_value_grads(keys, values, near, False, (), lanes)
    if lanes > 1:
        far = swap_lanes(near, lanes, groups)
        grads = key_value_grads(keys, values, far, True, grads, lanes)
    return grad_q, *grads


def solution(mesh):
    tokens = P(("tm", "space"), None)
    return jax.shard_map(
        per_device,
        mesh=mesh,
        in_specs=(tokens, tokens, tokens, tokens, P("tm", None, "space", None)),
        out_specs=(tokens, tokens, tokens),
        check_vma=False,
    )
```

```python
import functools
import math

import jax
import jax.numpy as jnp
from jax import lax
from jax.experimental import pallas as pl
from jax.experimental.pallas import tpu as pltpu
from jax.sharding import PartitionSpec as P

CONTRACT_ROWS = (((0,), (0,)), ((), ()))
CONTRACT_COLS = (((1,), (1,)), ((), ()))
VMEM_BYTES = 16 * 1024 * 1024
ANYWHERE = pl.BlockSpec(memory_space=pl.ANY)
IN_VMEM = pl.BlockSpec(memory_space=pltpu.VMEM)


def power_of_two(count):
    return count & (count - 1) == 0


def partner(group, hop, groups):
    if power_of_two(groups):
        return group ^ hop
    return (group + hop) % groups


def source(group, hop, groups):
    if power_of_two(groups):
        return group ^ hop
    return (group - hop + groups) % groups


def cost(flops, *arrays):
    moved = sum(array.size * array.dtype.itemsize for array in arrays)
    return pl.CostEstimate(flops=flops, bytes_accessed=moved, transcendentals=0)


def after(value, earlier):
    return lax.optimization_barrier((value, earlier))[0]


def place_on_space(lanes):
    index = lax.axis_index("space")
    return lax.div(index, lanes), lax.rem(index, lanes)


def swap_lanes(value, lanes, groups):
    pairs = [(g * lanes + c, g * lanes + 1 - c) for g in range(groups) for c in range(lanes)]
    return lax.ppermute(value, "space", pairs)


def hop_groups(value, hop, lanes, groups):
    pairs = [
        (g * lanes + c, partner(g, hop, groups) * lanes + c)
        for g in range(groups)
        for c in range(lanes)
    ]
    return lax.ppermute(value, "space", pairs)


def gather_groups(value, waits, lanes, groups):
    if power_of_two(groups):
        for step in range(groups.bit_length() - 1):
            start, done = waits[min(step, len(waits) - 1)]
            met = hop_groups(after(value, start), 1 << step, lanes, groups)
            value = jnp.concatenate([value, after(met, done)])
        return value
    return jnp.concatenate(
        [value] + [hop_groups(value, hop, lanes, groups) for hop in range(1, groups)]
    )


def products(scale, queries, grad_out):
    return scale * lax.dot_general(
        jnp.maximum(queries, 0),
        grad_out,
        CONTRACT_ROWS,
        preferred_element_type=jnp.float32,
    )


def partial_kernel(lanes, other, scale, q_ref, o_ref, part_ref):
    span, head = part_ref.shape
    _, lane = place_on_space(lanes)
    base = (1 - lane if other else lane) * span
    for h in range(span // head):
        rows = pl.ds(h * head, head)
        cols = pl.ds(pl.multiple_of(base + h * head, head), head)
        part_ref[rows, :] = products(
            scale, q_ref[:, rows if other else cols], o_ref[:, cols]
        ).astype(part_ref.dtype)


def partial_products(queries, grad_out, head, lanes, other, scale):
    tokens, width = grad_out.shape
    span = width // lanes
    return pl.pallas_call(
        functools.partial(partial_kernel, lanes, other, scale),
        out_shape=jax.ShapeDtypeStruct((span, head), jnp.bfloat16 if other else jnp.float32),
        in_specs=[IN_VMEM, IN_VMEM],
        out_specs=IN_VMEM,
        compiler_params=pltpu.CompilerParams(vmem_limit_bytes=VMEM_BYTES),
        cost_estimate=cost(2 * tokens * span * head, queries),
        name="partial_other" if other else "partial_own",
    )(queries, grad_out)


def cut_kernel(lanes, groups, *refs):
    parts, outs = refs[:lanes], refs[lanes:]
    group, _ = place_on_space(lanes)
    rows = outs[0].shape[0]
    for hop, out_ref in enumerate(outs):
        there = pl.ds(pl.multiple_of(partner(group, hop, groups) * rows, rows), rows)
        total = parts[0][there, :]
        for part in parts[1:]:
            total = total + part[there, :].astype(jnp.float32)
        out_ref[...] = total.astype(out_ref.dtype)


def cut_by_group(parts, lanes, groups):
    span, head = parts[0].shape
    rows = span // groups
    outs = [jax.ShapeDtypeStruct((rows, head), jnp.float32)]
    outs += [jax.ShapeDtypeStruct((rows, head), jnp.bfloat16)] * (groups - 1)
    return pl.pallas_call(
        functools.partial(cut_kernel, lanes, groups),
        out_shape=outs,
        in_specs=[IN_VMEM] * lanes,
        out_specs=[IN_VMEM] * groups,
        compiler_params=pltpu.CompilerParams(vmem_limit_bytes=VMEM_BYTES),
        cost_estimate=cost(span * head, *parts),
        name="cut_by_group",
    )(*parts)


def key_value_products(k_ref, v_ref, state, cols, dk_ref, dv_ref):
    head = state.shape[1]
    for h in range(state.shape[0] // head):
        local = pl.ds(h * head, head)
        keys, grad_state = k_ref[:, cols(h)], state[local, :]
        full = lax.dot_general(
            v_ref[:, cols(h)], grad_state, CONTRACT_COLS, preferred_element_type=jnp.float32
        )
        dk_ref[:, local] = jnp.where(keys > 0, full, 0.0).astype(dk_ref.dtype)
        dv_ref[:, local] = jnp.dot(
            jnp.maximum(keys, 0), grad_state, preferred_element_type=jnp.float32
        ).astype(dv_ref.dtype)
        yield h


def place_pieces(pieces, group, groups, state):
    for hop, piece in enumerate(pieces):
        rows = piece.shape[0]
        owner = source(group, hop, groups)
        state[pl.ds(pl.multiple_of(owner * rows, rows), rows), :] = piece[...]


def near_kernel(lanes, groups, q_ref, o_ref, k_ref, v_ref, *rest):
    sides, pieces = rest[:lanes], rest[lanes : lanes + groups]
    dq_hbm, dk_ref, dv_ref, saved, state, dq_buf, piece_sems, dq_sems = rest[lanes + groups :]
    heads, head, _ = saved.shape
    rows = sides[0].shape[2]
    group, lane = place_on_space(lanes)
    copies = []
    for other, side in enumerate(sides):
        there = 1 - lane if other else lane
        for hop in range(groups):
            owner = source(group, hop, groups) * lanes + there
            dst = pl.ds(pl.multiple_of(owner * rows, rows), rows)
            if rows % 16 == 0:
                saved[:, dst, :] = side[hop]
            else:
                copies.append(
                    pltpu.make_async_copy(
                        side.at[hop], saved.at[:, dst, :], piece_sems.at[other, hop]
                    )
                )
    for copy in copies:
        copy.start()
    for copy in copies:
        copy.wait()
    steps = dq_sems.shape[0]
    part = heads // steps
    copies = []
    for step in range(steps):
        for h in range(step * part, (step + 1) * part):
            cols = pl.ds(h * head, head)
            full = lax.dot_general(
                o_ref[:, cols], saved[h], CONTRACT_COLS, preferred_element_type=jnp.float32
            )
            dq_buf[:, cols] = jnp.where(q_ref[:, cols] > 0, full, 0.0).astype(dq_buf.dtype)
        cols = pl.ds(step * part * head, part * head)
        copies.append(pltpu.make_async_copy(dq_buf.at[:, cols], dq_hbm.at[:, cols], dq_sems.at[step]))
        copies[-1].start()
    place_pieces(pieces, group, groups, state)
    base = lane * state.shape[0]
    for _ in key_value_products(
        k_ref,
        v_ref,
        state,
        lambda h: pl.ds(pl.multiple_of(base + h * head, head), head),
        dk_ref,
        dv_ref,
    ):
        pass
    for copy in copies:
        copy.wait()


def near_grads(queries, grad_out, keys, values, sides, pieces):
    lanes, groups = len(sides), len(pieces)
    (tokens, width), heads, (rows, head) = queries.shape, sides[0].shape[1], pieces[0].shape
    span = groups * rows
    steps = math.gcd(heads, 4)
    return pl.pallas_call(
        functools.partial(near_kernel, lanes, groups),
        out_shape=(
            jax.ShapeDtypeStruct(queries.shape, queries.dtype),
            jax.ShapeDtypeStruct((tokens, span), keys.dtype),
            jax.ShapeDtypeStruct((tokens, span), values.dtype),
        ),
        in_specs=[IN_VMEM] * (4 + lanes + groups),
        out_specs=(ANYWHERE, IN_VMEM, IN_VMEM),
        scratch_shapes=[
            pltpu.VMEM((heads, head, head), sides[0].dtype),
            pltpu.VMEM((span, head), pieces[0].dtype),
            pltpu.VMEM((tokens, width), queries.dtype),
            pltpu.SemaphoreType.DMA((lanes, groups)),
            pltpu.SemaphoreType.DMA((steps,)),
        ],
        compiler_params=pltpu.CompilerParams(vmem_limit_bytes=VMEM_BYTES),
        cost_estimate=cost(4 * queries.size * head, queries, queries, grad_out, *sides),
        name="near_grads",
    )(queries, grad_out, keys, values, *sides, *pieces)


def far_kernel(lanes, groups, k_ref, v_ref, *rest):
    near, pieces = rest[:2], rest[2:-6]
    dk_hbm, dv_hbm, state, dk_buf, dv_buf, sems = rest[-6:]
    span, head = state.shape
    group, lane = place_on_space(lanes)
    outs = (dk_hbm, dv_hbm)
    copies = []
    for at in range(2):
        mine = pl.ds(pl.multiple_of(lane * span, head), span)
        copies.append(pltpu.make_async_copy(near[at], outs[at].at[:, mine], sems.at[at, 0]))
        copies[-1].start()
    if pieces:
        place_pieces(pieces, group, groups, state)
        base = (1 - lane) * span
        part = span // head // (sems.shape[1] - 1)
        for h in key_value_products(
            k_ref,
            v_ref,
            state,
            lambda h: pl.ds(pl.multiple_of(base + h * head, head), head),
            dk_buf,
            dv_buf,
        ):
            if (h + 1) % part == 0:
                src = pl.ds((h + 1 - part) * head, part * head)
                dst = pl.ds(pl.multiple_of(base + (h + 1 - part) * head, head), part * head)
                for at, buf in enumerate((dk_buf, dv_buf)):
                    copies.append(
                        pltpu.make_async_copy(
                            buf.at[:, src], outs[at].at[:, dst], sems.at[at, 1 + h // part]
                        )
                    )
                    copies[-1].start()
    for copy in copies:
        copy.wait()


def far_grads(keys, values, near, pieces, lanes, groups):
    tokens, span = near[0].shape
    head = pieces[0].shape[1] if pieces else span
    return pl.pallas_call(
        functools.partial(far_kernel, lanes, groups),
        out_shape=(
            jax.ShapeDtypeStruct(keys.shape, keys.dtype),
            jax.ShapeDtypeStruct(values.shape, values.dtype),
        ),
        in_specs=[IN_VMEM] * (4 + len(pieces)),
        out_specs=(ANYWHERE, ANYWHERE),
        scratch_shapes=[
            pltpu.VMEM((span, head), keys.dtype),
            pltpu.VMEM((tokens, span), keys.dtype),
            pltpu.VMEM((tokens, span), values.dtype),
            pltpu.SemaphoreType.DMA((2, 1 + math.gcd(span // head, 5))),
        ],
        compiler_params=pltpu.CompilerParams(vmem_limit_bytes=VMEM_BYTES),
        cost_estimate=cost(4 * tokens * span * head, *near),
        name="far_grads",
    )(keys, values, *near, *pieces)


def suffix_sum(share, blocks):
    block = lax.axis_index("tm")
    suffix = total = first = share
    if power_of_two(blocks):
        hop = 1
        while hop < blocks:
            pairs = [(b, b ^ hop) for b in range(blocks)]
            met = lax.ppermute(total.astype(jnp.bfloat16), "tm", pairs).astype(jnp.float32)
            suffix = suffix + jnp.where(block & hop == 0, met, 0.0)
            total = total + met
            first = total if hop == 1 else first
            hop *= 2
    else:
        for hop in range(1, blocks):
            pairs = [(b, b - hop) for b in range(hop, blocks)]
            later = lax.ppermute(share.astype(jnp.bfloat16), "tm", pairs)
            suffix = suffix + later.astype(jnp.float32)
    return suffix.astype(jnp.bfloat16), first


def per_device(queries, keys, values, grad_out, saved_state):
    heads, _, head = saved_state.shape[1:]
    blocks, devices = lax.axis_size("tm"), lax.axis_size("space")
    lanes = 2 if devices % 2 == 0 and heads % 2 == 0 else 1
    groups = devices // lanes
    far_first = range(groups - 1, 0, -1)
    scale = 1.0 / math.sqrt(queries.shape[0] * blocks * devices * head)

    parts = []
    if lanes > 1:
        _, lane = place_on_space(lanes)
        span = queries.shape[1] // lanes
        starts = (jnp.zeros_like(lane), (1 - lane) * span)
        cut = lax.dynamic_slice(
            queries, starts, (queries.shape[0], span), allow_negative_indices=False
        )
        theirs = partial_products(cut, grad_out, head, lanes, True, scale)
        parts.append(swap_lanes(theirs, lanes, groups))
        queries = after(queries, cut)
    parts.insert(0, partial_products(queries, grad_out, head, lanes, False, scale))
    share, *sends = cut_by_group(parts, lanes, groups)
    for hop in far_first:
        share = share + hop_groups(sends[hop - 1], hop, lanes, groups).astype(jnp.float32)
    own, first = suffix_sum(share, blocks)
    met = [hop_groups(own, hop, lanes, groups) for hop in far_first]

    saved = gather_groups(saved_state, [(parts[0], ()), (share, ())], lanes, groups)
    sides = [saved] + ([swap_lanes(saved, lanes, groups)] if lanes > 1 else [])

    near = [own, *met[::-1]]
    far = [swap_lanes(piece, lanes, groups) for piece in near] if lanes > 1 else []
    grad_q, *halves = near_grads(queries, grad_out, keys, values, sides, near)
    return grad_q, *far_grads(keys, values, halves, far, lanes, groups)


def solution(mesh):
    tokens = P(("tm", "space"), None)
    return jax.shard_map(
        per_device,
        mesh=mesh,
        in_specs=(tokens, tokens, tokens, tokens, P("tm", None, "space", None)),
        out_specs=(tokens, tokens, tokens),
        check_vma=False,
    )
```

```python
import functools
import math

import jax
import jax.numpy as jnp
from jax import lax
from jax.experimental import pallas as pl
from jax.experimental.pallas import tpu as pltpu
from jax.sharding import PartitionSpec as P

CONTRACT_ROWS = (((0,), (0,)), ((), ()))
CONTRACT_COLS = (((1,), (1,)), ((), ()))
VMEM_BYTES = 16 * 1024 * 1024
ANYWHERE = pl.BlockSpec(memory_space=pl.ANY)
IN_VMEM = pl.BlockSpec(memory_space=pltpu.VMEM)


def power_of_two(count):
    return count & (count - 1) == 0


def partner(group, hop, groups):
    if power_of_two(groups):
        return group ^ hop
    return (group + hop) % groups


def source(group, hop, groups):
    if power_of_two(groups):
        return group ^ hop
    return (group - hop + groups) % groups


def cost(flops, *arrays):
    moved = sum(array.size * array.dtype.itemsize for array in arrays)
    return pl.CostEstimate(flops=flops, bytes_accessed=moved, transcendentals=0)


def after(value, earlier):
    return lax.optimization_barrier((value, earlier))[0]


def place_on_space(lanes):
    index = lax.axis_index("space")
    return lax.div(index, lanes), lax.rem(index, lanes)


def swap_lanes(value, lanes, groups):
    pairs = [(g * lanes + c, g * lanes + 1 - c) for g in range(groups) for c in range(lanes)]
    return lax.ppermute(value, "space", pairs)


def hop_groups(value, hop, lanes, groups):
    pairs = [
        (g * lanes + c, partner(g, hop, groups) * lanes + c)
        for g in range(groups)
        for c in range(lanes)
    ]
    return lax.ppermute(value, "space", pairs)


def gather_groups(value, waits, lanes, groups):
    if power_of_two(groups):
        for step in range(groups.bit_length() - 1):
            start, done = waits[min(step, len(waits) - 1)]
            met = hop_groups(after(value, start), 1 << step, lanes, groups)
            value = jnp.concatenate([value, after(met, done)])
        return value
    return jnp.concatenate(
        [value] + [hop_groups(value, hop, lanes, groups) for hop in range(1, groups)]
    )


def products(scale, queries, grad_out):
    return scale * lax.dot_general(
        jnp.maximum(queries, 0),
        grad_out,
        CONTRACT_ROWS,
        preferred_element_type=jnp.float32,
    )


def partial_kernel(lanes, other, scale, q_ref, o_ref, part_ref):
    span, head = part_ref.shape
    _, lane = place_on_space(lanes)
    base = (1 - lane if other else lane) * span
    for h in range(span // head):
        rows = pl.ds(h * head, head)
        cols = pl.ds(pl.multiple_of(base + h * head, head), head)
        part_ref[rows, :] = products(
            scale, q_ref[:, rows if other else cols], o_ref[:, cols]
        ).astype(part_ref.dtype)


def partial_products(queries, grad_out, head, lanes, other, scale):
    tokens, width = grad_out.shape
    span = width // lanes
    return pl.pallas_call(
        functools.partial(partial_kernel, lanes, other, scale),
        out_shape=jax.ShapeDtypeStruct((span, head), jnp.bfloat16 if other else jnp.float32),
        in_specs=[IN_VMEM, IN_VMEM],
        out_specs=IN_VMEM,
        compiler_params=pltpu.CompilerParams(vmem_limit_bytes=VMEM_BYTES),
        cost_estimate=cost(2 * tokens * span * head, queries),
        name="partial_other" if other else "partial_own",
    )(queries, grad_out)


def cut_kernel(lanes, groups, *refs):
    parts, outs = refs[:lanes], refs[lanes:]
    group, _ = place_on_space(lanes)
    rows = outs[0].shape[0]
    for hop, out_ref in enumerate(outs):
        there = pl.ds(pl.multiple_of(partner(group, hop, groups) * rows, rows), rows)
        total = parts[0][there, :]
        for part in parts[1:]:
            total = total + part[there, :].astype(jnp.float32)
        out_ref[...] = total.astype(out_ref.dtype)


def cut_by_group(parts, lanes, groups):
    span, head = parts[0].shape
    rows = span // groups
    outs = [jax.ShapeDtypeStruct((rows, head), jnp.float32)]
    outs += [jax.ShapeDtypeStruct((rows, head), jnp.bfloat16)] * (groups - 1)
    return pl.pallas_call(
        functools.partial(cut_kernel, lanes, groups),
        out_shape=outs,
        in_specs=[IN_VMEM] * lanes,
        out_specs=[IN_VMEM] * groups,
        compiler_params=pltpu.CompilerParams(vmem_limit_bytes=VMEM_BYTES),
        cost_estimate=cost(span * head, *parts),
        name="cut_by_group",
    )(*parts)


def key_value_products(k_ref, v_ref, state, cols, dk_ref, dv_ref):
    head = state.shape[1]
    for h in range(state.shape[0] // head):
        local = pl.ds(h * head, head)
        keys, grad_state = k_ref[:, cols(h)], state[local, :]
        full = lax.dot_general(
            v_ref[:, cols(h)], grad_state, CONTRACT_COLS, preferred_element_type=jnp.float32
        )
        dk_ref[:, local] = jnp.where(keys > 0, full, 0.0).astype(dk_ref.dtype)
        dv_ref[:, local] = jnp.dot(
            jnp.maximum(keys, 0), grad_state, preferred_element_type=jnp.float32
        ).astype(dv_ref.dtype)
        yield h


def place_pieces(pieces, group, groups, state):
    for hop, piece in enumerate(pieces):
        rows = piece.shape[0]
        owner = source(group, hop, groups)
        state[pl.ds(pl.multiple_of(owner * rows, rows), rows), :] = piece[...]


def near_kernel(lanes, groups, q_ref, o_ref, k_ref, v_ref, *rest):
    sides, pieces = rest[:lanes], rest[lanes : lanes + groups]
    dq_ref, dk_ref, dv_ref, saved, state, sems = rest[lanes + groups :]
    heads, head, _ = saved.shape
    rows = sides[0].shape[2]
    group, lane = place_on_space(lanes)
    copies = []
    for other, side in enumerate(sides):
        there = 1 - lane if other else lane
        for hop in range(groups):
            owner = source(group, hop, groups) * lanes + there
            dst = pl.ds(pl.multiple_of(owner * rows, rows), rows)
            if rows % 16 == 0:
                saved[:, dst, :] = side[hop]
            else:
                copies.append(
                    pltpu.make_async_copy(side.at[hop], saved.at[:, dst, :], sems.at[other, hop])
                )
    for copy in copies:
        copy.start()
    for copy in copies:
        copy.wait()
    for h in range(heads):
        cols = pl.ds(h * head, head)
        full = lax.dot_general(
            o_ref[:, cols], saved[h], CONTRACT_COLS, preferred_element_type=jnp.float32
        )
        dq_ref[:, cols] = jnp.where(q_ref[:, cols] > 0, full, 0.0).astype(dq_ref.dtype)
    place_pieces(pieces, group, groups, state)
    base = lane * state.shape[0]
    for _ in key_value_products(
        k_ref,
        v_ref,
        state,
        lambda h: pl.ds(pl.multiple_of(base + h * head, head), head),
        dk_ref,
        dv_ref,
    ):
        pass


def near_grads(queries, grad_out, keys, values, sides, pieces):
    lanes, groups = len(sides), len(pieces)
    tokens, heads, (rows, head) = queries.shape[0], sides[0].shape[1], pieces[0].shape
    span = groups * rows
    return pl.pallas_call(
        functools.partial(near_kernel, lanes, groups),
        out_shape=(
            jax.ShapeDtypeStruct(queries.shape, queries.dtype),
            jax.ShapeDtypeStruct((tokens, span), keys.dtype),
            jax.ShapeDtypeStruct((tokens, span), values.dtype),
        ),
        in_specs=[IN_VMEM] * (4 + lanes + groups),
        out_specs=(IN_VMEM, IN_VMEM, IN_VMEM),
        scratch_shapes=[
            pltpu.VMEM((heads, head, head), sides[0].dtype),
            pltpu.VMEM((span, head), pieces[0].dtype),
            pltpu.SemaphoreType.DMA((lanes, groups)),
        ],
        compiler_params=pltpu.CompilerParams(vmem_limit_bytes=VMEM_BYTES),
        cost_estimate=cost(4 * queries.size * head, queries, queries, grad_out, *sides),
        name="near_grads",
    )(queries, grad_out, keys, values, *sides, *pieces)


def far_kernel(lanes, groups, k_ref, v_ref, *rest):
    dq_ref, near, pieces = rest[0], rest[1:3], rest[3:-8]
    dq_hbm, *outs = rest[-8:-5]
    state, dk_buf, dv_buf, sems, dq_sem = rest[-5:]
    span, head = state.shape
    group, lane = place_on_space(lanes)
    copies = [pltpu.make_async_copy(dq_ref, dq_hbm, dq_sem)]
    copies[0].start()
    for at in range(2):
        mine = pl.ds(pl.multiple_of(lane * span, head), span)
        copies.append(pltpu.make_async_copy(near[at], outs[at].at[:, mine], sems.at[at, 0]))
        copies[-1].start()
    if pieces:
        place_pieces(pieces, group, groups, state)
        base = (1 - lane) * span
        part = span // head // (sems.shape[1] - 1)
        for h in key_value_products(
            k_ref,
            v_ref,
            state,
            lambda h: pl.ds(pl.multiple_of(base + h * head, head), head),
            dk_buf,
            dv_buf,
        ):
            if (h + 1) % part == 0:
                src = pl.ds((h + 1 - part) * head, part * head)
                dst = pl.ds(pl.multiple_of(base + (h + 1 - part) * head, head), part * head)
                for at, buf in enumerate((dk_buf, dv_buf)):
                    copies.append(
                        pltpu.make_async_copy(
                            buf.at[:, src], outs[at].at[:, dst], sems.at[at, 1 + h // part]
                        )
                    )
                    copies[-1].start()
    for copy in copies:
        copy.wait()


def far_grads(keys, values, near, pieces, lanes, groups):
    tokens, span = near[1].shape
    head = pieces[0].shape[1] if pieces else span
    return pl.pallas_call(
        functools.partial(far_kernel, lanes, groups),
        out_shape=(
            jax.ShapeDtypeStruct(near[0].shape, near[0].dtype),
            jax.ShapeDtypeStruct(keys.shape, keys.dtype),
            jax.ShapeDtypeStruct(values.shape, values.dtype),
        ),
        in_specs=[IN_VMEM] * (5 + len(pieces)),
        out_specs=(ANYWHERE,) * 3,
        scratch_shapes=[
            pltpu.VMEM((span, head), keys.dtype),
            pltpu.VMEM((tokens, span), keys.dtype),
            pltpu.VMEM((tokens, span), values.dtype),
            pltpu.SemaphoreType.DMA((2, 1 + math.gcd(span // head, 5))),
            pltpu.SemaphoreType.DMA,
        ],
        compiler_params=pltpu.CompilerParams(vmem_limit_bytes=VMEM_BYTES),
        cost_estimate=cost(4 * tokens * span * head, *near),
        name="far_grads",
    )(keys, values, *near, *pieces)


def suffix_sum(share, blocks):
    block = lax.axis_index("tm")
    suffix = total = first = share
    if power_of_two(blocks):
        hop = 1
        while hop < blocks:
            pairs = [(b, b ^ hop) for b in range(blocks)]
            met = lax.ppermute(total.astype(jnp.bfloat16), "tm", pairs).astype(jnp.float32)
            suffix = suffix + jnp.where(block & hop == 0, met, 0.0)
            total = total + met
            first = total if hop == 1 else first
            hop *= 2
    else:
        for hop in range(1, blocks):
            pairs = [(b, b - hop) for b in range(hop, blocks)]
            later = lax.ppermute(share.astype(jnp.bfloat16), "tm", pairs)
            suffix = suffix + later.astype(jnp.float32)
    return suffix.astype(jnp.bfloat16), first


def per_device(queries, keys, values, grad_out, saved_state):
    heads, _, head = saved_state.shape[1:]
    blocks, devices = lax.axis_size("tm"), lax.axis_size("space")
    lanes = 2 if devices % 2 == 0 and heads % 2 == 0 else 1
    groups = devices // lanes
    far_first = range(groups - 1, 0, -1)
    scale = 1.0 / math.sqrt(queries.shape[0] * blocks * devices * head)

    parts = []
    if lanes > 1:
        _, lane = place_on_space(lanes)
        span = queries.shape[1] // lanes
        starts = (jnp.zeros_like(lane), (1 - lane) * span)
        cut = lax.dynamic_slice(
            queries, starts, (queries.shape[0], span), allow_negative_indices=False
        )
        theirs = partial_products(cut, grad_out, head, lanes, True, scale)
        parts.append(swap_lanes(theirs, lanes, groups))
        queries = after(queries, cut)
    parts.insert(0, partial_products(queries, grad_out, head, lanes, False, scale))
    share, *sends = cut_by_group(parts, lanes, groups)
    for hop in far_first:
        share = share + hop_groups(sends[hop - 1], hop, lanes, groups).astype(jnp.float32)
    own, first = suffix_sum(share, blocks)
    met = [hop_groups(own, hop, lanes, groups) for hop in far_first]

    saved = gather_groups(saved_state, [(parts[0], ()), (share, ())], lanes, groups)
    sides = [saved] + ([swap_lanes(saved, lanes, groups)] if lanes > 1 else [])

    near = [own, *met[::-1]]
    far = [swap_lanes(piece, lanes, groups) for piece in near] if lanes > 1 else []
    ready = near_grads(queries, grad_out, keys, values, sides, near)
    return far_grads(keys, values, ready, far, lanes, groups)


def solution(mesh):
    tokens = P(("tm", "space"), None)
    return jax.shard_map(
        per_device,
        mesh=mesh,
        in_specs=(tokens, tokens, tokens, tokens, P("tm", None, "space", None)),
        out_specs=(tokens, tokens, tokens),
        check_vma=False,
    )
```

```python
import functools
import math

import jax
import jax.numpy as jnp
from jax import lax
from jax.experimental import pallas as pl
from jax.experimental.pallas import tpu as pltpu
from jax.sharding import PartitionSpec as P

CONTRACT_ROWS = (((0,), (0,)), ((), ()))
CONTRACT_COLS = (((1,), (1,)), ((), ()))
VMEM_BYTES = 16 * 1024 * 1024
ANYWHERE = pl.BlockSpec(memory_space=pl.ANY)
IN_VMEM = pl.BlockSpec(memory_space=pltpu.VMEM)


def power_of_two(count):
    return count & (count - 1) == 0


def partner(group, hop, groups):
    if power_of_two(groups):
        return group ^ hop
    return (group + hop) % groups


def source(group, hop, groups):
    if power_of_two(groups):
        return group ^ hop
    return (group - hop + groups) % groups


def cost(flops, *arrays):
    moved = sum(array.size * array.dtype.itemsize for array in arrays)
    return pl.CostEstimate(flops=flops, bytes_accessed=moved, transcendentals=0)


def after(value, earlier):
    return lax.optimization_barrier((value, earlier))[0]


def place_on_space(lanes):
    index = lax.axis_index("space")
    return lax.div(index, lanes), lax.rem(index, lanes)


def swap_lanes(value, lanes, groups):
    pairs = [(g * lanes + c, g * lanes + 1 - c) for g in range(groups) for c in range(lanes)]
    return lax.ppermute(value, "space", pairs)


def hop_groups(value, hop, lanes, groups):
    pairs = [
        (g * lanes + c, partner(g, hop, groups) * lanes + c)
        for g in range(groups)
        for c in range(lanes)
    ]
    return lax.ppermute(value, "space", pairs)


def gather_groups(value, waits, lanes, groups):
    if power_of_two(groups):
        for step in range(groups.bit_length() - 1):
            start, done = waits[min(step, len(waits) - 1)]
            met = hop_groups(after(value, start), 1 << step, lanes, groups)
            value = jnp.concatenate([value, after(met, done)])
        return value
    return jnp.concatenate(
        [value] + [hop_groups(value, hop, lanes, groups) for hop in range(1, groups)]
    )


def products(scale, queries, grad_out):
    return scale * lax.dot_general(
        jnp.maximum(queries, 0),
        grad_out,
        CONTRACT_ROWS,
        preferred_element_type=jnp.float32,
    )


def partial_kernel(lanes, other, scale, q_ref, o_ref, part_ref):
    span, head = part_ref.shape
    _, lane = place_on_space(lanes)
    base = (1 - lane if other else lane) * span
    for h in range(span // head):
        rows = pl.ds(h * head, head)
        cols = pl.ds(pl.multiple_of(base + h * head, head), head)
        part_ref[rows, :] = products(
            scale, q_ref[:, rows if other else cols], o_ref[:, cols]
        ).astype(part_ref.dtype)


def partial_products(queries, grad_out, head, lanes, other, scale):
    tokens, width = grad_out.shape
    span = width // lanes
    return pl.pallas_call(
        functools.partial(partial_kernel, lanes, other, scale),
        out_shape=jax.ShapeDtypeStruct((span, head), jnp.bfloat16 if other else jnp.float32),
        in_specs=[IN_VMEM, IN_VMEM],
        out_specs=IN_VMEM,
        compiler_params=pltpu.CompilerParams(vmem_limit_bytes=VMEM_BYTES),
        cost_estimate=cost(2 * tokens * span * head, queries),
        name="partial_other" if other else "partial_own",
    )(queries, grad_out)


def cut_kernel(lanes, groups, *refs):
    parts, outs = refs[:lanes], refs[lanes:]
    group, _ = place_on_space(lanes)
    rows = outs[0].shape[0]
    for hop, out_ref in enumerate(outs):
        there = pl.ds(pl.multiple_of(partner(group, hop, groups) * rows, rows), rows)
        total = parts[0][there, :]
        for part in parts[1:]:
            total = total + part[there, :].astype(jnp.float32)
        out_ref[...] = total.astype(out_ref.dtype)


def cut_by_group(parts, lanes, groups):
    span, head = parts[0].shape
    rows = span // groups
    outs = [jax.ShapeDtypeStruct((rows, head), jnp.float32)]
    outs += [jax.ShapeDtypeStruct((rows, head), jnp.bfloat16)] * (groups - 1)
    return pl.pallas_call(
        functools.partial(cut_kernel, lanes, groups),
        out_shape=outs,
        in_specs=[IN_VMEM] * lanes,
        out_specs=[IN_VMEM] * groups,
        compiler_params=pltpu.CompilerParams(vmem_limit_bytes=VMEM_BYTES),
        cost_estimate=cost(span * head, *parts),
        name="cut_by_group",
    )(*parts)


def key_value_products(k_ref, v_ref, state, cols, dk_ref, dv_ref):
    head = state.shape[1]
    for h in range(state.shape[0] // head):
        local = pl.ds(h * head, head)
        keys, grad_state = k_ref[:, cols(h)], state[local, :]
        full = lax.dot_general(
            v_ref[:, cols(h)], grad_state, CONTRACT_COLS, preferred_element_type=jnp.float32
        )
        dk_ref[:, local] = jnp.where(keys > 0, full, 0.0).astype(dk_ref.dtype)
        dv_ref[:, local] = jnp.dot(
            jnp.maximum(keys, 0), grad_state, preferred_element_type=jnp.float32
        ).astype(dv_ref.dtype)
        yield h


def place_pieces(pieces, group, groups, state):
    for hop, piece in enumerate(pieces):
        rows = piece.shape[0]
        owner = source(group, hop, groups)
        state[pl.ds(pl.multiple_of(owner * rows, rows), rows), :] = piece[...]


def near_kernel(lanes, groups, q_ref, o_ref, k_ref, v_ref, *rest):
    sides, pieces = rest[:lanes], rest[lanes : lanes + groups]
    dq_ref, dk_ref, dv_ref, saved, state, sems = rest[lanes + groups :]
    heads, head, _ = saved.shape
    rows = sides[0].shape[2]
    group, lane = place_on_space(lanes)
    copies = []
    for other, side in enumerate(sides):
        there = 1 - lane if other else lane
        for hop in range(groups):
            owner = source(group, hop, groups) * lanes + there
            dst = pl.ds(pl.multiple_of(owner * rows, rows), rows)
            if rows % 16 == 0:
                saved[:, dst, :] = side[hop]
            else:
                copies.append(
                    pltpu.make_async_copy(side.at[hop], saved.at[:, dst, :], sems.at[other, hop])
                )
    for copy in copies:
        copy.start()
    for copy in copies:
        copy.wait()
    for h in range(heads):
        cols = pl.ds(h * head, head)
        full = lax.dot_general(
            o_ref[:, cols], saved[h], CONTRACT_COLS, preferred_element_type=jnp.float32
        )
        dq_ref[:, cols] = jnp.where(q_ref[:, cols] > 0, full, 0.0).astype(dq_ref.dtype)
    place_pieces(pieces, group, groups, state)
    base = lane * state.shape[0]
    for _ in key_value_products(
        k_ref,
        v_ref,
        state,
        lambda h: pl.ds(pl.multiple_of(base + h * head, head), head),
        dk_ref,
        dv_ref,
    ):
        pass


def near_grads(queries, grad_out, keys, values, sides, pieces):
    lanes, groups = len(sides), len(pieces)
    tokens, heads, (rows, head) = queries.shape[0], sides[0].shape[1], pieces[0].shape
    span = groups * rows
    return pl.pallas_call(
        functools.partial(near_kernel, lanes, groups),
        out_shape=(
            jax.ShapeDtypeStruct(queries.shape, queries.dtype),
            jax.ShapeDtypeStruct((tokens, span), keys.dtype),
            jax.ShapeDtypeStruct((tokens, span), values.dtype),
        ),
        in_specs=[IN_VMEM] * (4 + lanes + groups),
        out_specs=(IN_VMEM, IN_VMEM, IN_VMEM),
        scratch_shapes=[
            pltpu.VMEM((heads, head, head), sides[0].dtype),
            pltpu.VMEM((span, head), pieces[0].dtype),
            pltpu.SemaphoreType.DMA((lanes, groups)),
        ],
        compiler_params=pltpu.CompilerParams(vmem_limit_bytes=VMEM_BYTES),
        cost_estimate=cost(4 * queries.size * head, queries, queries, grad_out, *sides),
        name="near_grads",
    )(queries, grad_out, keys, values, *sides, *pieces)


def far_kernel(lanes, groups, k_ref, v_ref, *rest):
    dq_ref, near, pieces = rest[0], rest[1:3], rest[3:-8]
    dq_hbm, *outs = rest[-8:-5]
    state, dk_buf, dv_buf, sems, dq_sems = rest[-5:]
    span, head = state.shape
    group, lane = place_on_space(lanes)
    copies = []
    rows = dq_ref.shape[0] // dq_sems.shape[0]
    for at in range(dq_sems.shape[0]):
        mine = pl.ds(at * rows, rows)
        copies.append(pltpu.make_async_copy(dq_ref.at[mine, :], dq_hbm.at[mine, :], dq_sems.at[at]))
        copies[-1].start()
    for at in range(2):
        mine = pl.ds(pl.multiple_of(lane * span, head), span)
        copies.append(pltpu.make_async_copy(near[at], outs[at].at[:, mine], sems.at[at, 0]))
        copies[-1].start()
    if pieces:
        place_pieces(pieces, group, groups, state)
        base = (1 - lane) * span
        part = span // head // (sems.shape[1] - 1)
        for h in key_value_products(
            k_ref,
            v_ref,
            state,
            lambda h: pl.ds(pl.multiple_of(base + h * head, head), head),
            dk_buf,
            dv_buf,
        ):
            if (h + 1) % part == 0:
                src = pl.ds((h + 1 - part) * head, part * head)
                dst = pl.ds(pl.multiple_of(base + (h + 1 - part) * head, head), part * head)
                for at, buf in enumerate((dk_buf, dv_buf)):
                    copies.append(
                        pltpu.make_async_copy(
                            buf.at[:, src], outs[at].at[:, dst], sems.at[at, 1 + h // part]
                        )
                    )
                    copies[-1].start()
    for copy in copies:
        copy.wait()


def far_grads(keys, values, near, pieces, lanes, groups):
    tokens, span = near[1].shape
    head = pieces[0].shape[1] if pieces else span
    return pl.pallas_call(
        functools.partial(far_kernel, lanes, groups),
        out_shape=(
            jax.ShapeDtypeStruct(near[0].shape, near[0].dtype),
            jax.ShapeDtypeStruct(keys.shape, keys.dtype),
            jax.ShapeDtypeStruct(values.shape, values.dtype),
        ),
        in_specs=[IN_VMEM] * (5 + len(pieces)),
        out_specs=(ANYWHERE,) * 3,
        scratch_shapes=[
            pltpu.VMEM((span, head), keys.dtype),
            pltpu.VMEM((tokens, span), keys.dtype),
            pltpu.VMEM((tokens, span), values.dtype),
            pltpu.SemaphoreType.DMA((2, 1 + math.gcd(span // head, 5))),
            pltpu.SemaphoreType.DMA((math.gcd(tokens // 16, 4) if tokens % 16 == 0 else 1,)),
        ],
        compiler_params=pltpu.CompilerParams(vmem_limit_bytes=VMEM_BYTES),
        cost_estimate=cost(4 * tokens * span * head, *near),
        name="far_grads",
    )(keys, values, *near, *pieces)


def suffix_sum(share, blocks):
    block = lax.axis_index("tm")
    suffix = total = first = share
    if power_of_two(blocks):
        hop = 1
        while hop < blocks:
            pairs = [(b, b ^ hop) for b in range(blocks)]
            met = lax.ppermute(total.astype(jnp.bfloat16), "tm", pairs).astype(jnp.float32)
            suffix = suffix + jnp.where(block & hop == 0, met, 0.0)
            total = total + met
            first = total if hop == 1 else first
            hop *= 2
    else:
        for hop in range(1, blocks):
            pairs = [(b, b - hop) for b in range(hop, blocks)]
            later = lax.ppermute(share.astype(jnp.bfloat16), "tm", pairs)
            suffix = suffix + later.astype(jnp.float32)
    return suffix.astype(jnp.bfloat16), first


def per_device(queries, keys, values, grad_out, saved_state):
    heads, _, head = saved_state.shape[1:]
    blocks, devices = lax.axis_size("tm"), lax.axis_size("space")
    lanes = 2 if devices % 2 == 0 and heads % 2 == 0 else 1
    groups = devices // lanes
    far_first = range(groups - 1, 0, -1)
    scale = 1.0 / math.sqrt(queries.shape[0] * blocks * devices * head)

    parts = []
    if lanes > 1:
        _, lane = place_on_space(lanes)
        span = queries.shape[1] // lanes
        starts = (jnp.zeros_like(lane), (1 - lane) * span)
        cut = lax.dynamic_slice(
            queries, starts, (queries.shape[0], span), allow_negative_indices=False
        )
        theirs = partial_products(cut, grad_out, head, lanes, True, scale)
        parts.append(swap_lanes(theirs, lanes, groups))
        queries = after(queries, cut)
    parts.insert(0, partial_products(queries, grad_out, head, lanes, False, scale))
    share, *sends = cut_by_group(parts, lanes, groups)
    for hop in far_first:
        share = share + hop_groups(sends[hop - 1], hop, lanes, groups).astype(jnp.float32)
    own, first = suffix_sum(share, blocks)
    met = [hop_groups(own, hop, lanes, groups) for hop in far_first]

    saved = gather_groups(saved_state, [(parts[0], ()), (share, ())], lanes, groups)
    sides = [saved] + ([swap_lanes(saved, lanes, groups)] if lanes > 1 else [])

    near = [own, *met[::-1]]
    far = [swap_lanes(piece, lanes, groups) for piece in near] if lanes > 1 else []
    ready = near_grads(queries, grad_out, keys, values, sides, near)
    return far_grads(keys, values, ready, far, lanes, groups)


def solution(mesh):
    tokens = P(("tm", "space"), None)
    return jax.shard_map(
        per_device,
        mesh=mesh,
        in_specs=(tokens, tokens, tokens, tokens, P("tm", None, "space", None)),
        out_specs=(tokens, tokens, tokens),
        check_vma=False,
    )
```

```python
import functools
import math

import jax
import jax.numpy as jnp
from jax import lax
from jax.experimental import pallas as pl
from jax.experimental.pallas import tpu as pltpu
from jax.sharding import PartitionSpec as P

CONTRACT_ROWS = (((0,), (0,)), ((), ()))
CONTRACT_COLS = (((1,), (1,)), ((), ()))
VMEM_BYTES = 16 * 1024 * 1024
ANYWHERE = pl.BlockSpec(memory_space=pl.ANY)
IN_VMEM = pl.BlockSpec(memory_space=pltpu.VMEM)


def power_of_two(count):
    return count & (count - 1) == 0


def partner(group, hop, groups):
    if power_of_two(groups):
        return group ^ hop
    return (group + hop) % groups


def source(group, hop, groups):
    if power_of_two(groups):
        return group ^ hop
    return (group - hop + groups) % groups


def cost(flops, *arrays):
    moved = sum(array.size * array.dtype.itemsize for array in arrays)
    return pl.CostEstimate(flops=flops, bytes_accessed=moved, transcendentals=0)


def after(value, earlier):
    return lax.optimization_barrier((value, earlier))[0]


def place_on_space(lanes):
    index = lax.axis_index("space")
    return lax.div(index, lanes), lax.rem(index, lanes)


def swap_lanes(value, lanes, groups):
    pairs = [(g * lanes + c, g * lanes + 1 - c) for g in range(groups) for c in range(lanes)]
    return lax.ppermute(value, "space", pairs)


def hop_groups(value, hop, lanes, groups):
    pairs = [
        (g * lanes + c, partner(g, hop, groups) * lanes + c)
        for g in range(groups)
        for c in range(lanes)
    ]
    return lax.ppermute(value, "space", pairs)


def gather_groups(value, waits, lanes, groups):
    if power_of_two(groups):
        for step in range(groups.bit_length() - 1):
            start, done = waits[min(step, len(waits) - 1)]
            met = hop_groups(after(value, start), 1 << step, lanes, groups)
            value = jnp.concatenate([value, after(met, done)])
        return value
    return jnp.concatenate(
        [value] + [hop_groups(value, hop, lanes, groups) for hop in range(1, groups)]
    )


def products(scale, queries, grad_out):
    return scale * lax.dot_general(
        jnp.maximum(queries, 0),
        grad_out,
        CONTRACT_ROWS,
        preferred_element_type=jnp.float32,
    )


def partial_kernel(lanes, other, scale, q_ref, o_ref, part_ref):
    span, head = part_ref.shape
    _, lane = place_on_space(lanes)
    base = (1 - lane if other else lane) * span
    for h in range(span // head):
        rows = pl.ds(h * head, head)
        cols = pl.ds(pl.multiple_of(base + h * head, head), head)
        part_ref[rows, :] = products(
            scale, q_ref[:, rows if other else cols], o_ref[:, cols]
        ).astype(part_ref.dtype)


def partial_products(queries, grad_out, head, lanes, other, scale):
    tokens, width = grad_out.shape
    span = width // lanes
    return pl.pallas_call(
        functools.partial(partial_kernel, lanes, other, scale),
        out_shape=jax.ShapeDtypeStruct((span, head), jnp.bfloat16 if other else jnp.float32),
        in_specs=[IN_VMEM, IN_VMEM],
        out_specs=IN_VMEM,
        compiler_params=pltpu.CompilerParams(vmem_limit_bytes=VMEM_BYTES),
        cost_estimate=cost(2 * tokens * span * head, queries),
        name="partial_other" if other else "partial_own",
    )(queries, grad_out)


def cut_kernel(lanes, groups, *refs):
    parts, outs = refs[:lanes], refs[lanes:]
    group, _ = place_on_space(lanes)
    rows = outs[0].shape[0]
    for hop, out_ref in enumerate(outs):
        there = pl.ds(pl.multiple_of(partner(group, hop, groups) * rows, rows), rows)
        total = parts[0][there, :]
        for part in parts[1:]:
            total = total + part[there, :].astype(jnp.float32)
        out_ref[...] = total.astype(out_ref.dtype)


def cut_by_group(parts, lanes, groups):
    span, head = parts[0].shape
    rows = span // groups
    outs = [jax.ShapeDtypeStruct((rows, head), jnp.float32)]
    outs += [jax.ShapeDtypeStruct((rows, head), jnp.bfloat16)] * (groups - 1)
    return pl.pallas_call(
        functools.partial(cut_kernel, lanes, groups),
        out_shape=outs,
        in_specs=[IN_VMEM] * lanes,
        out_specs=[IN_VMEM] * groups,
        compiler_params=pltpu.CompilerParams(vmem_limit_bytes=VMEM_BYTES),
        cost_estimate=cost(span * head, *parts),
        name="cut_by_group",
    )(*parts)


def key_value_products(k_ref, v_ref, state, cols, dk_ref, dv_ref):
    head = state.shape[1]
    for h in range(state.shape[0] // head):
        local = pl.ds(h * head, head)
        keys, grad_state = k_ref[:, cols(h)], state[local, :]
        full = lax.dot_general(
            v_ref[:, cols(h)], grad_state, CONTRACT_COLS, preferred_element_type=jnp.float32
        )
        dk_ref[:, local] = jnp.where(keys > 0, full, 0.0).astype(dk_ref.dtype)
        dv_ref[:, local] = jnp.dot(
            jnp.maximum(keys, 0), grad_state, preferred_element_type=jnp.float32
        ).astype(dv_ref.dtype)
        yield h


def place_pieces(pieces, group, groups, state):
    for hop, piece in enumerate(pieces):
        rows = piece.shape[0]
        owner = source(group, hop, groups)
        state[pl.ds(pl.multiple_of(owner * rows, rows), rows), :] = piece[...]


def query_kernel(lanes, groups, q_ref, o_ref, *rest):
    sides, (dq_ref, saved, sems) = rest[:lanes], rest[lanes:]
    heads, head, _ = saved.shape
    rows = sides[0].shape[2]
    group, lane = place_on_space(lanes)
    copies = []
    for other, side in enumerate(sides):
        there = 1 - lane if other else lane
        for hop in range(groups):
            owner = source(group, hop, groups) * lanes + there
            dst = pl.ds(pl.multiple_of(owner * rows, rows), rows)
            if rows % 16 == 0:
                saved[:, dst, :] = side[hop]
            else:
                copies.append(
                    pltpu.make_async_copy(side.at[hop], saved.at[:, dst, :], sems.at[other, hop])
                )
    for copy in copies:
        copy.start()
    for copy in copies:
        copy.wait()
    for h in range(heads):
        cols = pl.ds(h * head, head)
        full = lax.dot_general(
            o_ref[:, cols], saved[h], CONTRACT_COLS, preferred_element_type=jnp.float32
        )
        dq_ref[:, cols] = jnp.where(q_ref[:, cols] > 0, full, 0.0).astype(dq_ref.dtype)


def query_grads(queries, grad_out, sides):
    lanes, (groups, heads, _, head) = len(sides), sides[0].shape
    return pl.pallas_call(
        functools.partial(query_kernel, lanes, groups),
        out_shape=jax.ShapeDtypeStruct(queries.shape, queries.dtype),
        in_specs=[IN_VMEM] * (2 + lanes),
        out_specs=IN_VMEM,
        scratch_shapes=[
            pltpu.VMEM((heads, head, head), sides[0].dtype),
            pltpu.SemaphoreType.DMA((lanes, groups)),
        ],
        compiler_params=pltpu.CompilerParams(vmem_limit_bytes=VMEM_BYTES),
        cost_estimate=cost(2 * queries.size * head, queries, grad_out, *sides),
        name="query_grads",
    )(queries, grad_out, *sides)


def near_kernel(lanes, groups, k_ref, v_ref, dq_ref, *rest):
    pieces, (dq_hbm, dk_ref, dv_ref, state, sems) = rest[:groups], rest[groups:]
    head = state.shape[1]
    group, lane = place_on_space(lanes)
    copies = []
    rows = dq_ref.shape[0] // sems.shape[0]
    for at in range(sems.shape[0]):
        mine = pl.ds(at * rows, rows)
        copies.append(pltpu.make_async_copy(dq_ref.at[mine, :], dq_hbm.at[mine, :], sems.at[at]))
        copies[-1].start()
    place_pieces(pieces, group, groups, state)
    base = lane * state.shape[0]
    for _ in key_value_products(
        k_ref,
        v_ref,
        state,
        lambda h: pl.ds(pl.multiple_of(base + h * head, head), head),
        dk_ref,
        dv_ref,
    ):
        pass
    for copy in copies:
        copy.wait()


def near_grads(keys, values, grad_q, pieces, lanes):
    tokens, groups, (rows, head) = keys.shape[0], len(pieces), pieces[0].shape
    span = groups * rows
    parts = math.gcd(tokens // 16, 4) if tokens % 16 == 0 else 1
    return pl.pallas_call(
        functools.partial(near_kernel, lanes, groups),
        out_shape=(
            jax.ShapeDtypeStruct(grad_q.shape, grad_q.dtype),
            jax.ShapeDtypeStruct((tokens, span), keys.dtype),
            jax.ShapeDtypeStruct((tokens, span), values.dtype),
        ),
        in_specs=[IN_VMEM] * (3 + groups),
        out_specs=(ANYWHERE, IN_VMEM, IN_VMEM),
        scratch_shapes=[
            pltpu.VMEM((span, head), pieces[0].dtype),
            pltpu.SemaphoreType.DMA((parts,)),
        ],
        compiler_params=pltpu.CompilerParams(vmem_limit_bytes=VMEM_BYTES),
        cost_estimate=cost(4 * tokens * span * head, *pieces),
        name="near_grads",
    )(keys, values, grad_q, *pieces)


def far_kernel(lanes, groups, k_ref, v_ref, *rest):
    near, pieces = rest[:2], rest[2:-6]
    dk_hbm, dv_hbm, state, dk_buf, dv_buf, sems = rest[-6:]
    span, head = state.shape
    group, lane = place_on_space(lanes)
    outs = (dk_hbm, dv_hbm)
    copies = []
    for at in range(2):
        mine = pl.ds(pl.multiple_of(lane * span, head), span)
        copies.append(pltpu.make_async_copy(near[at], outs[at].at[:, mine], sems.at[at, 0]))
        copies[-1].start()
    if pieces:
        place_pieces(pieces, group, groups, state)
        base = (1 - lane) * span
        part = span // head // (sems.shape[1] - 1)
        for h in key_value_products(
            k_ref,
            v_ref,
            state,
            lambda h: pl.ds(pl.multiple_of(base + h * head, head), head),
            dk_buf,
            dv_buf,
        ):
            if (h + 1) % part == 0:
                src = pl.ds((h + 1 - part) * head, part * head)
                dst = pl.ds(pl.multiple_of(base + (h + 1 - part) * head, head), part * head)
                for at, buf in enumerate((dk_buf, dv_buf)):
                    copies.append(
                        pltpu.make_async_copy(
                            buf.at[:, src], outs[at].at[:, dst], sems.at[at, 1 + h // part]
                        )
                    )
                    copies[-1].start()
    for copy in copies:
        copy.wait()


def far_grads(keys, values, near, pieces, lanes, groups):
    tokens, span = near[0].shape
    head = pieces[0].shape[1] if pieces else span
    return pl.pallas_call(
        functools.partial(far_kernel, lanes, groups),
        out_shape=(
            jax.ShapeDtypeStruct(keys.shape, keys.dtype),
            jax.ShapeDtypeStruct(values.shape, values.dtype),
        ),
        in_specs=[IN_VMEM] * (4 + len(pieces)),
        out_specs=(ANYWHERE, ANYWHERE),
        scratch_shapes=[
            pltpu.VMEM((span, head), keys.dtype),
            pltpu.VMEM((tokens, span), keys.dtype),
            pltpu.VMEM((tokens, span), values.dtype),
            pltpu.SemaphoreType.DMA((2, 1 + math.gcd(span // head, 5))),
        ],
        compiler_params=pltpu.CompilerParams(vmem_limit_bytes=VMEM_BYTES),
        cost_estimate=cost(4 * tokens * span * head, *near),
        name="far_grads",
    )(keys, values, *near, *pieces)


def suffix_sum(share, blocks):
    block = lax.axis_index("tm")
    suffix = total = first = share
    if power_of_two(blocks):
        hop = 1
        while hop < blocks:
            pairs = [(b, b ^ hop) for b in range(blocks)]
            met = lax.ppermute(total.astype(jnp.bfloat16), "tm", pairs).astype(jnp.float32)
            suffix = suffix + jnp.where(block & hop == 0, met, 0.0)
            total = total + met
            first = total if hop == 1 else first
            hop *= 2
    else:
        for hop in range(1, blocks):
            pairs = [(b, b - hop) for b in range(hop, blocks)]
            later = lax.ppermute(share.astype(jnp.bfloat16), "tm", pairs)
            suffix = suffix + later.astype(jnp.float32)
    return suffix.astype(jnp.bfloat16), first


def per_device(queries, keys, values, grad_out, saved_state):
    heads, _, head = saved_state.shape[1:]
    blocks, devices = lax.axis_size("tm"), lax.axis_size("space")
    lanes = 2 if devices % 2 == 0 and heads % 2 == 0 else 1
    groups = devices // lanes
    far_first = range(groups - 1, 0, -1)
    scale = 1.0 / math.sqrt(queries.shape[0] * blocks * devices * head)

    parts = []
    if lanes > 1:
        _, lane = place_on_space(lanes)
        span = queries.shape[1] // lanes
        starts = (jnp.zeros_like(lane), (1 - lane) * span)
        cut = lax.dynamic_slice(
            queries, starts, (queries.shape[0], span), allow_negative_indices=False
        )
        theirs = partial_products(cut, grad_out, head, lanes, True, scale)
        parts.append(swap_lanes(theirs, lanes, groups))
        queries = after(queries, cut)
    parts.insert(0, partial_products(queries, grad_out, head, lanes, False, scale))
    share, *sends = cut_by_group(parts, lanes, groups)
    for hop in far_first:
        share = share + hop_groups(sends[hop - 1], hop, lanes, groups).astype(jnp.float32)
    own, first = suffix_sum(share, blocks)
    met = [hop_groups(own, hop, lanes, groups) for hop in far_first]

    saved = gather_groups(saved_state, [(parts[0], ()), (share, ())], lanes, groups)
    sides = [saved] + ([swap_lanes(saved, lanes, groups)] if lanes > 1 else [])

    grad_q = query_grads(queries, grad_out, sides)
    near = [own, *met[::-1]]
    if met:
        near[1] = after(near[1], grad_q)
    far = [swap_lanes(piece, lanes, groups) for piece in near] if lanes > 1 else []
    grad_q, *halves = near_grads(keys, values, grad_q, near, lanes)
    return grad_q, *far_grads(keys, values, halves, far, lanes, groups)


def solution(mesh):
    tokens = P(("tm", "space"), None)
    return jax.shard_map(
        per_device,
        mesh=mesh,
        in_specs=(tokens, tokens, tokens, tokens, P("tm", None, "space", None)),
        out_specs=(tokens, tokens, tokens),
        check_vma=False,
    )
```

```python
import functools
import math

import jax
import jax.numpy as jnp
from jax import lax
from jax.experimental import pallas as pl
from jax.experimental.pallas import tpu as pltpu
from jax.sharding import PartitionSpec as P

CONTRACT_ROWS = (((0,), (0,)), ((), ()))
CONTRACT_COLS = (((1,), (1,)), ((), ()))
VMEM_BYTES = 16 * 1024 * 1024
ANYWHERE = pl.BlockSpec(memory_space=pl.ANY)
IN_VMEM = pl.BlockSpec(memory_space=pltpu.VMEM)


def power_of_two(count):
    return count & (count - 1) == 0


def partner(group, hop, groups):
    if power_of_two(groups):
        return group ^ hop
    return (group + hop) % groups


def source(group, hop, groups):
    if power_of_two(groups):
        return group ^ hop
    return (group - hop + groups) % groups


def cost(flops, *arrays):
    moved = sum(array.size * array.dtype.itemsize for array in arrays)
    return pl.CostEstimate(flops=flops, bytes_accessed=moved, transcendentals=0)


def after(value, earlier):
    return lax.optimization_barrier((value, earlier))[0]


def place_on_space(lanes):
    index = lax.axis_index("space")
    return lax.div(index, lanes), lax.rem(index, lanes)


def swap_lanes(value, lanes, groups):
    pairs = [(g * lanes + c, g * lanes + 1 - c) for g in range(groups) for c in range(lanes)]
    return lax.ppermute(value, "space", pairs)


def hop_groups(value, hop, lanes, groups):
    pairs = [
        (g * lanes + c, partner(g, hop, groups) * lanes + c)
        for g in range(groups)
        for c in range(lanes)
    ]
    return lax.ppermute(value, "space", pairs)


def gather_groups(value, waits, lanes, groups):
    if power_of_two(groups):
        for step in range(groups.bit_length() - 1):
            start, done = waits[min(step, len(waits) - 1)]
            met = hop_groups(after(value, start), 1 << step, lanes, groups)
            value = jnp.concatenate([value, after(met, done)])
        return value
    return jnp.concatenate(
        [value] + [hop_groups(value, hop, lanes, groups) for hop in range(1, groups)]
    )


def products(scale, queries, grad_out):
    return scale * lax.dot_general(
        jnp.maximum(queries, 0),
        grad_out,
        CONTRACT_ROWS,
        preferred_element_type=jnp.float32,
    )


def partial_kernel(lanes, other, scale, q_ref, o_ref, part_ref):
    span, head = part_ref.shape
    _, lane = place_on_space(lanes)
    base = (1 - lane if other else lane) * span
    for h in range(span // head):
        rows = pl.ds(h * head, head)
        cols = pl.ds(pl.multiple_of(base + h * head, head), head)
        part_ref[rows, :] = products(
            scale, q_ref[:, rows if other else cols], o_ref[:, cols]
        ).astype(part_ref.dtype)


def partial_products(queries, grad_out, head, lanes, other, scale):
    tokens, width = grad_out.shape
    span = width // lanes
    return pl.pallas_call(
        functools.partial(partial_kernel, lanes, other, scale),
        out_shape=jax.ShapeDtypeStruct((span, head), jnp.bfloat16 if other else jnp.float32),
        in_specs=[IN_VMEM, IN_VMEM],
        out_specs=IN_VMEM,
        compiler_params=pltpu.CompilerParams(vmem_limit_bytes=VMEM_BYTES),
        cost_estimate=cost(2 * tokens * span * head, queries),
        name="partial_other" if other else "partial_own",
    )(queries, grad_out)


def cut_kernel(lanes, groups, *refs):
    parts, outs = refs[:lanes], refs[lanes:]
    group, _ = place_on_space(lanes)
    rows = outs[0].shape[0]
    for hop, out_ref in enumerate(outs):
        there = pl.ds(pl.multiple_of(partner(group, hop, groups) * rows, rows), rows)
        total = parts[0][there, :]
        for part in parts[1:]:
            total = total + part[there, :].astype(jnp.float32)
        out_ref[...] = total.astype(out_ref.dtype)


def cut_by_group(parts, lanes, groups):
    span, head = parts[0].shape
    rows = span // groups
    outs = [jax.ShapeDtypeStruct((rows, head), jnp.float32)]
    outs += [jax.ShapeDtypeStruct((rows, head), jnp.bfloat16)] * (groups - 1)
    return pl.pallas_call(
        functools.partial(cut_kernel, lanes, groups),
        out_shape=outs,
        in_specs=[IN_VMEM] * lanes,
        out_specs=[IN_VMEM] * groups,
        compiler_params=pltpu.CompilerParams(vmem_limit_bytes=VMEM_BYTES),
        cost_estimate=cost(span * head, *parts),
        name="cut_by_group",
    )(*parts)


def key_value_products(k_ref, v_ref, state, cols, dk_ref, dv_ref):
    head = state.shape[1]
    for h in range(state.shape[0] // head):
        local = pl.ds(h * head, head)
        keys, grad_state = k_ref[:, cols(h)], state[local, :]
        full = lax.dot_general(
            v_ref[:, cols(h)], grad_state, CONTRACT_COLS, preferred_element_type=jnp.float32
        )
        dk_ref[:, local] = jnp.where(keys > 0, full, 0.0).astype(dk_ref.dtype)
        dv_ref[:, local] = jnp.dot(
            jnp.maximum(keys, 0), grad_state, preferred_element_type=jnp.float32
        ).astype(dv_ref.dtype)
        yield h


def place_pieces(pieces, group, groups, state):
    for hop, piece in enumerate(pieces):
        rows = piece.shape[0]
        owner = source(group, hop, groups)
        state[pl.ds(pl.multiple_of(owner * rows, rows), rows), :] = piece[...]


def near_kernel(lanes, groups, q_ref, o_ref, k_ref, v_ref, *rest):
    sides, pieces = rest[:lanes], rest[lanes : lanes + groups]
    dq_ref, dk_ref, dv_ref, saved, state, sems = rest[lanes + groups :]
    heads, head, _ = saved.shape
    rows = sides[0].shape[2]
    group, lane = place_on_space(lanes)
    copies = []
    for other, side in enumerate(sides):
        there = 1 - lane if other else lane
        for hop in range(groups):
            owner = source(group, hop, groups) * lanes + there
            dst = pl.ds(pl.multiple_of(owner * rows, rows), rows)
            if rows % 16 == 0:
                saved[:, dst, :] = side[hop]
            else:
                copies.append(
                    pltpu.make_async_copy(side.at[hop], saved.at[:, dst, :], sems.at[other, hop])
                )
    for copy in copies:
        copy.start()
    for copy in copies:
        copy.wait()
    for h in range(heads):
        cols = pl.ds(h * head, head)
        full = lax.dot_general(
            o_ref[:, cols], saved[h], CONTRACT_COLS, preferred_element_type=jnp.float32
        )
        dq_ref[:, cols] = jnp.where(q_ref[:, cols] > 0, full, 0.0).astype(dq_ref.dtype)
    place_pieces(pieces, group, groups, state)
    base = lane * state.shape[0]
    for _ in key_value_products(
        k_ref,
        v_ref,
        state,
        lambda h: pl.ds(pl.multiple_of(base + h * head, head), head),
        dk_ref,
        dv_ref,
    ):
        pass


def near_grads(queries, grad_out, keys, values, sides, pieces):
    lanes, groups = len(sides), len(pieces)
    tokens, heads, (rows, head) = queries.shape[0], sides[0].shape[1], pieces[0].shape
    span = groups * rows
    return pl.pallas_call(
        functools.partial(near_kernel, lanes, groups),
        out_shape=(
            jax.ShapeDtypeStruct(queries.shape, queries.dtype),
            jax.ShapeDtypeStruct((tokens, span), keys.dtype),
            jax.ShapeDtypeStruct((tokens, span), values.dtype),
        ),
        in_specs=[IN_VMEM] * (4 + lanes + groups),
        out_specs=(IN_VMEM, IN_VMEM, IN_VMEM),
        scratch_shapes=[
            pltpu.VMEM((heads, head, head), sides[0].dtype),
            pltpu.VMEM((span, head), pieces[0].dtype),
            pltpu.SemaphoreType.DMA((lanes, groups)),
        ],
        compiler_params=pltpu.CompilerParams(vmem_limit_bytes=VMEM_BYTES),
        cost_estimate=cost(4 * queries.size * head, queries, queries, grad_out, *sides),
        name="near_grads",
    )(queries, grad_out, keys, values, *sides, *pieces)


def far_kernel(lanes, groups, k_ref, v_ref, *rest):
    dq_ref, near, pieces = rest[0], rest[1:3], rest[3:-8]
    dq_hbm, *outs = rest[-8:-5]
    state, dk_buf, dv_buf, sems, dq_sem = rest[-5:]
    span, head = state.shape
    group, lane = place_on_space(lanes)
    copies = [pltpu.make_async_copy(dq_ref, dq_hbm, dq_sem)]
    copies[0].start()
    for at in range(2):
        mine = pl.ds(pl.multiple_of(lane * span, head), span)
        copies.append(pltpu.make_async_copy(near[at], outs[at].at[:, mine], sems.at[at, 0]))
        copies[-1].start()
    if pieces:
        place_pieces(pieces, group, groups, state)
        base = (1 - lane) * span
        part = span // head // (sems.shape[1] - 1)
        for h in key_value_products(
            k_ref,
            v_ref,
            state,
            lambda h: pl.ds(pl.multiple_of(base + h * head, head), head),
            dk_buf,
            dv_buf,
        ):
            if (h + 1) % part == 0:
                src = pl.ds((h + 1 - part) * head, part * head)
                dst = pl.ds(pl.multiple_of(base + (h + 1 - part) * head, head), part * head)
                for at, buf in enumerate((dk_buf, dv_buf)):
                    copies.append(
                        pltpu.make_async_copy(
                            buf.at[:, src], outs[at].at[:, dst], sems.at[at, 1 + h // part]
                        )
                    )
                    copies[-1].start()
    for copy in copies:
        copy.wait()


def far_grads(keys, values, near, pieces, lanes, groups):
    tokens, span = near[1].shape
    head = pieces[0].shape[1] if pieces else span
    return pl.pallas_call(
        functools.partial(far_kernel, lanes, groups),
        out_shape=(
            jax.ShapeDtypeStruct(near[0].shape, near[0].dtype),
            jax.ShapeDtypeStruct(keys.shape, keys.dtype),
            jax.ShapeDtypeStruct(values.shape, values.dtype),
        ),
        in_specs=[IN_VMEM] * (5 + len(pieces)),
        out_specs=(ANYWHERE,) * 3,
        scratch_shapes=[
            pltpu.VMEM((span, head), keys.dtype),
            pltpu.VMEM((tokens, span), keys.dtype),
            pltpu.VMEM((tokens, span), values.dtype),
            pltpu.SemaphoreType.DMA((2, 1 + math.gcd(span // head, 5))),
            pltpu.SemaphoreType.DMA,
        ],
        compiler_params=pltpu.CompilerParams(vmem_limit_bytes=VMEM_BYTES),
        cost_estimate=cost(4 * tokens * span * head, *near),
        name="far_grads",
    )(keys, values, *near, *pieces)


def suffix_sum(share, blocks):
    block = lax.axis_index("tm")
    suffix = total = first = share
    if power_of_two(blocks):
        hop = 1
        while hop < blocks:
            pairs = [(b, b ^ hop) for b in range(blocks)]
            met = lax.ppermute(total.astype(jnp.bfloat16), "tm", pairs).astype(jnp.float32)
            suffix = suffix + jnp.where(block & hop == 0, met, 0.0)
            total = total + met
            first = total if hop == 1 else first
            hop *= 2
    else:
        for hop in range(1, blocks):
            pairs = [(b, b - hop) for b in range(hop, blocks)]
            later = lax.ppermute(share.astype(jnp.bfloat16), "tm", pairs)
            suffix = suffix + later.astype(jnp.float32)
    return suffix.astype(jnp.bfloat16), first


def per_device(queries, keys, values, grad_out, saved_state):
    heads, _, head = saved_state.shape[1:]
    blocks, devices = lax.axis_size("tm"), lax.axis_size("space")
    lanes = 2 if devices % 2 == 0 and heads % 2 == 0 else 1
    groups = devices // lanes
    far_first = range(groups - 1, 0, -1)
    scale = 1.0 / math.sqrt(queries.shape[0] * blocks * devices * head)

    parts = []
    if lanes > 1:
        _, lane = place_on_space(lanes)
        span = queries.shape[1] // lanes
        starts = (jnp.zeros_like(lane), (1 - lane) * span)
        cut = lax.dynamic_slice(
            queries, starts, (queries.shape[0], span), allow_negative_indices=False
        )
        theirs = partial_products(cut, grad_out, head, lanes, True, scale)
        parts.append(swap_lanes(theirs, lanes, groups))
        queries = after(queries, cut)
    parts.insert(0, partial_products(queries, grad_out, head, lanes, False, scale))
    share, *sends = cut_by_group(parts, lanes, groups)
    for hop in far_first:
        share = share + hop_groups(sends[hop - 1], hop, lanes, groups).astype(jnp.float32)
    own, first = suffix_sum(share, blocks)
    met = [hop_groups(own, hop, lanes, groups) for hop in far_first]

    saved = gather_groups(saved_state, [((), ()), (share, ())], lanes, groups)
    sides = [saved] + ([swap_lanes(saved, lanes, groups)] if lanes > 1 else [])

    near = [own, *met[::-1]]
    far = [swap_lanes(piece, lanes, groups) for piece in near] if lanes > 1 else []
    ready = near_grads(queries, grad_out, keys, values, sides, near)
    return far_grads(keys, values, ready, far, lanes, groups)


def solution(mesh):
    tokens = P(("tm", "space"), None)
    return jax.shard_map(
        per_device,
        mesh=mesh,
        in_specs=(tokens, tokens, tokens, tokens, P("tm", None, "space", None)),
        out_specs=(tokens, tokens, tokens),
        check_vma=False,
    )
```

```python
import functools
import math

import jax
import jax.numpy as jnp
from jax import lax
from jax.experimental import pallas as pl
from jax.experimental.pallas import tpu as pltpu
from jax.sharding import PartitionSpec as P

CONTRACT_ROWS = (((0,), (0,)), ((), ()))
CONTRACT_COLS = (((1,), (1,)), ((), ()))
VMEM_BYTES = 16 * 1024 * 1024
ANYWHERE = pl.BlockSpec(memory_space=pl.ANY)
IN_VMEM = pl.BlockSpec(memory_space=pltpu.VMEM)


def power_of_two(count):
    return count & (count - 1) == 0


def partner(group, hop, groups):
    if power_of_two(groups):
        return group ^ hop
    return (group + hop) % groups


def source(group, hop, groups):
    if power_of_two(groups):
        return group ^ hop
    return (group - hop + groups) % groups


def cost(flops, *arrays):
    moved = sum(array.size * array.dtype.itemsize for array in arrays)
    return pl.CostEstimate(flops=flops, bytes_accessed=moved, transcendentals=0)


def after(value, earlier):
    return lax.optimization_barrier((value, earlier))[0]


def place_on_space(lanes):
    index = lax.axis_index("space")
    return lax.div(index, lanes), lax.rem(index, lanes)


def swap_lanes(value, lanes, groups):
    pairs = [(g * lanes + c, g * lanes + 1 - c) for g in range(groups) for c in range(lanes)]
    return lax.ppermute(value, "space", pairs)


def hop_groups(value, hop, lanes, groups):
    pairs = [
        (g * lanes + c, partner(g, hop, groups) * lanes + c)
        for g in range(groups)
        for c in range(lanes)
    ]
    return lax.ppermute(value, "space", pairs)


def gather_groups(value, waits, lanes, groups):
    if power_of_two(groups):
        for step in range(groups.bit_length() - 1):
            start, done = waits[min(step, len(waits) - 1)]
            met = hop_groups(after(value, start), 1 << step, lanes, groups)
            value = jnp.concatenate([value, after(met, done)])
        return value
    return jnp.concatenate(
        [value] + [hop_groups(value, hop, lanes, groups) for hop in range(1, groups)]
    )


def products(scale, queries, grad_out):
    return scale * lax.dot_general(
        jnp.maximum(queries, 0),
        grad_out,
        CONTRACT_ROWS,
        preferred_element_type=jnp.float32,
    )


def partial_kernel(lanes, other, scale, q_ref, o_ref, part_ref):
    span, head = part_ref.shape
    _, lane = place_on_space(lanes)
    base = (1 - lane if other else lane) * span
    for h in range(span // head):
        rows = pl.ds(h * head, head)
        cols = pl.ds(pl.multiple_of(base + h * head, head), head)
        part_ref[rows, :] = products(
            scale, q_ref[:, rows if other else cols], o_ref[:, cols]
        ).astype(part_ref.dtype)


def partial_products(queries, grad_out, head, lanes, other, scale):
    tokens, width = grad_out.shape
    span = width // lanes
    return pl.pallas_call(
        functools.partial(partial_kernel, lanes, other, scale),
        out_shape=jax.ShapeDtypeStruct((span, head), jnp.bfloat16 if other else jnp.float32),
        in_specs=[IN_VMEM, IN_VMEM],
        out_specs=IN_VMEM,
        compiler_params=pltpu.CompilerParams(vmem_limit_bytes=VMEM_BYTES),
        cost_estimate=cost(2 * tokens * span * head, queries),
        name="partial_other" if other else "partial_own",
    )(queries, grad_out)


def cut_kernel(lanes, groups, *refs):
    parts, outs = refs[:lanes], refs[lanes:]
    group, _ = place_on_space(lanes)
    rows = outs[0].shape[0]
    for hop, out_ref in enumerate(outs):
        there = pl.ds(pl.multiple_of(partner(group, hop, groups) * rows, rows), rows)
        total = parts[0][there, :]
        for part in parts[1:]:
            total = total + part[there, :].astype(jnp.float32)
        out_ref[...] = total.astype(out_ref.dtype)


def cut_by_group(parts, lanes, groups):
    span, head = parts[0].shape
    rows = span // groups
    outs = [jax.ShapeDtypeStruct((rows, head), jnp.float32)]
    outs += [jax.ShapeDtypeStruct((rows, head), jnp.bfloat16)] * (groups - 1)
    return pl.pallas_call(
        functools.partial(cut_kernel, lanes, groups),
        out_shape=outs,
        in_specs=[IN_VMEM] * lanes,
        out_specs=[IN_VMEM] * groups,
        compiler_params=pltpu.CompilerParams(vmem_limit_bytes=VMEM_BYTES),
        cost_estimate=cost(span * head, *parts),
        name="cut_by_group",
    )(*parts)


def key_value_products(k_ref, v_ref, state, cols, dk_ref, dv_ref):
    head = state.shape[1]
    for h in range(state.shape[0] // head):
        local = pl.ds(h * head, head)
        keys, grad_state = k_ref[:, cols(h)], state[local, :]
        full = lax.dot_general(
            v_ref[:, cols(h)], grad_state, CONTRACT_COLS, preferred_element_type=jnp.float32
        )
        dk_ref[:, local] = jnp.where(keys > 0, full, 0.0).astype(dk_ref.dtype)
        dv_ref[:, local] = jnp.dot(
            jnp.maximum(keys, 0), grad_state, preferred_element_type=jnp.float32
        ).astype(dv_ref.dtype)
        yield h


def place_pieces(pieces, group, groups, state):
    for hop, piece in enumerate(pieces):
        rows = piece.shape[0]
        owner = source(group, hop, groups)
        state[pl.ds(pl.multiple_of(owner * rows, rows), rows), :] = piece[...]


def near_kernel(lanes, groups, q_ref, o_ref, k_ref, v_ref, *rest):
    sides, pieces = rest[:lanes], rest[lanes : lanes + groups]
    dq_hbm, dq_ref, dk_ref, dv_ref, saved, state, dq_buf, sems, dq_sems = rest[lanes + groups :]
    heads, head, _ = saved.shape
    rows = sides[0].shape[2]
    group, lane = place_on_space(lanes)
    copies = []
    for other, side in enumerate(sides):
        there = 1 - lane if other else lane
        for hop in range(groups):
            owner = source(group, hop, groups) * lanes + there
            dst = pl.ds(pl.multiple_of(owner * rows, rows), rows)
            if rows % 16 == 0:
                saved[:, dst, :] = side[hop]
            else:
                copies.append(
                    pltpu.make_async_copy(side.at[hop], saved.at[:, dst, :], sems.at[other, hop])
                )
    for copy in copies:
        copy.start()
    for copy in copies:
        copy.wait()
    early = dq_buf.shape[1] // head
    part = early // dq_sems.shape[0]
    copies = []
    for h in range(heads):
        cols = pl.ds(h * head, head)
        full = lax.dot_general(
            o_ref[:, cols], saved[h], CONTRACT_COLS, preferred_element_type=jnp.float32
        )
        value = jnp.where(q_ref[:, cols] > 0, full, 0.0).astype(dq_ref.dtype)
        if h >= early:
            dq_ref[:, pl.ds((h - early) * head, head)] = value
            continue
        dq_buf[:, cols] = value
        if (h + 1) % part == 0:
            cols = pl.ds((h + 1 - part) * head, part * head)
            copies.append(
                pltpu.make_async_copy(
                    dq_buf.at[:, cols], dq_hbm.at[:, cols], dq_sems.at[h // part]
                )
            )
            copies[-1].start()
    place_pieces(pieces, group, groups, state)
    base = lane * state.shape[0]
    for _ in key_value_products(
        k_ref,
        v_ref,
        state,
        lambda h: pl.ds(pl.multiple_of(base + h * head, head), head),
        dk_ref,
        dv_ref,
    ):
        pass
    for copy in copies:
        copy.wait()


def near_grads(queries, grad_out, keys, values, sides, pieces):
    lanes, groups = len(sides), len(pieces)
    tokens, heads, (rows, head) = queries.shape[0], sides[0].shape[1], pieces[0].shape
    span = groups * rows
    early = max(heads // 2, 1)
    late = heads - early
    return pl.pallas_call(
        functools.partial(near_kernel, lanes, groups),
        out_shape=(
            jax.ShapeDtypeStruct(queries.shape, queries.dtype),
            jax.ShapeDtypeStruct((tokens, late * head), queries.dtype),
            jax.ShapeDtypeStruct((tokens, span), keys.dtype),
            jax.ShapeDtypeStruct((tokens, span), values.dtype),
        ),
        in_specs=[IN_VMEM] * (4 + lanes + groups),
        out_specs=(ANYWHERE, IN_VMEM, IN_VMEM, IN_VMEM),
        scratch_shapes=[
            pltpu.VMEM((heads, head, head), sides[0].dtype),
            pltpu.VMEM((span, head), pieces[0].dtype),
            pltpu.VMEM((tokens, early * head), queries.dtype),
            pltpu.SemaphoreType.DMA((lanes, groups)),
            pltpu.SemaphoreType.DMA((math.gcd(early, 5),)),
        ],
        compiler_params=pltpu.CompilerParams(vmem_limit_bytes=VMEM_BYTES),
        cost_estimate=cost(4 * queries.size * head, queries, queries, grad_out, *sides),
        name="near_grads",
    )(queries, grad_out, keys, values, *sides, *pieces)


def far_kernel(lanes, groups, k_ref, v_ref, *rest):
    dq_ref, near, pieces = rest[1], rest[2:4], rest[4:-8]
    dq_hbm, *outs = rest[-8:-5]
    state, dk_buf, dv_buf, sems, dq_sem = rest[-5:]
    span, head = state.shape
    group, lane = place_on_space(lanes)
    late = pl.ds(dq_hbm.shape[1] - dq_ref.shape[1], dq_ref.shape[1])
    copies = [pltpu.make_async_copy(dq_ref, dq_hbm.at[:, late], dq_sem)]
    copies[0].start()
    for at in range(2):
        mine = pl.ds(pl.multiple_of(lane * span, head), span)
        copies.append(pltpu.make_async_copy(near[at], outs[at].at[:, mine], sems.at[at, 0]))
        copies[-1].start()
    if pieces:
        place_pieces(pieces, group, groups, state)
        base = (1 - lane) * span
        part = span // head // (sems.shape[1] - 1)
        for h in key_value_products(
            k_ref,
            v_ref,
            state,
            lambda h: pl.ds(pl.multiple_of(base + h * head, head), head),
            dk_buf,
            dv_buf,
        ):
            if (h + 1) % part == 0:
                src = pl.ds((h + 1 - part) * head, part * head)
                dst = pl.ds(pl.multiple_of(base + (h + 1 - part) * head, head), part * head)
                for at, buf in enumerate((dk_buf, dv_buf)):
                    copies.append(
                        pltpu.make_async_copy(
                            buf.at[:, src], outs[at].at[:, dst], sems.at[at, 1 + h // part]
                        )
                    )
                    copies[-1].start()
    for copy in copies:
        copy.wait()


def far_grads(keys, values, near, pieces, lanes, groups):
    tokens, span = near[2].shape
    head = pieces[0].shape[1] if pieces else span
    return pl.pallas_call(
        functools.partial(far_kernel, lanes, groups),
        out_shape=(
            jax.ShapeDtypeStruct(near[0].shape, near[0].dtype),
            jax.ShapeDtypeStruct(keys.shape, keys.dtype),
            jax.ShapeDtypeStruct(values.shape, values.dtype),
        ),
        in_specs=[IN_VMEM, IN_VMEM, ANYWHERE] + [IN_VMEM] * (3 + len(pieces)),
        input_output_aliases={2: 0},
        out_specs=(ANYWHERE,) * 3,
        scratch_shapes=[
            pltpu.VMEM((span, head), keys.dtype),
            pltpu.VMEM((tokens, span), keys.dtype),
            pltpu.VMEM((tokens, span), values.dtype),
            pltpu.SemaphoreType.DMA((2, 1 + math.gcd(span // head, 5))),
            pltpu.SemaphoreType.DMA,
        ],
        compiler_params=pltpu.CompilerParams(vmem_limit_bytes=VMEM_BYTES),
        cost_estimate=cost(4 * tokens * span * head, *near),
        name="far_grads",
    )(keys, values, *near, *pieces)


def suffix_sum(share, blocks):
    block = lax.axis_index("tm")
    suffix = total = first = share
    if power_of_two(blocks):
        hop = 1
        while hop < blocks:
            pairs = [(b, b ^ hop) for b in range(blocks)]
            met = lax.ppermute(total.astype(jnp.bfloat16), "tm", pairs).astype(jnp.float32)
            suffix = suffix + jnp.where(block & hop == 0, met, 0.0)
            total = total + met
            first = total if hop == 1 else first
            hop *= 2
    else:
        for hop in range(1, blocks):
            pairs = [(b, b - hop) for b in range(hop, blocks)]
            later = lax.ppermute(share.astype(jnp.bfloat16), "tm", pairs)
            suffix = suffix + later.astype(jnp.float32)
    return suffix.astype(jnp.bfloat16), first


def per_device(queries, keys, values, grad_out, saved_state):
    heads, _, head = saved_state.shape[1:]
    blocks, devices = lax.axis_size("tm"), lax.axis_size("space")
    lanes = 2 if devices % 2 == 0 and heads % 2 == 0 else 1
    groups = devices // lanes
    far_first = range(groups - 1, 0, -1)
    scale = 1.0 / math.sqrt(queries.shape[0] * blocks * devices * head)

    parts = []
    if lanes > 1:
        _, lane = place_on_space(lanes)
        span = queries.shape[1] // lanes
        starts = (jnp.zeros_like(lane), (1 - lane) * span)
        cut = lax.dynamic_slice(
            queries, starts, (queries.shape[0], span), allow_negative_indices=False
        )
        theirs = partial_products(cut, grad_out, head, lanes, True, scale)
        parts.append(swap_lanes(theirs, lanes, groups))
        queries = after(queries, cut)
    parts.insert(0, partial_products(queries, grad_out, head, lanes, False, scale))
    share, *sends = cut_by_group(parts, lanes, groups)
    for hop in far_first:
        share = share + hop_groups(sends[hop - 1], hop, lanes, groups).astype(jnp.float32)
    own, first = suffix_sum(share, blocks)
    met = [hop_groups(own, hop, lanes, groups) for hop in far_first]

    saved = gather_groups(saved_state, [((), ()), (share, ())], lanes, groups)
    sides = [saved] + ([swap_lanes(saved, lanes, groups)] if lanes > 1 else [])

    near = [own, *met[::-1]]
    far = [swap_lanes(piece, lanes, groups) for piece in near] if lanes > 1 else []
    ready = near_grads(queries, grad_out, keys, values, sides, near)
    return far_grads(keys, values, ready, far, lanes, groups)


def solution(mesh):
    tokens = P(("tm", "space"), None)
    return jax.shard_map(
        per_device,
        mesh=mesh,
        in_specs=(tokens, tokens, tokens, tokens, P("tm", None, "space", None)),
        out_specs=(tokens, tokens, tokens),
        check_vma=False,
    )
```

```python
import functools
import math

import jax
import jax.numpy as jnp
from jax import lax
from jax.experimental import pallas as pl
from jax.experimental.pallas import tpu as pltpu
from jax.sharding import PartitionSpec as P

CONTRACT_ROWS = (((0,), (0,)), ((), ()))
CONTRACT_COLS = (((1,), (1,)), ((), ()))
VMEM_BYTES = 16 * 1024 * 1024
ANYWHERE = pl.BlockSpec(memory_space=pl.ANY)
IN_VMEM = pl.BlockSpec(memory_space=pltpu.VMEM)


def power_of_two(count):
    return count & (count - 1) == 0


def partner(group, hop, groups):
    if power_of_two(groups):
        return group ^ hop
    return (group + hop) % groups


def source(group, hop, groups):
    if power_of_two(groups):
        return group ^ hop
    return (group - hop + groups) % groups


def cost(flops, *arrays):
    moved = sum(array.size * array.dtype.itemsize for array in arrays)
    return pl.CostEstimate(flops=flops, bytes_accessed=moved, transcendentals=0)


def after(value, earlier):
    return lax.optimization_barrier((value, earlier))[0]


def place_on_space(lanes):
    index = lax.axis_index("space")
    return lax.div(index, lanes), lax.rem(index, lanes)


def swap_lanes(value, lanes, groups):
    pairs = [(g * lanes + c, g * lanes + 1 - c) for g in range(groups) for c in range(lanes)]
    return lax.ppermute(value, "space", pairs)


def hop_groups(value, hop, lanes, groups):
    pairs = [
        (g * lanes + c, partner(g, hop, groups) * lanes + c)
        for g in range(groups)
        for c in range(lanes)
    ]
    return lax.ppermute(value, "space", pairs)


def gather_groups(value, waits, lanes, groups):
    if power_of_two(groups):
        for step in range(groups.bit_length() - 1):
            start, done = waits[min(step, len(waits) - 1)]
            met = hop_groups(after(value, start), 1 << step, lanes, groups)
            value = jnp.concatenate([value, after(met, done)])
        return value
    return jnp.concatenate(
        [value] + [hop_groups(value, hop, lanes, groups) for hop in range(1, groups)]
    )


def products(scale, queries, grad_out):
    return scale * lax.dot_general(
        jnp.maximum(queries, 0),
        grad_out,
        CONTRACT_ROWS,
        preferred_element_type=jnp.float32,
    )


def partial_kernel(lanes, other, scale, q_ref, o_ref, part_ref):
    span, head = part_ref.shape
    _, lane = place_on_space(lanes)
    base = (1 - lane if other else lane) * span
    for h in range(span // head):
        rows = pl.ds(h * head, head)
        cols = pl.ds(pl.multiple_of(base + h * head, head), head)
        part_ref[rows, :] = products(
            scale, q_ref[:, rows if other else cols], o_ref[:, cols]
        ).astype(part_ref.dtype)


def partial_products(queries, grad_out, head, lanes, other, scale):
    tokens, width = grad_out.shape
    span = width // lanes
    return pl.pallas_call(
        functools.partial(partial_kernel, lanes, other, scale),
        out_shape=jax.ShapeDtypeStruct((span, head), jnp.bfloat16 if other else jnp.float32),
        in_specs=[IN_VMEM, IN_VMEM],
        out_specs=IN_VMEM,
        compiler_params=pltpu.CompilerParams(vmem_limit_bytes=VMEM_BYTES),
        cost_estimate=cost(2 * tokens * span * head, queries),
        name="partial_other" if other else "partial_own",
    )(queries, grad_out)


def cut_kernel(lanes, groups, *refs):
    parts, outs = refs[:lanes], refs[lanes:]
    group, _ = place_on_space(lanes)
    rows = outs[0].shape[0]
    for hop, out_ref in enumerate(outs):
        there = pl.ds(pl.multiple_of(partner(group, hop, groups) * rows, rows), rows)
        total = parts[0][there, :]
        for part in parts[1:]:
            total = total + part[there, :].astype(jnp.float32)
        out_ref[...] = total.astype(out_ref.dtype)


def cut_by_group(parts, lanes, groups):
    span, head = parts[0].shape
    rows = span // groups
    outs = [jax.ShapeDtypeStruct((rows, head), jnp.float32)]
    outs += [jax.ShapeDtypeStruct((rows, head), jnp.bfloat16)] * (groups - 1)
    return pl.pallas_call(
        functools.partial(cut_kernel, lanes, groups),
        out_shape=outs,
        in_specs=[IN_VMEM] * lanes,
        out_specs=[IN_VMEM] * groups,
        compiler_params=pltpu.CompilerParams(vmem_limit_bytes=VMEM_BYTES),
        cost_estimate=cost(span * head, *parts),
        name="cut_by_group",
    )(*parts)


def key_value_products(k_ref, v_ref, state, cols, dk_ref, dv_ref):
    head = state.shape[1]
    for h in range(state.shape[0] // head):
        local = pl.ds(h * head, head)
        keys, grad_state = k_ref[:, cols(h)], state[local, :]
        full = lax.dot_general(
            v_ref[:, cols(h)], grad_state, CONTRACT_COLS, preferred_element_type=jnp.float32
        )
        dk_ref[:, local] = jnp.where(keys > 0, full, 0.0).astype(dk_ref.dtype)
        dv_ref[:, local] = jnp.dot(
            jnp.maximum(keys, 0), grad_state, preferred_element_type=jnp.float32
        ).astype(dv_ref.dtype)
        yield h


def place_pieces(pieces, group, groups, state):
    for hop, piece in enumerate(pieces):
        rows = piece.shape[0]
        owner = source(group, hop, groups)
        state[pl.ds(pl.multiple_of(owner * rows, rows), rows), :] = piece[...]


def near_kernel(lanes, groups, q_ref, o_ref, k_ref, v_ref, *rest):
    sides, pieces = rest[:lanes], rest[lanes : lanes + groups]
    dq_ref, dk_ref, dv_ref, saved, state, sems = rest[lanes + groups :]
    heads, head, _ = saved.shape
    rows = sides[0].shape[2]
    group, lane = place_on_space(lanes)
    copies = []
    for other, side in enumerate(sides):
        there = 1 - lane if other else lane
        for hop in range(groups):
            owner = source(group, hop, groups) * lanes + there
            dst = pl.ds(pl.multiple_of(owner * rows, rows), rows)
            if rows % 16 == 0:
                saved[:, dst, :] = side[hop]
            else:
                copies.append(
                    pltpu.make_async_copy(side.at[hop], saved.at[:, dst, :], sems.at[other, hop])
                )
    for copy in copies:
        copy.start()
    for copy in copies:
        copy.wait()
    for h in range(heads):
        cols = pl.ds(h * head, head)
        full = lax.dot_general(
            o_ref[:, cols], saved[h], CONTRACT_COLS, preferred_element_type=jnp.float32
        )
        dq_ref[:, cols] = jnp.where(q_ref[:, cols] > 0, full, 0.0).astype(dq_ref.dtype)
    place_pieces(pieces, group, groups, state)
    base = lane * state.shape[0]
    for _ in key_value_products(
        k_ref,
        v_ref,
        state,
        lambda h: pl.ds(pl.multiple_of(base + h * head, head), head),
        dk_ref,
        dv_ref,
    ):
        pass


def near_grads(queries, grad_out, keys, values, sides, pieces):
    lanes, groups = len(sides), len(pieces)
    tokens, heads, (rows, head) = queries.shape[0], sides[0].shape[1], pieces[0].shape
    span = groups * rows
    return pl.pallas_call(
        functools.partial(near_kernel, lanes, groups),
        out_shape=(
            jax.ShapeDtypeStruct(queries.shape, queries.dtype),
            jax.ShapeDtypeStruct((tokens, span), keys.dtype),
            jax.ShapeDtypeStruct((tokens, span), values.dtype),
        ),
        in_specs=[IN_VMEM] * (4 + lanes + groups),
        out_specs=(IN_VMEM, IN_VMEM, IN_VMEM),
        scratch_shapes=[
            pltpu.VMEM((heads, head, head), sides[0].dtype),
            pltpu.VMEM((span, head), pieces[0].dtype),
            pltpu.SemaphoreType.DMA((lanes, groups)),
        ],
        compiler_params=pltpu.CompilerParams(vmem_limit_bytes=VMEM_BYTES),
        cost_estimate=cost(4 * queries.size * head, queries, queries, grad_out, *sides),
        name="near_grads",
    )(queries, grad_out, keys, values, *sides, *pieces)


def far_kernel(lanes, groups, k_ref, v_ref, *rest):
    dq_ref, near, pieces = rest[0], rest[1:3], rest[3:-8]
    dq_hbm, *outs = rest[-8:-5]
    state, dk_buf, dv_buf, sems, dq_sem = rest[-5:]
    span, head = state.shape
    group, lane = place_on_space(lanes)
    copies = [pltpu.make_async_copy(dq_ref, dq_hbm, dq_sem)]
    copies[0].start()
    for at in range(2):
        mine = pl.ds(pl.multiple_of(lane * span, head), span)
        copies.append(pltpu.make_async_copy(near[at], outs[at].at[:, mine], sems.at[at, 0]))
        copies[-1].start()
    if pieces:
        place_pieces(pieces, group, groups, state)
        base = (1 - lane) * span
        part = span // head // (sems.shape[1] - 1)
        for h in key_value_products(
            k_ref,
            v_ref,
            state,
            lambda h: pl.ds(pl.multiple_of(base + h * head, head), head),
            dk_buf,
            dv_buf,
        ):
            if (h + 1) % part == 0:
                src = pl.ds((h + 1 - part) * head, part * head)
                dst = pl.ds(pl.multiple_of(base + (h + 1 - part) * head, head), part * head)
                for at, buf in enumerate((dk_buf, dv_buf)):
                    copies.append(
                        pltpu.make_async_copy(
                            buf.at[:, src], outs[at].at[:, dst], sems.at[at, 1 + h // part]
                        )
                    )
                    copies[-1].start()
    for copy in copies:
        copy.wait()


def far_grads(keys, values, near, pieces, lanes, groups):
    tokens, span = near[1].shape
    head = pieces[0].shape[1] if pieces else span
    return pl.pallas_call(
        functools.partial(far_kernel, lanes, groups),
        out_shape=(
            jax.ShapeDtypeStruct(near[0].shape, near[0].dtype),
            jax.ShapeDtypeStruct(keys.shape, keys.dtype),
            jax.ShapeDtypeStruct(values.shape, values.dtype),
        ),
        in_specs=[IN_VMEM] * (5 + len(pieces)),
        out_specs=(ANYWHERE,) * 3,
        scratch_shapes=[
            pltpu.VMEM((span, head), keys.dtype),
            pltpu.VMEM((tokens, span), keys.dtype),
            pltpu.VMEM((tokens, span), values.dtype),
            pltpu.SemaphoreType.DMA((2, 1 + math.gcd(span // head, 5))),
            pltpu.SemaphoreType.DMA,
        ],
        compiler_params=pltpu.CompilerParams(vmem_limit_bytes=VMEM_BYTES),
        cost_estimate=cost(4 * tokens * span * head, *near),
        name="far_grads",
    )(keys, values, *near, *pieces)


def suffix_sum(share, blocks):
    block = lax.axis_index("tm")
    suffix = total = first = share
    if power_of_two(blocks):
        hop = 1
        while hop < blocks:
            pairs = [(b, b ^ hop) for b in range(blocks)]
            met = lax.ppermute(total.astype(jnp.bfloat16), "tm", pairs).astype(jnp.float32)
            suffix = suffix + jnp.where(block & hop == 0, met, 0.0)
            total = total + met
            first = total if hop == 1 else first
            hop *= 2
    else:
        for hop in range(1, blocks):
            pairs = [(b, b - hop) for b in range(hop, blocks)]
            later = lax.ppermute(share.astype(jnp.bfloat16), "tm", pairs)
            suffix = suffix + later.astype(jnp.float32)
    return suffix.astype(jnp.bfloat16), first


def per_device(queries, keys, values, grad_out, saved_state):
    heads, _, head = saved_state.shape[1:]
    blocks, devices = lax.axis_size("tm"), lax.axis_size("space")
    lanes = 2 if devices % 2 == 0 and heads % 2 == 0 else 1
    groups = devices // lanes
    far_first = sorted(range(1, groups), key=lambda hop: (-hop.bit_count(), hop))
    scale = 1.0 / math.sqrt(queries.shape[0] * blocks * devices * head)

    parts = []
    if lanes > 1:
        _, lane = place_on_space(lanes)
        span = queries.shape[1] // lanes
        starts = (jnp.zeros_like(lane), (1 - lane) * span)
        cut = lax.dynamic_slice(
            queries, starts, (queries.shape[0], span), allow_negative_indices=False
        )
        theirs = partial_products(cut, grad_out, head, lanes, True, scale)
        parts.append(swap_lanes(theirs, lanes, groups))
        queries = after(queries, cut)
    parts.insert(0, partial_products(queries, grad_out, head, lanes, False, scale))
    share, *sends = cut_by_group(parts, lanes, groups)
    for hop in far_first:
        share = share + hop_groups(sends[hop - 1], hop, lanes, groups).astype(jnp.float32)
    own, first = suffix_sum(share, blocks)
    met = [hop_groups(own, hop, lanes, groups) for hop in far_first]

    saved = gather_groups(saved_state, [((), ()), (share, ())], lanes, groups)
    sides = [saved] + ([swap_lanes(saved, lanes, groups)] if lanes > 1 else [])

    near = [own] + [met[far_first.index(hop)] for hop in range(1, groups)]
    far = [swap_lanes(piece, lanes, groups) for piece in near] if lanes > 1 else []
    ready = near_grads(queries, grad_out, keys, values, sides, near)
    return far_grads(keys, values, ready, far, lanes, groups)


def solution(mesh):
    tokens = P(("tm", "space"), None)
    return jax.shard_map(
        per_device,
        mesh=mesh,
        in_specs=(tokens, tokens, tokens, tokens, P("tm", None, "space", None)),
        out_specs=(tokens, tokens, tokens),
        check_vma=False,
    )
```

```python
import functools
import math

import jax
import jax.numpy as jnp
from jax import lax
from jax.experimental import pallas as pl
from jax.experimental.pallas import tpu as pltpu
from jax.sharding import PartitionSpec as P

CONTRACT_ROWS = (((0,), (0,)), ((), ()))
CONTRACT_COLS = (((1,), (1,)), ((), ()))
VMEM_BYTES = 16 * 1024 * 1024
ANYWHERE = pl.BlockSpec(memory_space=pl.ANY)
IN_VMEM = pl.BlockSpec(memory_space=pltpu.VMEM)


def power_of_two(count):
    return count & (count - 1) == 0


def partner(group, hop, groups):
    if power_of_two(groups):
        return group ^ hop
    return (group + hop) % groups


def source(group, hop, groups):
    if power_of_two(groups):
        return group ^ hop
    return (group - hop + groups) % groups


def cost(flops, *arrays):
    moved = sum(array.size * array.dtype.itemsize for array in arrays)
    return pl.CostEstimate(flops=flops, bytes_accessed=moved, transcendentals=0)


def after(value, earlier):
    return lax.optimization_barrier((value, earlier))[0]


def place_on_space(lanes):
    index = lax.axis_index("space")
    return lax.div(index, lanes), lax.rem(index, lanes)


def swap_lanes(value, lanes, groups):
    pairs = [(g * lanes + c, g * lanes + 1 - c) for g in range(groups) for c in range(lanes)]
    return lax.ppermute(value, "space", pairs)


def hop_groups(value, hop, lanes, groups):
    pairs = [
        (g * lanes + c, partner(g, hop, groups) * lanes + c)
        for g in range(groups)
        for c in range(lanes)
    ]
    return lax.ppermute(value, "space", pairs)


def gather_groups(value, waits, lanes, groups):
    if power_of_two(groups):
        for step in range(groups.bit_length() - 1):
            start, done = waits[min(step, len(waits) - 1)]
            met = hop_groups(after(value, start), 1 << step, lanes, groups)
            value = jnp.concatenate([value, after(met, done)])
        return value
    return jnp.concatenate(
        [value] + [hop_groups(value, hop, lanes, groups) for hop in range(1, groups)]
    )


def products(scale, queries, grad_out):
    return scale * lax.dot_general(
        jnp.maximum(queries, 0),
        grad_out,
        CONTRACT_ROWS,
        preferred_element_type=jnp.float32,
    )


def partial_kernel(lanes, groups, hops, other, scale, q_ref, o_ref, part_ref, whole):
    head, rows = part_ref.shape[1], part_ref.shape[0] // len(hops)
    span, count = o_ref.shape[1] // lanes, whole.shape[0] // part_ref.shape[1]
    group, lane = place_on_space(lanes)
    base = (1 - lane if other else lane) * span
    for at, hop in enumerate(hops):
        start = partner(group, hop, groups) * rows
        first = jnp.minimum(lax.div(start, head), span // head - count) * head
        for h in range(count):
            local = pl.ds(pl.multiple_of(first + h * head, head), head)
            cols = pl.ds(pl.multiple_of(base + first + h * head, head), head)
            whole[pl.ds(h * head, head), :] = products(
                scale, q_ref[:, local if other else cols], o_ref[:, cols]
            )
        mine = pl.ds(pl.multiple_of(start - first, math.gcd(rows, head)), rows)
        part_ref[pl.ds(at * rows, rows), :] = whole[mine, :].astype(part_ref.dtype)


def partial_products(queries, grad_out, head, lanes, groups, hops, other, scale):
    tokens, width = grad_out.shape
    span = width // lanes
    rows = span // groups
    count = min(-(-(rows + head - math.gcd(rows, head)) // head), span // head)
    return pl.pallas_call(
        functools.partial(partial_kernel, lanes, groups, hops, other, scale),
        out_shape=jax.ShapeDtypeStruct(
            (len(hops) * rows, head), jnp.bfloat16 if other else jnp.float32
        ),
        in_specs=[IN_VMEM, IN_VMEM],
        out_specs=IN_VMEM,
        scratch_shapes=[pltpu.VMEM((count * head, head), jnp.float32)],
        compiler_params=pltpu.CompilerParams(vmem_limit_bytes=VMEM_BYTES),
        cost_estimate=cost(2 * tokens * len(hops) * rows * head, queries),
        name="partial_other" if other else "partial_own",
    )(queries, grad_out)


def key_value_products(k_ref, v_ref, state, cols, dk_ref, dv_ref):
    head = state.shape[1]
    for h in range(state.shape[0] // head):
        local = pl.ds(h * head, head)
        keys, grad_state = k_ref[:, cols(h)], state[local, :]
        full = lax.dot_general(
            v_ref[:, cols(h)], grad_state, CONTRACT_COLS, preferred_element_type=jnp.float32
        )
        dk_ref[:, local] = jnp.where(keys > 0, full, 0.0).astype(dk_ref.dtype)
        dv_ref[:, local] = jnp.dot(
            jnp.maximum(keys, 0), grad_state, preferred_element_type=jnp.float32
        ).astype(dv_ref.dtype)
        yield h


def place_pieces(pieces, group, groups, state):
    for hop, piece in enumerate(pieces):
        rows = piece.shape[0]
        owner = source(group, hop, groups)
        state[pl.ds(pl.multiple_of(owner * rows, rows), rows), :] = piece[...]


def near_kernel(lanes, groups, q_ref, o_ref, k_ref, v_ref, *rest):
    sides, pieces = rest[:lanes], rest[lanes : lanes + groups]
    dq_ref, dk_ref, dv_ref, saved, state, sems = rest[lanes + groups :]
    heads, head, _ = saved.shape
    rows = sides[0].shape[2]
    group, lane = place_on_space(lanes)
    copies = []
    for other, side in enumerate(sides):
        there = 1 - lane if other else lane
        for hop in range(groups):
            owner = source(group, hop, groups) * lanes + there
            dst = pl.ds(pl.multiple_of(owner * rows, rows), rows)
            if rows % 16 == 0:
                saved[:, dst, :] = side[hop]
            else:
                copies.append(
                    pltpu.make_async_copy(side.at[hop], saved.at[:, dst, :], sems.at[other, hop])
                )
    for copy in copies:
        copy.start()
    for copy in copies:
        copy.wait()
    for h in range(heads):
        cols = pl.ds(h * head, head)
        full = lax.dot_general(
            o_ref[:, cols], saved[h], CONTRACT_COLS, preferred_element_type=jnp.float32
        )
        dq_ref[:, cols] = jnp.where(q_ref[:, cols] > 0, full, 0.0).astype(dq_ref.dtype)
    place_pieces(pieces, group, groups, state)
    base = lane * state.shape[0]
    for _ in key_value_products(
        k_ref,
        v_ref,
        state,
        lambda h: pl.ds(pl.multiple_of(base + h * head, head), head),
        dk_ref,
        dv_ref,
    ):
        pass


def near_grads(queries, grad_out, keys, values, sides, pieces):
    lanes, groups = len(sides), len(pieces)
    tokens, heads, (rows, head) = queries.shape[0], sides[0].shape[1], pieces[0].shape
    span = groups * rows
    return pl.pallas_call(
        functools.partial(near_kernel, lanes, groups),
        out_shape=(
            jax.ShapeDtypeStruct(queries.shape, queries.dtype),
            jax.ShapeDtypeStruct((tokens, span), keys.dtype),
            jax.ShapeDtypeStruct((tokens, span), values.dtype),
        ),
        in_specs=[IN_VMEM] * (4 + lanes + groups),
        out_specs=(IN_VMEM, IN_VMEM, IN_VMEM),
        scratch_shapes=[
            pltpu.VMEM((heads, head, head), sides[0].dtype),
            pltpu.VMEM((span, head), pieces[0].dtype),
            pltpu.SemaphoreType.DMA((lanes, groups)),
        ],
        compiler_params=pltpu.CompilerParams(vmem_limit_bytes=VMEM_BYTES),
        cost_estimate=cost(4 * queries.size * head, queries, queries, grad_out, *sides),
        name="near_grads",
    )(queries, grad_out, keys, values, *sides, *pieces)


def far_kernel(lanes, groups, k_ref, v_ref, *rest):
    dq_ref, near, pieces = rest[0], rest[1:3], rest[3:-8]
    dq_hbm, *outs = rest[-8:-5]
    state, dk_buf, dv_buf, sems, dq_sem = rest[-5:]
    span, head = state.shape
    group, lane = place_on_space(lanes)
    copies = [pltpu.make_async_copy(dq_ref, dq_hbm, dq_sem)]
    copies[0].start()
    for at in range(2):
        mine = pl.ds(pl.multiple_of(lane * span, head), span)
        copies.append(pltpu.make_async_copy(near[at], outs[at].at[:, mine], sems.at[at, 0]))
        copies[-1].start()
    if pieces:
        place_pieces(pieces, group, groups, state)
        base = (1 - lane) * span
        part = span // head // (sems.shape[1] - 1)
        for h in key_value_products(
            k_ref,
            v_ref,
            state,
            lambda h: pl.ds(pl.multiple_of(base + h * head, head), head),
            dk_buf,
            dv_buf,
        ):
            if (h + 1) % part == 0:
                src = pl.ds((h + 1 - part) * head, part * head)
                dst = pl.ds(pl.multiple_of(base + (h + 1 - part) * head, head), part * head)
                for at, buf in enumerate((dk_buf, dv_buf)):
                    copies.append(
                        pltpu.make_async_copy(
                            buf.at[:, src], outs[at].at[:, dst], sems.at[at, 1 + h // part]
                        )
                    )
                    copies[-1].start()
    for copy in copies:
        copy.wait()


def far_grads(keys, values, near, pieces, lanes, groups):
    tokens, span = near[1].shape
    head = pieces[0].shape[1] if pieces else span
    return pl.pallas_call(
        functools.partial(far_kernel, lanes, groups),
        out_shape=(
            jax.ShapeDtypeStruct(near[0].shape, near[0].dtype),
            jax.ShapeDtypeStruct(keys.shape, keys.dtype),
            jax.ShapeDtypeStruct(values.shape, values.dtype),
        ),
        in_specs=[IN_VMEM] * (5 + len(pieces)),
        out_specs=(ANYWHERE,) * 3,
        scratch_shapes=[
            pltpu.VMEM((span, head), keys.dtype),
            pltpu.VMEM((tokens, span), keys.dtype),
            pltpu.VMEM((tokens, span), values.dtype),
            pltpu.SemaphoreType.DMA((2, 1 + math.gcd(span // head, 5))),
            pltpu.SemaphoreType.DMA,
        ],
        compiler_params=pltpu.CompilerParams(vmem_limit_bytes=VMEM_BYTES),
        cost_estimate=cost(4 * tokens * span * head, *near),
        name="far_grads",
    )(keys, values, *near, *pieces)


def suffix_sum(share, blocks):
    block = lax.axis_index("tm")
    suffix = total = first = share
    if power_of_two(blocks):
        hop = 1
        while hop < blocks:
            pairs = [(b, b ^ hop) for b in range(blocks)]
            met = lax.ppermute(total.astype(jnp.bfloat16), "tm", pairs).astype(jnp.float32)
            suffix = suffix + jnp.where(block & hop == 0, met, 0.0)
            total = total + met
            first = total if hop == 1 else first
            hop *= 2
    else:
        for hop in range(1, blocks):
            pairs = [(b, b - hop) for b in range(hop, blocks)]
            later = lax.ppermute(share.astype(jnp.bfloat16), "tm", pairs)
            suffix = suffix + later.astype(jnp.float32)
    return suffix.astype(jnp.bfloat16), first


def per_device(queries, keys, values, grad_out, saved_state):
    heads, _, head = saved_state.shape[1:]
    blocks, devices = lax.axis_size("tm"), lax.axis_size("space")
    lanes = 2 if devices % 2 == 0 and heads % 2 == 0 else 1
    groups = devices // lanes
    far_first = range(groups - 1, 0, -1)
    scale = 1.0 / math.sqrt(queries.shape[0] * blocks * devices * head)

    batches = [tuple(far_first[:1]), (0, *far_first[1:])] if groups > 1 else [(0,)]
    swapped = [None] * len(batches)
    if lanes > 1:
        _, lane = place_on_space(lanes)
        span = queries.shape[1] // lanes
        starts = (jnp.zeros_like(lane), (1 - lane) * span)
        cut = lax.dynamic_slice(
            queries, starts, (queries.shape[0], span), allow_negative_indices=False
        )
        swapped = [
            swap_lanes(
                partial_products(cut, grad_out, head, lanes, groups, hops, True, scale),
                lanes,
                groups,
            )
            for hops in batches
        ]
        queries = after(queries, cut)
    pieces = {}
    for hops, theirs in zip(batches, swapped):
        total = partial_products(queries, grad_out, head, lanes, groups, hops, False, scale)
        if theirs is not None:
            total = total + theirs.astype(jnp.float32)
        pieces.update(zip(hops, jnp.split(total, len(hops))))
    share = pieces[0]
    for hop in far_first:
        send = pieces[hop].astype(jnp.bfloat16)
        share = share + hop_groups(send, hop, lanes, groups).astype(jnp.float32)
    own, first = suffix_sum(share, blocks)
    met = [hop_groups(own, hop, lanes, groups) for hop in far_first]

    saved = gather_groups(saved_state, [((), ()), (share, ())], lanes, groups)
    sides = [saved] + ([swap_lanes(saved, lanes, groups)] if lanes > 1 else [])

    near = [own, *met[::-1]]
    far = [swap_lanes(piece, lanes, groups) for piece in near] if lanes > 1 else []
    ready = near_grads(queries, grad_out, keys, values, sides, near)
    return far_grads(keys, values, ready, far, lanes, groups)


def solution(mesh):
    tokens = P(("tm", "space"), None)
    return jax.shard_map(
        per_device,
        mesh=mesh,
        in_specs=(tokens, tokens, tokens, tokens, P("tm", None, "space", None)),
        out_specs=(tokens, tokens, tokens),
        check_vma=False,
    )
```

```python
import functools
import math

import jax
import jax.numpy as jnp
from jax import lax
from jax.experimental import pallas as pl
from jax.experimental.pallas import tpu as pltpu
from jax.sharding import PartitionSpec as P

CONTRACT_ROWS = (((0,), (0,)), ((), ()))
CONTRACT_COLS = (((1,), (1,)), ((), ()))
VMEM_BYTES = 16 * 1024 * 1024
ANYWHERE = pl.BlockSpec(memory_space=pl.ANY)
IN_VMEM = pl.BlockSpec(memory_space=pltpu.VMEM)


def power_of_two(count):
    return count & (count - 1) == 0


def partner(group, hop, groups):
    if power_of_two(groups):
        return group ^ hop
    return (group + hop) % groups


def source(group, hop, groups):
    if power_of_two(groups):
        return group ^ hop
    return (group - hop + groups) % groups


def cost(flops, *arrays):
    moved = sum(array.size * array.dtype.itemsize for array in arrays)
    return pl.CostEstimate(flops=flops, bytes_accessed=moved, transcendentals=0)


def after(value, earlier):
    return lax.optimization_barrier((value, earlier))[0]


def place_on_space(lanes):
    index = lax.axis_index("space")
    return lax.div(index, lanes), lax.rem(index, lanes)


def swap_lanes(value, lanes, groups):
    pairs = [(g * lanes + c, g * lanes + 1 - c) for g in range(groups) for c in range(lanes)]
    return lax.ppermute(value, "space", pairs)


def hop_groups(value, hop, lanes, groups):
    pairs = [
        (g * lanes + c, partner(g, hop, groups) * lanes + c)
        for g in range(groups)
        for c in range(lanes)
    ]
    return lax.ppermute(value, "space", pairs)


def gather_groups(value, waits, lanes, groups):
    if power_of_two(groups):
        for step in range(groups.bit_length() - 1):
            start, done = waits[min(step, len(waits) - 1)]
            met = hop_groups(after(value, start), 1 << step, lanes, groups)
            value = jnp.concatenate([value, after(met, done)])
        return value
    return jnp.concatenate(
        [value] + [hop_groups(value, hop, lanes, groups) for hop in range(1, groups)]
    )


def products(scale, queries, grad_out):
    return scale * lax.dot_general(
        jnp.maximum(queries, 0),
        grad_out,
        CONTRACT_ROWS,
        preferred_element_type=jnp.float32,
    )


def partial_kernel(lanes, other, scale, q_ref, o_ref, part_ref):
    span, head = part_ref.shape
    _, lane = place_on_space(lanes)
    base = (1 - lane if other else lane) * span
    for h in range(span // head):
        rows = pl.ds(h * head, head)
        cols = pl.ds(pl.multiple_of(base + h * head, head), head)
        part_ref[rows, :] = products(
            scale, q_ref[:, rows if other else cols], o_ref[:, cols]
        ).astype(part_ref.dtype)


def partial_products(queries, grad_out, head, lanes, other, scale):
    tokens, width = grad_out.shape
    span = width // lanes
    return pl.pallas_call(
        functools.partial(partial_kernel, lanes, other, scale),
        out_shape=jax.ShapeDtypeStruct((span, head), jnp.bfloat16 if other else jnp.float32),
        in_specs=[IN_VMEM, IN_VMEM],
        out_specs=IN_VMEM,
        compiler_params=pltpu.CompilerParams(vmem_limit_bytes=VMEM_BYTES),
        cost_estimate=cost(2 * tokens * span * head, queries),
        name="partial_other" if other else "partial_own",
    )(queries, grad_out)


def cut_kernel(lanes, groups, *refs):
    parts, outs = refs[:lanes], refs[lanes:]
    group, _ = place_on_space(lanes)
    rows = outs[0].shape[0]
    for hop, out_ref in enumerate(outs):
        there = pl.ds(pl.multiple_of(partner(group, hop, groups) * rows, rows), rows)
        total = parts[0][there, :]
        for part in parts[1:]:
            total = total + part[there, :].astype(jnp.float32)
        out_ref[...] = total.astype(out_ref.dtype)


def cut_by_group(parts, lanes, groups):
    span, head = parts[0].shape
    rows = span // groups
    outs = [jax.ShapeDtypeStruct((rows, head), jnp.float32)]
    outs += [jax.ShapeDtypeStruct((rows, head), jnp.bfloat16)] * (groups - 1)
    return pl.pallas_call(
        functools.partial(cut_kernel, lanes, groups),
        out_shape=outs,
        in_specs=[IN_VMEM] * lanes,
        out_specs=[IN_VMEM] * groups,
        compiler_params=pltpu.CompilerParams(vmem_limit_bytes=VMEM_BYTES),
        cost_estimate=cost(span * head, *parts),
        name="cut_by_group",
    )(*parts)


def key_value_products(k_ref, v_ref, state, cols, dk_ref, dv_ref):
    head = state.shape[1]
    for h in range(state.shape[0] // head):
        local = pl.ds(h * head, head)
        keys, grad_state = k_ref[:, cols(h)], state[local, :]
        full = lax.dot_general(
            v_ref[:, cols(h)], grad_state, CONTRACT_COLS, preferred_element_type=jnp.float32
        )
        dk_ref[:, local] = jnp.where(keys > 0, full, 0.0).astype(dk_ref.dtype)
        dv_ref[:, local] = jnp.dot(
            jnp.maximum(keys, 0), grad_state, preferred_element_type=jnp.float32
        ).astype(dv_ref.dtype)
        yield h


def place_pieces(pieces, group, groups, state):
    for hop, piece in enumerate(pieces):
        rows = piece.shape[0]
        owner = source(group, hop, groups)
        state[pl.ds(pl.multiple_of(owner * rows, rows), rows), :] = piece[...]


def near_kernel(lanes, groups, q_ref, o_ref, k_ref, v_ref, *rest):
    sides, pieces = rest[:lanes], rest[lanes : lanes + groups]
    dq_ref, dk_ref, dv_ref, saved, state, sems = rest[lanes + groups :]
    heads, head, _ = saved.shape
    rows = sides[0].shape[2]
    group, lane = place_on_space(lanes)
    copies = []
    for other, side in enumerate(sides):
        there = 1 - lane if other else lane
        for hop in range(groups):
            owner = source(group, hop, groups) * lanes + there
            dst = pl.ds(pl.multiple_of(owner * rows, rows), rows)
            if rows % 16 == 0:
                saved[:, dst, :] = side[hop]
            else:
                copies.append(
                    pltpu.make_async_copy(side.at[hop], saved.at[:, dst, :], sems.at[other, hop])
                )
    for copy in copies:
        copy.start()
    for copy in copies:
        copy.wait()
    for h in range(heads):
        cols = pl.ds(h * head, head)
        full = lax.dot_general(
            o_ref[:, cols], saved[h], CONTRACT_COLS, preferred_element_type=jnp.float32
        )
        dq_ref[:, cols] = jnp.where(q_ref[:, cols] > 0, full, 0.0).astype(dq_ref.dtype)
    place_pieces(pieces, group, groups, state)
    base = lane * state.shape[0]
    for _ in key_value_products(
        k_ref,
        v_ref,
        state,
        lambda h: pl.ds(pl.multiple_of(base + h * head, head), head),
        dk_ref,
        dv_ref,
    ):
        pass


def near_grads(queries, grad_out, keys, values, sides, pieces):
    lanes, groups = len(sides), len(pieces)
    tokens, heads, (rows, head) = queries.shape[0], sides[0].shape[1], pieces[0].shape
    span = groups * rows
    return pl.pallas_call(
        functools.partial(near_kernel, lanes, groups),
        out_shape=(
            jax.ShapeDtypeStruct(queries.shape, queries.dtype),
            jax.ShapeDtypeStruct((tokens, span), keys.dtype),
            jax.ShapeDtypeStruct((tokens, span), values.dtype),
        ),
        in_specs=[IN_VMEM] * (4 + lanes + groups),
        out_specs=(IN_VMEM, IN_VMEM, IN_VMEM),
        scratch_shapes=[
            pltpu.VMEM((heads, head, head), sides[0].dtype),
            pltpu.VMEM((span, head), pieces[0].dtype),
            pltpu.SemaphoreType.DMA((lanes, groups)),
        ],
        compiler_params=pltpu.CompilerParams(vmem_limit_bytes=VMEM_BYTES),
        cost_estimate=cost(4 * queries.size * head, queries, queries, grad_out, *sides),
        name="near_grads",
    )(queries, grad_out, keys, values, *sides, *pieces)


def far_kernel(lanes, groups, k_ref, v_ref, *rest):
    dq_ref, near, pieces = rest[0], rest[1:3], rest[3:-8]
    dq_hbm, *outs = rest[-8:-5]
    state, dk_buf, dv_buf, sems, dq_sem = rest[-5:]
    span, head = state.shape
    group, lane = place_on_space(lanes)
    copies = [pltpu.make_async_copy(dq_ref, dq_hbm, dq_sem)]
    copies[0].start()
    for at in range(2):
        mine = pl.ds(pl.multiple_of(lane * span, head), span)
        copies.append(pltpu.make_async_copy(near[at], outs[at].at[:, mine], sems.at[at, 0]))
        copies[-1].start()
    if pieces:
        place_pieces(pieces, group, groups, state)
        base = (1 - lane) * span
        part = span // head // (sems.shape[1] - 1)
        for h in key_value_products(
            k_ref,
            v_ref,
            state,
            lambda h: pl.ds(pl.multiple_of(base + h * head, head), head),
            dk_buf,
            dv_buf,
        ):
            if (h + 1) % part == 0:
                src = pl.ds((h + 1 - part) * head, part * head)
                dst = pl.ds(pl.multiple_of(base + (h + 1 - part) * head, head), part * head)
                for at, buf in enumerate((dk_buf, dv_buf)):
                    copies.append(
                        pltpu.make_async_copy(
                            buf.at[:, src], outs[at].at[:, dst], sems.at[at, 1 + h // part]
                        )
                    )
                    copies[-1].start()
    for copy in copies:
        copy.wait()


def far_grads(keys, values, near, pieces, lanes, groups):
    tokens, span = near[1].shape
    head = pieces[0].shape[1] if pieces else span
    return pl.pallas_call(
        functools.partial(far_kernel, lanes, groups),
        out_shape=(
            jax.ShapeDtypeStruct(near[0].shape, near[0].dtype),
            jax.ShapeDtypeStruct(keys.shape, keys.dtype),
            jax.ShapeDtypeStruct(values.shape, values.dtype),
        ),
        in_specs=[IN_VMEM] * (5 + len(pieces)),
        out_specs=(ANYWHERE,) * 3,
        scratch_shapes=[
            pltpu.VMEM((span, head), keys.dtype),
            pltpu.VMEM((tokens, span), keys.dtype),
            pltpu.VMEM((tokens, span), values.dtype),
            pltpu.SemaphoreType.DMA((2, 1 + math.gcd(span // head, 2))),
            pltpu.SemaphoreType.DMA,
        ],
        compiler_params=pltpu.CompilerParams(vmem_limit_bytes=VMEM_BYTES),
        cost_estimate=cost(4 * tokens * span * head, *near),
        name="far_grads",
    )(keys, values, *near, *pieces)


def suffix_sum(share, blocks):
    block = lax.axis_index("tm")
    suffix = total = first = share
    if power_of_two(blocks):
        hop = 1
        while hop < blocks:
            pairs = [(b, b ^ hop) for b in range(blocks)]
            met = lax.ppermute(total.astype(jnp.bfloat16), "tm", pairs).astype(jnp.float32)
            suffix = suffix + jnp.where(block & hop == 0, met, 0.0)
            total = total + met
            first = total if hop == 1 else first
            hop *= 2
    else:
        for hop in range(1, blocks):
            pairs = [(b, b - hop) for b in range(hop, blocks)]
            later = lax.ppermute(share.astype(jnp.bfloat16), "tm", pairs)
            suffix = suffix + later.astype(jnp.float32)
    return suffix.astype(jnp.bfloat16), first


def per_device(queries, keys, values, grad_out, saved_state):
    heads, _, head = saved_state.shape[1:]
    blocks, devices = lax.axis_size("tm"), lax.axis_size("space")
    lanes = 2 if devices % 2 == 0 and heads % 2 == 0 else 1
    groups = devices // lanes
    far_first = range(groups - 1, 0, -1)
    scale = 1.0 / math.sqrt(queries.shape[0] * blocks * devices * head)

    parts = []
    if lanes > 1:
        _, lane = place_on_space(lanes)
        span = queries.shape[1] // lanes
        starts = (jnp.zeros_like(lane), (1 - lane) * span)
        cut = lax.dynamic_slice(
            queries, starts, (queries.shape[0], span), allow_negative_indices=False
        )
        theirs = partial_products(cut, grad_out, head, lanes, True, scale)
        parts.append(swap_lanes(theirs, lanes, groups))
        queries = after(queries, cut)
    parts.insert(0, partial_products(queries, grad_out, head, lanes, False, scale))
    share, *sends = cut_by_group(parts, lanes, groups)
    for hop in far_first:
        share = share + hop_groups(sends[hop - 1], hop, lanes, groups).astype(jnp.float32)
    own, first = suffix_sum(share, blocks)
    met = [hop_groups(own, hop, lanes, groups) for hop in far_first]

    saved = gather_groups(saved_state, [((), ()), (share, ())], lanes, groups)
    sides = [saved] + ([swap_lanes(saved, lanes, groups)] if lanes > 1 else [])

    near = [own, *met[::-1]]
    far = [swap_lanes(piece, lanes, groups) for piece in near] if lanes > 1 else []
    ready = near_grads(queries, grad_out, keys, values, sides, near)
    return far_grads(keys, values, ready, far, lanes, groups)


def solution(mesh):
    tokens = P(("tm", "space"), None)
    return jax.shard_map(
        per_device,
        mesh=mesh,
        in_specs=(tokens, tokens, tokens, tokens, P("tm", None, "space", None)),
        out_specs=(tokens, tokens, tokens),
        check_vma=False,
    )
```

```python
import functools
import math

import jax
import jax.numpy as jnp
from jax import lax
from jax.experimental import pallas as pl
from jax.experimental.pallas import tpu as pltpu
from jax.sharding import PartitionSpec as P

CONTRACT_ROWS = (((0,), (0,)), ((), ()))
CONTRACT_COLS = (((1,), (1,)), ((), ()))
VMEM_BYTES = 16 * 1024 * 1024
ANYWHERE = pl.BlockSpec(memory_space=pl.ANY)
IN_VMEM = pl.BlockSpec(memory_space=pltpu.VMEM)


def power_of_two(count):
    return count & (count - 1) == 0


def partner(group, hop, groups):
    if power_of_two(groups):
        return group ^ hop
    return (group + hop) % groups


def source(group, hop, groups):
    if power_of_two(groups):
        return group ^ hop
    return (group - hop + groups) % groups


def cost(flops, *arrays):
    moved = sum(array.size * array.dtype.itemsize for array in arrays)
    return pl.CostEstimate(flops=flops, bytes_accessed=moved, transcendentals=0)


def after(value, earlier):
    return lax.optimization_barrier((value, earlier))[0]


def place_on_space(lanes):
    index = lax.axis_index("space")
    return lax.div(index, lanes), lax.rem(index, lanes)


def swap_lanes(value, lanes, groups):
    pairs = [(g * lanes + c, g * lanes + 1 - c) for g in range(groups) for c in range(lanes)]
    return lax.ppermute(value, "space", pairs)


def hop_groups(value, hop, lanes, groups):
    pairs = [
        (g * lanes + c, partner(g, hop, groups) * lanes + c)
        for g in range(groups)
        for c in range(lanes)
    ]
    return lax.ppermute(value, "space", pairs)


def gather_groups(value, waits, lanes, groups):
    if power_of_two(groups):
        for step in range(groups.bit_length() - 1):
            start, done = waits[min(step, len(waits) - 1)]
            met = hop_groups(after(value, start), 1 << step, lanes, groups)
            value = jnp.concatenate([value, after(met, done)])
        return value
    return jnp.concatenate(
        [value] + [hop_groups(value, hop, lanes, groups) for hop in range(1, groups)]
    )


def products(scale, queries, grad_out):
    return scale * lax.dot_general(
        jnp.maximum(queries, 0),
        grad_out,
        CONTRACT_ROWS,
        preferred_element_type=jnp.float32,
    )


def partial_kernel(lanes, other, scale, q_ref, o_ref, part_ref):
    span, head = part_ref.shape
    _, lane = place_on_space(lanes)
    base = (1 - lane if other else lane) * span
    for h in range(span // head):
        rows = pl.ds(h * head, head)
        cols = pl.ds(pl.multiple_of(base + h * head, head), head)
        part_ref[rows, :] = products(
            scale, q_ref[:, rows if other else cols], o_ref[:, cols]
        ).astype(part_ref.dtype)


def partial_products(queries, grad_out, head, lanes, other, scale):
    tokens, width = grad_out.shape
    span = width // lanes
    return pl.pallas_call(
        functools.partial(partial_kernel, lanes, other, scale),
        out_shape=jax.ShapeDtypeStruct((span, head), jnp.bfloat16 if other else jnp.float32),
        in_specs=[IN_VMEM, IN_VMEM],
        out_specs=IN_VMEM,
        compiler_params=pltpu.CompilerParams(vmem_limit_bytes=VMEM_BYTES),
        cost_estimate=cost(2 * tokens * span * head, queries),
        name="partial_other" if other else "partial_own",
    )(queries, grad_out)


def cut_kernel(lanes, groups, *refs):
    parts, outs = refs[:lanes], refs[lanes:]
    group, _ = place_on_space(lanes)
    rows = outs[0].shape[0]
    for hop, out_ref in enumerate(outs):
        there = pl.ds(pl.multiple_of(partner(group, hop, groups) * rows, rows), rows)
        total = parts[0][there, :]
        for part in parts[1:]:
            total = total + part[there, :].astype(jnp.float32)
        out_ref[...] = total.astype(out_ref.dtype)


def cut_by_group(parts, lanes, groups):
    span, head = parts[0].shape
    rows = span // groups
    outs = [jax.ShapeDtypeStruct((rows, head), jnp.float32)]
    outs += [jax.ShapeDtypeStruct((rows, head), jnp.bfloat16)] * (groups - 1)
    return pl.pallas_call(
        functools.partial(cut_kernel, lanes, groups),
        out_shape=outs,
        in_specs=[IN_VMEM] * lanes,
        out_specs=[IN_VMEM] * groups,
        compiler_params=pltpu.CompilerParams(vmem_limit_bytes=VMEM_BYTES),
        cost_estimate=cost(span * head, *parts),
        name="cut_by_group",
    )(*parts)


def key_value_products(k_ref, v_ref, state, cols, dk_ref, dv_ref):
    head = state.shape[1]
    for h in range(state.shape[0] // head):
        local = pl.ds(h * head, head)
        keys, grad_state = k_ref[:, cols(h)], state[local, :]
        full = lax.dot_general(
            v_ref[:, cols(h)], grad_state, CONTRACT_COLS, preferred_element_type=jnp.float32
        )
        dk_ref[:, local] = jnp.where(keys > 0, full, 0.0).astype(dk_ref.dtype)
        dv_ref[:, local] = jnp.dot(
            jnp.maximum(keys, 0), grad_state, preferred_element_type=jnp.float32
        ).astype(dv_ref.dtype)
        yield h


def place_pieces(pieces, group, groups, state):
    for hop, piece in enumerate(pieces):
        rows = piece.shape[0]
        owner = source(group, hop, groups)
        state[pl.ds(pl.multiple_of(owner * rows, rows), rows), :] = piece[...]


def near_kernel(lanes, groups, q_ref, o_ref, k_ref, v_ref, *rest):
    sides, pieces = rest[:lanes], rest[lanes : lanes + groups]
    dq_ref, dk_ref, dv_ref, saved, state, sems = rest[lanes + groups :]
    heads, head, _ = saved.shape
    rows = sides[0].shape[2]
    group, lane = place_on_space(lanes)
    copies = []
    for other, side in enumerate(sides):
        there = 1 - lane if other else lane
        for hop in range(groups):
            owner = source(group, hop, groups) * lanes + there
            dst = pl.ds(pl.multiple_of(owner * rows, rows), rows)
            if rows % 16 == 0:
                saved[:, dst, :] = side[hop]
            else:
                copies.append(
                    pltpu.make_async_copy(side.at[hop], saved.at[:, dst, :], sems.at[other, hop])
                )
    for copy in copies:
        copy.start()
    for copy in copies:
        copy.wait()
    for h in range(heads):
        cols = pl.ds(h * head, head)
        full = lax.dot_general(
            o_ref[:, cols], saved[h], CONTRACT_COLS, preferred_element_type=jnp.float32
        )
        dq_ref[:, cols] = jnp.where(q_ref[:, cols] > 0, full, 0.0).astype(dq_ref.dtype)
    place_pieces(pieces, group, groups, state)
    base = lane * state.shape[0]
    for _ in key_value_products(
        k_ref,
        v_ref,
        state,
        lambda h: pl.ds(pl.multiple_of(base + h * head, head), head),
        dk_ref,
        dv_ref,
    ):
        pass


def near_grads(queries, grad_out, keys, values, sides, pieces):
    lanes, groups = len(sides), len(pieces)
    tokens, heads, (rows, head) = queries.shape[0], sides[0].shape[1], pieces[0].shape
    span = groups * rows
    return pl.pallas_call(
        functools.partial(near_kernel, lanes, groups),
        out_shape=(
            jax.ShapeDtypeStruct(queries.shape, queries.dtype),
            jax.ShapeDtypeStruct((tokens, span), keys.dtype),
            jax.ShapeDtypeStruct((tokens, span), values.dtype),
        ),
        in_specs=[IN_VMEM] * (4 + lanes + groups),
        out_specs=(IN_VMEM, IN_VMEM, IN_VMEM),
        scratch_shapes=[
            pltpu.VMEM((heads, head, head), sides[0].dtype),
            pltpu.VMEM((span, head), pieces[0].dtype),
            pltpu.SemaphoreType.DMA((lanes, groups)),
        ],
        compiler_params=pltpu.CompilerParams(vmem_limit_bytes=VMEM_BYTES),
        cost_estimate=cost(4 * queries.size * head, queries, queries, grad_out, *sides),
        name="near_grads",
    )(queries, grad_out, keys, values, *sides, *pieces)


def far_kernel(lanes, groups, k_ref, v_ref, *rest):
    dq_ref, near, pieces = rest[0], rest[1:3], rest[3:-8]
    dq_hbm, *outs = rest[-8:-5]
    state, dk_buf, dv_buf, sems, dq_sem = rest[-5:]
    span, head = state.shape
    group, lane = place_on_space(lanes)
    copies = [pltpu.make_async_copy(dq_ref, dq_hbm, dq_sem)]
    copies[0].start()
    for at in range(2):
        mine = pl.ds(pl.multiple_of(lane * span, head), span)
        copies.append(pltpu.make_async_copy(near[at], outs[at].at[:, mine], sems.at[at, 0]))
        copies[-1].start()
    if pieces:
        place_pieces(pieces, group, groups, state)
        base = (1 - lane) * span
        part = span // head // (sems.shape[1] - 1)
        for h in key_value_products(
            k_ref,
            v_ref,
            state,
            lambda h: pl.ds(pl.multiple_of(base + h * head, head), head),
            dk_buf,
            dv_buf,
        ):
            if (h + 1) % part == 0:
                src = pl.ds((h + 1 - part) * head, part * head)
                dst = pl.ds(pl.multiple_of(base + (h + 1 - part) * head, head), part * head)
                for at, buf in enumerate((dk_buf, dv_buf)):
                    copies.append(
                        pltpu.make_async_copy(
                            buf.at[:, src], outs[at].at[:, dst], sems.at[at, 1 + h // part]
                        )
                    )
                    copies[-1].start()
    for copy in copies:
        copy.wait()


def far_grads(keys, values, near, pieces, lanes, groups):
    tokens, span = near[1].shape
    head = pieces[0].shape[1] if pieces else span
    return pl.pallas_call(
        functools.partial(far_kernel, lanes, groups),
        out_shape=(
            jax.ShapeDtypeStruct(near[0].shape, near[0].dtype),
            jax.ShapeDtypeStruct(keys.shape, keys.dtype),
            jax.ShapeDtypeStruct(values.shape, values.dtype),
        ),
        in_specs=[IN_VMEM] * (5 + len(pieces)),
        out_specs=(ANYWHERE,) * 3,
        scratch_shapes=[
            pltpu.VMEM((span, head), keys.dtype),
            pltpu.VMEM((tokens, span), keys.dtype),
            pltpu.VMEM((tokens, span), values.dtype),
            pltpu.SemaphoreType.DMA((2, 1 + (span // head))),
            pltpu.SemaphoreType.DMA,
        ],
        compiler_params=pltpu.CompilerParams(vmem_limit_bytes=VMEM_BYTES),
        cost_estimate=cost(4 * tokens * span * head, *near),
        name="far_grads",
    )(keys, values, *near, *pieces)


def suffix_sum(share, blocks):
    block = lax.axis_index("tm")
    suffix = total = first = share
    if power_of_two(blocks):
        hop = 1
        while hop < blocks:
            pairs = [(b, b ^ hop) for b in range(blocks)]
            met = lax.ppermute(total.astype(jnp.bfloat16), "tm", pairs).astype(jnp.float32)
            suffix = suffix + jnp.where(block & hop == 0, met, 0.0)
            total = total + met
            first = total if hop == 1 else first
            hop *= 2
    else:
        for hop in range(1, blocks):
            pairs = [(b, b - hop) for b in range(hop, blocks)]
            later = lax.ppermute(share.astype(jnp.bfloat16), "tm", pairs)
            suffix = suffix + later.astype(jnp.float32)
    return suffix.astype(jnp.bfloat16), first


def per_device(queries, keys, values, grad_out, saved_state):
    heads, _, head = saved_state.shape[1:]
    blocks, devices = lax.axis_size("tm"), lax.axis_size("space")
    lanes = 2 if devices % 2 == 0 and heads % 2 == 0 else 1
    groups = devices // lanes
    far_first = range(groups - 1, 0, -1)
    scale = 1.0 / math.sqrt(queries.shape[0] * blocks * devices * head)

    parts = []
    if lanes > 1:
        _, lane = place_on_space(lanes)
        span = queries.shape[1] // lanes
        starts = (jnp.zeros_like(lane), (1 - lane) * span)
        cut = lax.dynamic_slice(
            queries, starts, (queries.shape[0], span), allow_negative_indices=False
        )
        theirs = partial_products(cut, grad_out, head, lanes, True, scale)
        parts.append(swap_lanes(theirs, lanes, groups))
        queries = after(queries, cut)
    parts.insert(0, partial_products(queries, grad_out, head, lanes, False, scale))
    share, *sends = cut_by_group(parts, lanes, groups)
    for hop in far_first:
        share = share + hop_groups(sends[hop - 1], hop, lanes, groups).astype(jnp.float32)
    own, first = suffix_sum(share, blocks)
    met = [hop_groups(own, hop, lanes, groups) for hop in far_first]

    saved = gather_groups(saved_state, [((), ()), (share, ())], lanes, groups)
    sides = [saved] + ([swap_lanes(saved, lanes, groups)] if lanes > 1 else [])

    near = [own, *met[::-1]]
    far = [swap_lanes(piece, lanes, groups) for piece in near] if lanes > 1 else []
    ready = near_grads(queries, grad_out, keys, values, sides, near)
    return far_grads(keys, values, ready, far, lanes, groups)


def solution(mesh):
    tokens = P(("tm", "space"), None)
    return jax.shard_map(
        per_device,
        mesh=mesh,
        in_specs=(tokens, tokens, tokens, tokens, P("tm", None, "space", None)),
        out_specs=(tokens, tokens, tokens),
        check_vma=False,
    )
```
